32 devices in a mesh: dp: 4 (over y, x), fsdp: 8 (over z, core).
Axes of the slice: x: 2, y: 2, z: 4, core: 2. Of those that a mesh axis runs over, the one named last changes fastest.
Arguments:
- tokens: bfloat16 [32, 512, 768], P(('dp', 'fsdp')), may hold values from -6 to 6
- segments: int32 [32, 512], P(('dp', 'fsdp')), may hold values from 0 to 3, never falling along the last dimension, each value on 1 to 256 neighbouring positions
- cotangent: bfloat16 [32, 512, 768], P(('dp', 'fsdp')), may hold values from -6 to 6
- joint_weight: float32 [2, 768, 2304], P(None, 'fsdp'), may hold values from -0.21875 to 0.21875
- output_weight: float32 [2, 768, 768], P(None, 'fsdp'), may hold values from -0.875 to 0.875
- expand_weight: float32 [2, 768, 3072], P(None, 'fsdp'), may hold values from -0.21875 to 0.21875
- shrink_weight: float32 [2, 3072, 768], P(None, 'fsdp'), may hold values from -0.109375 to 0.109375
- norm_gains: float32 [2, 2, 768], P(None, None, 'fsdp'), may hold values from 0.5 to 1.5
- biases: float32 [2, 6, 768], P(None, None, 'fsdp'), may hold values from -1.25 to 1.25
- hidden_bias: float32 [2, 3072], P(None, 'fsdp'), may hold values from -1.25 to 1.25
- joint_rows: float32 [2, 768], P(None, 'fsdp'), may hold values from 0.14 to 2.9
- joint_columns: float32 [2, 2304], replicated, may hold values from 0.2 to 0.8
- output_rows: float32 [2, 768], P(None, 'fsdp'), may hold values from 0.014 to 0.29
- output_columns: float32 [2, 768], replicated, may hold values from 0.02 to 0.08
- expand_rows: float32 [2, 768], P(None, 'fsdp'), may hold values from 0.07 to 1.42
- expand_columns: float32 [2, 3072], replicated, may hold values from 0.1 to 0.4
- shrink_rows: float32 [2, 3072], P(None, 'fsdp'), may hold values from 0.21 to 4.3
- shrink_columns: float32 [2, 768], replicated, may hold values from 0.3 to 1.2
- gain_moments: float32 [2, 2, 768], P(None, None, 'fsdp'), may hold values from 0.7 to 14.2
- bias_moments: float32 [2, 6, 768], P(None, None, 'fsdp'), may hold values from 0.14 to 2.9
- hidden_moments: float32 [2, 3072], P(None, 'fsdp'), may hold values from 0.07 to 1.42
Outputs:
- activations: bfloat16 [32, 512, 768], P(('dp', 'fsdp'))
- input_gradient: bfloat16 [32, 512, 768], P(('dp', 'fsdp'))
- joint_gradient: float32 [2, 768, 2304], P(None, 'fsdp')
- output_gradient: float32 [2, 768, 768], P(None, 'fsdp')
- expand_gradient: float32 [2, 768, 3072], P(None, 'fsdp')
- shrink_gradient: float32 [2, 3072, 768], P(None, 'fsdp')
- gain_gradient: float32 [2, 2, 768], P(None, None, 'fsdp')
- bias_gradient: float32 [2, 6, 768], P(None, None, 'fsdp')
- hidden_gradient: float32 [2, 3072], P(None, 'fsdp')
- joint_next: float32 [2, 768, 2304], P(None, 'fsdp')
- output_next: float32 [2, 768, 768], P(None, 'fsdp')
- expand_next: float32 [2, 768, 3072], P(None, 'fsdp')
- shrink_next: float32 [2, 3072, 768], P(None, 'fsdp')
- gains_next: float32 [2, 2, 768], P(None, None, 'fsdp')
- biases_next: float32 [2, 6, 768], P(None, None, 'fsdp')
- hidden_bias_next: float32 [2, 3072], P(None, 'fsdp')
- joint_copy: bfloat16 [2, 768, 2304], P(None, 'fsdp')
- output_copy: bfloat16 [2, 768, 768], P(None, 'fsdp')
- expand_copy: bfloat16 [2, 768, 3072], P(None, 'fsdp')
- shrink_copy: bfloat16 [2, 3072, 768], P(None, 'fsdp')
- joint_rows_next: float32 [2, 768], P(None, 'fsdp')
- joint_columns_next: float32 [2, 2304], replicated
- output_rows_next: float32 [2, 768], P(None, 'fsdp')
- output_columns_next: float32 [2, 768], replicated
- expand_rows_next: float32 [2, 768], P(None, 'fsdp')
- expand_columns_next: float32 [2, 3072], replicated
- shrink_rows_next: float32 [2, 3072], P(None, 'fsdp')
- shrink_columns_next: float32 [2, 768], replicated
- gain_moments_next: float32 [2, 2, 768], P(None, None, 'fsdp')
- bias_moments_next: float32 [2, 6, 768], P(None, None, 'fsdp')
- hidden_moments_next: float32 [2, 3072], P(None, 'fsdp')
The draws below stay inside these ranges and needn't reach their ends.
Inputs may be any that keep to these rules, and one draw needn't show every extreme that they name: `segments`: within each row of 512 slots the page numbers never fall, and each page takes 1 to 256 consecutive slots.
All inputs are finite; a program needn't handle non-finite values.
Results may differ from the reference program's by a relative error of at most 0.022.
Values may be sent and summed in bfloat16 or wider, within the bound.
A program may use at most 256 MiB of HBM per device.

```python
import math
import jax
import jax.numpy as jnp
import numpy as np
from jax import lax

HEADS = 12
HEAD_SIZE = 64
D = 768
FF = 3072
LAYERS = 2
SLOTS = 512
PAGES = 4
PAGE_MOST = 256
ROWS = 32


def rising_state(key, shape, base, top):
    count = shape[-1]
    position = jnp.arange(count, dtype=jnp.float32) / max(count - 1, 1)
    rise = jnp.exp(jnp.log(top) * position)
    factor = jnp.exp2(jax.random.uniform(key, shape, jnp.float32, -0.5, 0.5))
    return (base * rise * factor).astype(jnp.float32)


def draw_joint_rows(key, part):
    key = jax.random.fold_in(key, 11)
    top = 6.0
    return rising_state(key, (LAYERS, D), 0.2, top)


def draw_output_rows(key, part):
    key = jax.random.fold_in(key, 12)
    top = 6.0
    return rising_state(key, (LAYERS, D), 0.02, top)


def draw_expand_rows(key, part):
    key = jax.random.fold_in(key, 13)
    top = 6.0
    return rising_state(key, (LAYERS, D), 0.1, top)


def draw_shrink_rows(key, part):
    key = jax.random.fold_in(key, 14)
    top = 6.0
    return rising_state(key, (LAYERS, FF), 0.3, top)


def draw_gain_moments(key, part):
    key = jax.random.fold_in(key, 15)
    top = 6.0
    return rising_state(key, (LAYERS, 2, D), 1.0, top)


def draw_bias_moments(key, part):
    key = jax.random.fold_in(key, 16)
    top = 6.0
    return rising_state(key, (LAYERS, 6, D), 0.2, top)


def draw_hidden_moments(key, part):
    key = jax.random.fold_in(key, 17)
    top = 6.0
    return rising_state(key, (LAYERS, FF), 0.1, top)


def shard_levels(rng, shape, pieces, least, high):
    level, own = 1.0, jax.random.fold_in(rng, 6)
    for dim, parts in pieces:
        steps = jnp.exp(jax.random.uniform(jax.random.fold_in(own, dim), (parts,), jnp.float32, least / len(pieces), high / len(pieces)))
        level = level * jnp.repeat(steps, shape[dim] // parts).reshape([-1 if axis == dim else 1 for axis in range(len(shape))])
    return level


def split_up(count, total, limit, skew):
    loads = [(1 << 20) // math.isqrt(rank ** skew) + 1 for rank in range(2, count + 1)]
    surplus, holding = total - limit - (count - 1), [1] * (count - 1)
    while surplus > 0:
        candidates = [i for i in range(count - 1) if holding[i] < limit]
        mass, remaining = sum([loads[i] for i in candidates]), surplus
        for i in candidates:
            more = min(limit - holding[i], max(1, remaining * loads[i] // mass), surplus)
            holding[i] = holding[i] + more
            surplus = surplus - more
    return np.array([limit] + holding)


def ragged_sizes(stream_key, amount, total, most, slope):
    if amount == 2:
        one = jax.random.randint(stream_key, (), max(1, total - most), min(most, total - 1) + 1)
        return jnp.stack([one, total - one])
    lengths = jnp.asarray(split_up(amount, total, most, slope), jnp.int32)
    twos = (amount - 1) // 2
    source_of, taker = lengths[1:1 + 2 * twos:2], lengths[2:2 + 2 * twos:2]
    slack = jnp.minimum(source_of - 1, most - taker)
    passed = jax.random.randint(jax.random.fold_in(stream_key, 1), (twos,), 0, 1 << 20) % (slack + 1)
    lengths = lengths.at[1:1 + 2 * twos:2].set(source_of - passed).at[2:2 + 2 * twos:2].set(taker + passed)
    return lengths[jax.random.permutation(jax.random.fold_in(stream_key, 2), amount)]


def gaussian(own_key, shape, width, most, shards=(), kind=jnp.bfloat16):
    factor_of = shard_levels(own_key, shape, shards, -0.22, 0.18) if shards else 1.0
    values = jax.random.normal(own_key, shape, jnp.float32) * width * factor_of
    return jnp.minimum(jnp.maximum(values, -most), most).astype(kind)


def setup_inputs(seed: int = 0) -> dict:
    streams_of = jax.random.split(jax.random.key(seed), 22)
    return {
        "tokens": gaussian(streams_of[0], (ROWS, SLOTS, D), 1.0, 6.0, ((0, 32),)),
        "segments": jax.vmap(lambda own: jnp.searchsorted(jnp.cumsum(ragged_sizes(own, PAGES, SLOTS, PAGE_MOST, 1)), jnp.arange(SLOTS), side="right"))(jax.random.split(streams_of[1], ROWS)).reshape((ROWS, SLOTS)).astype(jnp.int32),
        "cotangent": gaussian(streams_of[2], (ROWS, SLOTS, D), 1.0, 6.0, ((0, 32),)),
        "joint_weight": gaussian(streams_of[3], (LAYERS, D, 3 * D), D ** -0.5, 0.21875, ((1, 8),), jnp.float32),
        "output_weight": gaussian(streams_of[4], (LAYERS, D, D), (D // 16) ** -0.5, 0.875, ((1, 8),), jnp.float32),
        "expand_weight": gaussian(streams_of[5], (LAYERS, D, FF), D ** -0.5, 0.21875, ((1, 8),), jnp.float32),
        "shrink_weight": gaussian(streams_of[6], (LAYERS, FF, D), FF ** -0.5, 0.109375, ((1, 8),), jnp.float32),
        "norm_gains": jnp.clip(1.0 + 0.1 * jax.random.normal(streams_of[7], (LAYERS, 2, D), jnp.float32), 0.5, 1.5),
        "biases": gaussian(streams_of[8], (LAYERS, 6, D), 0.2, 1.25, ((2, 8),), jnp.float32),
        "hidden_bias": gaussian(streams_of[9], (LAYERS, FF), 0.2, 1.25, ((1, 8),), jnp.float32),
        "joint_rows": draw_joint_rows(jax.random.fold_in(streams_of[21], 71), 0),
        "joint_columns": jnp.clip(jnp.exp(jax.random.uniform(streams_of[11], (LAYERS, 3 * D), jnp.float32, math.log(0.2), math.log(0.8))), 0.2, 0.8),
        "output_rows": draw_output_rows(jax.random.fold_in(streams_of[21], 71), 0),
        "output_columns": jnp.clip(jnp.exp(jax.random.uniform(streams_of[13], (LAYERS, D), jnp.float32, math.log(0.02), math.log(0.08))), 0.02, 0.08),
        "expand_rows": draw_expand_rows(jax.random.fold_in(streams_of[21], 71), 0),
        "expand_columns": jnp.clip(jnp.exp(jax.random.uniform(streams_of[15], (LAYERS, FF), jnp.float32, math.log(0.1), math.log(0.4))), 0.1, 0.4),
        "shrink_rows": draw_shrink_rows(jax.random.fold_in(streams_of[21], 71), 0),
        "shrink_columns": jnp.clip(jnp.exp(jax.random.uniform(streams_of[17], (LAYERS, D), jnp.float32, math.log(0.3), math.log(1.2))), 0.3, 1.2),
        "gain_moments": draw_gain_moments(jax.random.fold_in(streams_of[21], 71), 0),
        "bias_moments": draw_bias_moments(jax.random.fold_in(streams_of[21], 71), 0),
        "hidden_moments": draw_hidden_moments(jax.random.fold_in(streams_of[21], 71), 0),
    }


NORM_EPSILON = 1e-12
SCORE_SCALE = 0.125
MASK_VALUE = -1e+30
FLOOR_SQUARE = 1e-30
FLOOR_SCALE = 0.001
DECAY_RATE = 0.5
CLIP_LIMIT = 0.25
STEP_RATE = 4.0

@jax.custom_vjp
def low(v):
    return lax.optimization_barrier(v.astype(jnp.bfloat16)).astype(jnp.float32)

@jax.custom_vjp
def low_back(v):
    return v

def low_keep(v):
    return (low(v), None)

def low_pass(kept, grad):
    return (grad,)

def back_keep(v):
    return (v, None)

def back_low(kept, grad):
    return (low(grad),)
low.defvjp(low_keep, low_pass)
low_back.defvjp(back_keep, back_low)

def product(left, right):
    return jnp.dot(left, right, precision=lax.Precision.HIGHEST, preferred_element_type=jnp.float32)

def layer_norm(values, gain, shift):
    average = lax.optimization_barrier(jnp.mean(values, axis=-1, keepdims=True))
    centered = values - average
    variance = lax.optimization_barrier(jnp.mean(centered * centered, axis=-1, keepdims=True))
    return centered * lax.rsqrt(variance + NORM_EPSILON) * gain + shift

def attend_row(packed):
    query_rows, key_rows, value_rows, segment_row = packed
    scores = jnp.einsum('qhe,khe->hqk', query_rows, key_rows, precision=lax.Precision.HIGHEST) * SCORE_SCALE
    scores = low_back(scores)
    allowed = segment_row[:, None] == segment_row[None, :]
    scores = jnp.where(allowed[None], scores, MASK_VALUE)
    weights = low(jax.nn.softmax(scores, axis=-1))
    return jnp.einsum('hqk,khe->qhe', weights, value_rows, precision=lax.Precision.HIGHEST)

def encoder_layer(hidden_in, segments, joint_matrix, output_matrix, expand_matrix, shrink_matrix, gain_rows, bias_rows, inner_bias):
    gain_low = low(gain_rows)
    bias_low = low(bias_rows)
    zero_block = jnp.zeros_like(bias_low[0])
    joint_bias = jnp.concatenate([bias_low[0], zero_block, bias_low[1]])
    joint_out = low(low_back(product(low(hidden_in), low(joint_matrix)) + joint_bias))
    shaped = joint_out.reshape(ROWS, SLOTS, 3, HEADS, HEAD_SIZE)
    context = lax.map(jax.checkpoint(attend_row), (shaped[:, :, 0], shaped[:, :, 1], shaped[:, :, 2], segments))
    context = low(low_back(context.reshape(ROWS * SLOTS, D)))
    attended = low_back(product(context, low(output_matrix)) + bias_low[2])
    first_norm = layer_norm(hidden_in + attended, gain_low[0], bias_low[3])
    pre_active = low_back(product(low(first_norm), low(expand_matrix)) + low(inner_bias))
    active = low(jax.nn.gelu(pre_active, approximate=False))
    branch = low_back(product(active, low(shrink_matrix)) + bias_low[4])
    return layer_norm(first_norm + branch, gain_low[1], bias_low[5])

def factored(weight, gradient, rows_old, columns_old):
    squared = gradient * gradient + FLOOR_SQUARE
    rows_next = DECAY_RATE * rows_old + (1.0 - DECAY_RATE) * lax.optimization_barrier(jnp.mean(squared, axis=1))
    columns_next = DECAY_RATE * columns_old + (1.0 - DECAY_RATE) * lax.optimization_barrier(jnp.mean(squared, axis=0))
    estimate = rows_next[:, None] * columns_next[None, :] / jnp.mean(rows_next)
    update = gradient * lax.rsqrt(estimate)
    clip_ratio = jnp.sqrt(jnp.mean(update * update)) / CLIP_LIMIT
    update = update / jnp.maximum(clip_ratio, 1.0)
    stride = STEP_RATE * jnp.maximum(FLOOR_SCALE, jnp.sqrt(jnp.mean(weight * weight)))
    return (weight - stride * update, rows_next, columns_next)

def unfactored(weight, gradient, moments_old):
    moments_next = DECAY_RATE * moments_old + (1.0 - DECAY_RATE) * (gradient * gradient + FLOOR_SQUARE)
    update = gradient * lax.rsqrt(moments_next)
    clip_ratio = jnp.sqrt(jnp.mean(update * update)) / CLIP_LIMIT
    update = update / jnp.maximum(clip_ratio, 1.0)
    stride = STEP_RATE * jnp.maximum(FLOOR_SCALE, jnp.sqrt(jnp.mean(weight * weight)))
    return (weight - stride * update, moments_next)

def reference(tokens, segments, cotangent, joint_weight, output_weight, expand_weight, shrink_weight, norm_gains, biases, hidden_bias, joint_rows, joint_columns, output_rows, output_columns, expand_rows, expand_columns, shrink_rows, shrink_columns, gain_moments, bias_moments, hidden_moments):
    masters = (joint_weight, output_weight, expand_weight, shrink_weight, norm_gains, biases, hidden_bias)

    def forward(inputs, *params):
        hidden = inputs.reshape(ROWS * SLOTS, D)
        for layer_number in range(LAYERS):
            hidden = encoder_layer(hidden, segments, *[p[layer_number] for p in params])
        return hidden
    result, pullback = jax.vjp(forward, tokens.astype(jnp.float32), *masters)
    gradients = pullback(cotangent.astype(jnp.float32).reshape(ROWS * SLOTS, D))
    root_scale = 1.0 / math.sqrt(ROWS * SLOTS)
    weight_grads = [g * root_scale for g in gradients[1:]]
    matrix_step = jax.vmap(factored)
    joint_next, joint_rows_next, joint_columns_next = matrix_step(joint_weight, weight_grads[0], joint_rows, joint_columns)
    output_next, output_rows_next, output_columns_next = matrix_step(output_weight, weight_grads[1], output_rows, output_columns)
    expand_next, expand_rows_next, expand_columns_next = matrix_step(expand_weight, weight_grads[2], expand_rows, expand_columns)
    shrink_next, shrink_rows_next, shrink_columns_next = matrix_step(shrink_weight, weight_grads[3], shrink_rows, shrink_columns)
    vector_step = jax.vmap(jax.vmap(unfactored))
    gains_next, gain_moments_next = vector_step(norm_gains, weight_grads[4], gain_moments)
    biases_next, bias_moments_next = vector_step(biases, weight_grads[5], bias_moments)
    hidden_bias_next, hidden_moments_next = jax.vmap(unfactored)(hidden_bias, weight_grads[6], hidden_moments)
    activations = result.reshape(ROWS, SLOTS, D).astype(jnp.bfloat16)
    input_gradient = gradients[0].reshape(ROWS, SLOTS, D).astype(jnp.bfloat16)
    return (activations, input_gradient, weight_grads[0], weight_grads[1], weight_grads[2], weight_grads[3], weight_grads[4], weight_grads[5], weight_grads[6], joint_next, output_next, expand_next, shrink_next, gains_next, biases_next, hidden_bias_next, joint_next.astype(jnp.bfloat16), output_next.astype(jnp.bfloat16), expand_next.astype(jnp.bfloat16), shrink_next.astype(jnp.bfloat16), joint_rows_next, joint_columns_next, output_rows_next, output_columns_next, expand_rows_next, expand_columns_next, shrink_rows_next, shrink_columns_next, gain_moments_next, bias_moments_next, hidden_moments_next)
```

```python
from functools import partial
import math

import jax
import jax.numpy as jnp
from jax import lax
from jax.sharding import PartitionSpec as P
from jax.experimental import pallas as pl
from jax.experimental.pallas import tpu as pltpu

HEADS = 12
HEAD_SIZE = 64


NORM_EPSILON = 1e-12
SCORE_SCALE = 0.125
MASK_VALUE = -1e30
FLOOR_SQUARE = 1e-30
FLOOR_SCALE = 0.001
DECAY_RATE = 0.5
CLIP_LIMIT = 0.25
STEP_RATE = 4.0


def product(left, right):
    return jnp.dot(left, right, preferred_element_type=jnp.float32)


def product_left(left, right):
    return lax.dot_general(
        left, right, (((0,), (0,)), ((), ())), preferred_element_type=jnp.float32
    )


def product_right(left, right):
    return lax.dot_general(
        left, right, (((1,), (1,)), ((), ())), preferred_element_type=jnp.float32
    )


def normalize(values):
    average = jnp.mean(values, axis=-1, keepdims=True)
    centered = values - average
    variance = jnp.mean(centered * centered, axis=-1, keepdims=True)
    inverse = lax.rsqrt(variance + NORM_EPSILON)
    return (centered * inverse, inverse)


def normalize_back(grad_scaled, scaled, inverse):
    first_mean = jnp.mean(grad_scaled, axis=-1, keepdims=True)
    second_mean = jnp.mean(grad_scaled * scaled, axis=-1, keepdims=True)
    return inverse * (grad_scaled - first_mean - scaled * second_mean)


def split_heads(joint_row):
    slot_count = joint_row.shape[0]
    shaped = joint_row.reshape(slot_count, 3, HEADS, HEAD_SIZE)
    return (shaped[:, 0], shaped[:, 1], shaped[:, 2])


def masked_scores(query_rows, key_rows, segment_row):
    scores = (
        jnp.einsum("qhe,khe->hqk", query_rows, key_rows, preferred_element_type=jnp.float32)
        * SCORE_SCALE
    )
    allowed = segment_row[:, None] == segment_row[None, :]
    return jnp.where(allowed[None], scores, MASK_VALUE)


def attend_forward(packed):
    joint_row, segment_row = packed
    query_rows, key_rows, value_rows = split_heads(joint_row)
    scores = masked_scores(query_rows, key_rows, segment_row)
    highest = jnp.max(scores, axis=-1, keepdims=True)
    raised = jnp.exp(scores - highest)
    denominator = jnp.sum(raised, axis=-1, keepdims=True)
    weights = (raised / denominator).astype(jnp.bfloat16)
    context = jnp.einsum("hqk,khe->qhe", weights, value_rows, preferred_element_type=jnp.float32)
    logsum = (highest + jnp.log(denominator))[:, :, 0]
    return (context.astype(jnp.bfloat16).reshape(joint_row.shape[0], HEADS * HEAD_SIZE), logsum)


def attend_backward(packed):
    joint_row, segment_row, logsum, grad_row = packed
    slot_count = joint_row.shape[0]
    query_rows, key_rows, value_rows = split_heads(joint_row)
    scores = masked_scores(query_rows, key_rows, segment_row)
    probabilities = jnp.exp(scores - logsum[:, :, None])
    upstream = grad_row.reshape(slot_count, HEADS, HEAD_SIZE)
    grad_probs = jnp.einsum(
        "qhe,khe->hqk", upstream, value_rows, preferred_element_type=jnp.float32
    )
    row_delta = jnp.sum(probabilities * grad_probs, axis=-1, keepdims=True)
    grad_scores = (probabilities * (grad_probs - row_delta)).astype(jnp.bfloat16)
    grad_query = (
        jnp.einsum("hqk,khe->qhe", grad_scores, key_rows, preferred_element_type=jnp.float32)
        * SCORE_SCALE
    )
    grad_key = (
        jnp.einsum("hqk,qhe->khe", grad_scores, query_rows, preferred_element_type=jnp.float32)
        * SCORE_SCALE
    )
    grad_value = jnp.einsum(
        "hqk,qhe->khe",
        probabilities.astype(jnp.bfloat16),
        upstream,
        preferred_element_type=jnp.float32,
    )
    stacked = jnp.stack([grad_query, grad_key, grad_value], axis=1)
    return stacked.reshape(slot_count, 3 * HEADS * HEAD_SIZE).astype(jnp.bfloat16)


def block_forward(hidden_in, segments, weights):
    joint_matrix, output_matrix, expand_matrix, shrink_matrix, gain_rows, bias_rows, inner_bias = (
        weights
    )
    gain_values = gain_rows.astype(jnp.float32)
    bias_values = bias_rows.astype(jnp.float32)
    row_count, slot_count = segments.shape
    zero_block = jnp.zeros_like(bias_values[0])
    joint_bias = jnp.concatenate([bias_values[0], zero_block, bias_values[1]])
    joint_out = (product(hidden_in.astype(jnp.bfloat16), joint_matrix) + joint_bias).astype(
        jnp.bfloat16
    )
    context, logsum = lax.map(
        attend_forward, (joint_out.reshape(row_count, slot_count, -1), segments)
    )
    context = context.reshape(row_count * slot_count, -1)
    attended = product(context, output_matrix) + bias_values[2]
    first_scaled, first_inverse = normalize(hidden_in + attended)
    first_norm = first_scaled * gain_values[0] + bias_values[3]
    pre_active = product(first_norm.astype(jnp.bfloat16), expand_matrix) + inner_bias.astype(
        jnp.float32
    )
    active = jax.nn.gelu(pre_active, approximate=False).astype(jnp.bfloat16)
    branch = product(active, shrink_matrix) + bias_values[4]
    second_scaled, second_inverse = normalize(first_norm + branch)
    result = second_scaled * gain_values[1] + bias_values[5]
    stored = (
        hidden_in,
        joint_out,
        context,
        logsum,
        first_scaled,
        first_inverse,
        pre_active,
        second_scaled,
        second_inverse,
    )
    return (result, stored)


def block_backward(grad_out, segments, weights, stored):
    joint_matrix, output_matrix, expand_matrix, shrink_matrix, gain_rows, bias_rows, inner_bias = (
        weights
    )
    (
        hidden_in,
        joint_out,
        context,
        logsum,
        first_scaled,
        first_inverse,
        pre_active,
        second_scaled,
        second_inverse,
    ) = stored
    gain_values = gain_rows.astype(jnp.float32)
    bias_values = bias_rows.astype(jnp.float32)
    row_count, slot_count = segments.shape
    features = hidden_in.shape[1]
    grad_second_bias = jnp.sum(grad_out, axis=0)
    grad_second_gain = jnp.sum(grad_out * second_scaled, axis=0)
    grad_sum = normalize_back(grad_out * gain_values[1], second_scaled, second_inverse)
    grad_branch = grad_sum.astype(jnp.bfloat16)
    active, gelu_back = jax.vjp(partial(jax.nn.gelu, approximate=False), pre_active)
    grad_shrink = product_left(active.astype(jnp.bfloat16), grad_branch)
    grad_active = product_right(grad_branch, shrink_matrix)
    grad_pre = gelu_back(grad_active)[0].astype(jnp.bfloat16)
    first_norm = first_scaled * gain_values[0] + bias_values[3]
    grad_expand = product_left(first_norm.astype(jnp.bfloat16), grad_pre)
    grad_first = grad_sum + product_right(grad_pre, expand_matrix)
    grad_first_bias = jnp.sum(grad_first, axis=0)
    grad_first_gain = jnp.sum(grad_first * first_scaled, axis=0)
    grad_middle = normalize_back(grad_first * gain_values[0], first_scaled, first_inverse)
    grad_attended = grad_middle.astype(jnp.bfloat16)
    grad_output = product_left(context, grad_attended)
    grad_context = product_right(grad_attended, output_matrix).astype(jnp.bfloat16)
    grad_joint_out = lax.map(
        attend_backward,
        (
            joint_out.reshape(row_count, slot_count, -1),
            segments,
            logsum,
            grad_context.reshape(row_count, slot_count, -1),
        ),
    )
    grad_joint_out = grad_joint_out.reshape(row_count * slot_count, -1)
    grad_joint = product_left(hidden_in.astype(jnp.bfloat16), grad_joint_out)
    grad_input = grad_middle + product_right(grad_joint_out, joint_matrix)
    joint_sums = jnp.sum(grad_joint_out, axis=0, dtype=jnp.float32)
    bias_grads = jnp.stack(
        [
            joint_sums[:features],
            joint_sums[2 * features :],
            jnp.sum(grad_attended, axis=0, dtype=jnp.float32),
            grad_first_bias,
            jnp.sum(grad_branch, axis=0, dtype=jnp.float32),
            grad_second_bias,
        ]
    )
    gain_grads = jnp.stack([grad_first_gain, grad_second_gain])
    inner_grad = jnp.sum(grad_pre, axis=0, dtype=jnp.float32)
    return (
        grad_input,
        (grad_joint, grad_output, grad_expand, grad_shrink, gain_grads, bias_grads, inner_grad),
    )


def factored_partials(gradient, weight, rows_old):
    squared = gradient * gradient + FLOOR_SQUARE
    rows_next = DECAY_RATE * rows_old + (1.0 - DECAY_RATE) * jnp.mean(squared, axis=2)
    return (
        rows_next,
        jnp.sum(squared, axis=1),
        jnp.sum(rows_next, axis=1),
        jnp.sum(weight * weight, axis=(1, 2)),
    )


def vector_partials(gradient, moments_old):
    moments_next = DECAY_RATE * moments_old + (1.0 - DECAY_RATE) * (
        gradient * gradient + FLOOR_SQUARE
    )
    return (moments_next, gradient * lax.rsqrt(moments_next))


def local_plain(
    tokens,
    segments,
    cotangent,
    joint_weight,
    output_weight,
    expand_weight,
    shrink_weight,
    norm_gains,
    biases,
    hidden_bias,
    joint_rows,
    joint_columns,
    output_rows,
    output_columns,
    expand_rows,
    expand_columns,
    shrink_rows,
    shrink_columns,
    gain_moments,
    bias_moments,
    hidden_moments,
):
    layers = joint_weight.shape[0]
    row_count, slot_count, features = tokens.shape
    hidden = tokens.astype(jnp.float32).reshape(row_count * slot_count, features)
    gathered_list = []
    stored_list = []
    for number in range(layers):
        weights = (
            lax.all_gather(joint_weight[number].astype(jnp.bfloat16), "fsdp", axis=0, tiled=True),
            lax.all_gather(output_weight[number].astype(jnp.bfloat16), "fsdp", axis=0, tiled=True),
            lax.all_gather(expand_weight[number].astype(jnp.bfloat16), "fsdp", axis=0, tiled=True),
            lax.all_gather(shrink_weight[number].astype(jnp.bfloat16), "fsdp", axis=0, tiled=True),
            lax.all_gather(norm_gains[number].astype(jnp.bfloat16), "fsdp", axis=1, tiled=True),
            lax.all_gather(biases[number].astype(jnp.bfloat16), "fsdp", axis=1, tiled=True),
            lax.all_gather(hidden_bias[number].astype(jnp.bfloat16), "fsdp", axis=0, tiled=True),
        )
        hidden, stored = block_forward(hidden, segments, weights)
        gathered_list.append(weights)
        stored_list.append(stored)
    activations = hidden.reshape(row_count, slot_count, features).astype(jnp.bfloat16)
    grad_hidden = cotangent.astype(jnp.float32).reshape(row_count * slot_count, features)
    collected = []
    for number in reversed(range(layers)):
        weights = (
            lax.all_gather(joint_weight[number].astype(jnp.bfloat16), "fsdp", axis=0, tiled=True),
            lax.all_gather(output_weight[number].astype(jnp.bfloat16), "fsdp", axis=0, tiled=True),
            lax.all_gather(expand_weight[number].astype(jnp.bfloat16), "fsdp", axis=0, tiled=True),
            lax.all_gather(shrink_weight[number].astype(jnp.bfloat16), "fsdp", axis=0, tiled=True),
            lax.all_gather(norm_gains[number].astype(jnp.bfloat16), "fsdp", axis=1, tiled=True),
            lax.all_gather(biases[number].astype(jnp.bfloat16), "fsdp", axis=1, tiled=True),
            lax.all_gather(hidden_bias[number].astype(jnp.bfloat16), "fsdp", axis=0, tiled=True),
        )
        grad_hidden, local_grads = block_backward(
            grad_hidden, segments, weights, stored_list[number]
        )
        grad_joint, grad_output, grad_expand, grad_shrink, gain_grads, bias_grads, inner_grad = (
            local_grads
        )
        shards = (
            lax.psum_scatter(grad_joint, "fsdp", scatter_dimension=0, tiled=True),
            lax.psum_scatter(grad_output, "fsdp", scatter_dimension=0, tiled=True),
            lax.psum_scatter(grad_expand, "fsdp", scatter_dimension=0, tiled=True),
            lax.psum_scatter(grad_shrink, "fsdp", scatter_dimension=0, tiled=True),
            lax.psum_scatter(gain_grads, "fsdp", scatter_dimension=1, tiled=True),
            lax.psum_scatter(bias_grads, "fsdp", scatter_dimension=1, tiled=True),
            lax.psum_scatter(inner_grad, "fsdp", scatter_dimension=0, tiled=True),
        )
        summed = (
            lax.psum(shards[0].astype(jnp.bfloat16), "dp").astype(jnp.float32),
            lax.psum(shards[1].astype(jnp.bfloat16), "dp").astype(jnp.float32),
            lax.psum(shards[2].astype(jnp.bfloat16), "dp").astype(jnp.float32),
            lax.psum(shards[3].astype(jnp.bfloat16), "dp").astype(jnp.float32),
            lax.psum(shards[4].astype(jnp.bfloat16), "dp").astype(jnp.float32),
            lax.psum(shards[5].astype(jnp.bfloat16), "dp").astype(jnp.float32),
            lax.psum(shards[6].astype(jnp.bfloat16), "dp").astype(jnp.float32),
        )
        collected.append(summed)
    collected = collected[::-1]
    input_gradient = grad_hidden.reshape(row_count, slot_count, features).astype(jnp.bfloat16)
    fsdp_count = lax.axis_size("fsdp")
    token_total = row_count * slot_count * lax.axis_size("dp") * fsdp_count
    root_scale = 1.0 / math.sqrt(token_total)
    stacked_grads = [
        jnp.stack([entry[index] for entry in collected]) * root_scale for index in range(7)
    ]
    matrices = (
        (stacked_grads[0], joint_weight, joint_rows, joint_columns),
        (stacked_grads[1], output_weight, output_rows, output_columns),
        (stacked_grads[2], expand_weight, expand_rows, expand_columns),
        (stacked_grads[3], shrink_weight, shrink_rows, shrink_columns),
    )
    partial_list = [factored_partials(item[0], item[1], item[2]) for item in matrices]
    vectors = (
        (stacked_grads[4], norm_gains, gain_moments),
        (stacked_grads[5], biases, bias_moments),
        (stacked_grads[6][:, None, :], hidden_bias[:, None, :], hidden_moments[:, None, :]),
    )
    vector_list = [vector_partials(item[0], item[2]) for item in vectors]
    vector_squares = jnp.concatenate(
        [jnp.sum(item[1] * item[1], axis=2) for item in vectors], axis=1
    )
    statistics = lax.psum(
        (
            partial_list[0][1],
            partial_list[1][1],
            partial_list[2][1],
            partial_list[3][1],
            jnp.stack([item[2] for item in partial_list], axis=1),
            jnp.stack([item[3] for item in partial_list], axis=1),
            vector_squares,
        ),
        "fsdp",
    )
    updates = []
    columns_list = []
    for index in range(4):
        gradient = matrices[index][0]
        total_rows = gradient.shape[1] * fsdp_count
        rows_next = partial_list[index][0]
        columns_next = DECAY_RATE * matrices[index][3] + (1.0 - DECAY_RATE) * (
            statistics[index] / total_rows
        )
        row_average = statistics[4][:, index] / total_rows
        estimate = rows_next[:, :, None] * columns_next[:, None, :] / row_average[:, None, None]
        updates.append(gradient * lax.rsqrt(estimate))
        columns_list.append(columns_next)
    matrix_squares = jnp.stack([jnp.sum(item * item, axis=(1, 2)) for item in updates], axis=1)
    vector_updates = jnp.concatenate(
        [jnp.sum(item[1] * item[1], axis=2) for item in vector_list], axis=1
    )
    norms = lax.psum((matrix_squares, vector_updates), "fsdp")
    matrix_next = []
    for index in range(4):
        gradient = matrices[index][0]
        entry_count = gradient.shape[1] * fsdp_count * gradient.shape[2]
        clip_ratio = jnp.sqrt(norms[0][:, index] / entry_count) / CLIP_LIMIT
        update = updates[index] / jnp.maximum(clip_ratio, 1.0)[:, None, None]
        stride = STEP_RATE * jnp.maximum(
            FLOOR_SCALE, jnp.sqrt(statistics[5][:, index] / entry_count)
        )
        matrix_next.append(matrices[index][1] - stride[:, None, None] * update)
    vector_next = []
    offset = 0
    for index in range(3):
        gradient = vectors[index][0]
        kinds = gradient.shape[1]
        entry_count = gradient.shape[2] * fsdp_count
        clip_ratio = jnp.sqrt(norms[1][:, offset : offset + kinds] / entry_count) / CLIP_LIMIT
        update = vector_list[index][1] / jnp.maximum(clip_ratio, 1.0)[:, :, None]
        stride = STEP_RATE * jnp.maximum(
            FLOOR_SCALE, jnp.sqrt(statistics[6][:, offset : offset + kinds] / entry_count)
        )
        vector_next.append(vectors[index][1] - stride[:, :, None] * update)
        offset = offset + kinds
    return (
        activations,
        input_gradient,
        stacked_grads[0],
        stacked_grads[1],
        stacked_grads[2],
        stacked_grads[3],
        stacked_grads[4],
        stacked_grads[5],
        stacked_grads[6],
        matrix_next[0],
        matrix_next[1],
        matrix_next[2],
        matrix_next[3],
        vector_next[0],
        vector_next[1],
        vector_next[2][:, 0, :],
        matrix_next[0].astype(jnp.bfloat16),
        matrix_next[1].astype(jnp.bfloat16),
        matrix_next[2].astype(jnp.bfloat16),
        matrix_next[3].astype(jnp.bfloat16),
        partial_list[0][0],
        columns_list[0],
        partial_list[1][0],
        columns_list[1],
        partial_list[2][0],
        columns_list[2],
        partial_list[3][0],
        columns_list[3],
        vector_list[0][0],
        vector_list[1][0],
        vector_list[2][0][:, 0, :],
    )


F32 = jnp.float32
BF = jnp.bfloat16
T = 512
D = 768


def nn(a, b):
    return lax.dot_general(a, b, (((1,), (0,)), ((), ())), preferred_element_type=F32)


def nt(a, b):
    return lax.dot_general(a, b, (((1,), (1,)), ((), ())), preferred_element_type=F32)


def rows_at(i, n):
    return pl.ds(pl.multiple_of(i * n, n), n)


def build_mask(seg_ref, bias_ref):
    row = seg_ref[...]
    wide = jnp.broadcast_to(row, (128, T)).T
    for j in range(T // 128):
        bias_ref[:, j * 128 : (j + 1) * 128] = jnp.where(
            wide == row[:, j * 128 : (j + 1) * 128], 0.0, MASK_VALUE
        ).astype(F32)


def joint_forward(xb, wa, vec, joint, tile=256):
    for b in range(3):
        @pl.loop(0, T // tile)
        def _(i, b=b):
            r = rows_at(i, tile)
            out = nn(xb[r, :], wa[b])
            if b == 0:
                out = out + vec[2:3, :]
            if b == 2:
                out = out + vec[3:4, :]
            joint[b, r, :] = out.astype(BF)


def head_masks():
    lane = lax.broadcasted_iota(jnp.int32, (1, 128), 1)
    return [
        jnp.where(lane < 64, 1.0, 0.0).astype(F32),
        jnp.where(lane >= 64, 1.0, 0.0).astype(F32),
    ]


def attend_forward_pair(p, joint, bias, ctx, logsum):
    lanes = pl.ds(pl.multiple_of(p * 128, 128), 128)
    masks = head_masks()
    q2 = joint[0, :, lanes]
    k2 = joint[1, :, lanes]
    vt = joint[2, :, lanes].T
    outs, sums = [], []
    for h in range(2):
        qm = q2 * (masks[h] * 0.125).astype(BF)
        st = nt(k2, qm) + bias[...]
        top = jnp.max(st, axis=0, keepdims=True)
        e = jnp.exp(st - top)
        total = jnp.sum(e, axis=0, keepdims=True)
        ct = nn(vt[64 * h : 64 * h + 64, :], e.astype(BF))
        outs.append(ct * (1.0 / total))
        sums.append(top + jnp.log(total))
    ctx[:, lanes] = jnp.concatenate(outs, axis=0).T.astype(BF)
    logsum[p] = jnp.concatenate(sums, axis=0)


def norm_parts(u):
    avg = jnp.mean(u, axis=-1, keepdims=True)
    c = u - avg
    var = jnp.mean(c * c, axis=-1, keepdims=True)
    inv = lax.rsqrt(var + NORM_EPSILON)
    return c * inv, inv


def out_forward(ctx, x, wo, vec, n1, r1, h, hb, tile=128):
    @pl.loop(0, T // tile)
    def _(i):
        r = rows_at(i, tile)
        u = nn(ctx[r, :], wo[...]) + vec[4:5, :] + x[r, :].astype(F32)
        n, inv = norm_parts(u)
        y = n * vec[0:1, :] + vec[5:6, :]
        n1[r, :] = n.astype(n1.dtype)
        r1[r, :] = jnp.broadcast_to(inv, (tile, 128))
        h[r, :] = y
        hb[r, :] = y.astype(BF)


def gelu_parts(z):
    a = jnp.abs(z)
    e = jnp.exp(z * z * -0.5)
    t = 1.0 / (1.0 + 0.23164189 * a)
    poly = t * (
        0.127414796 + t * (-0.142248368 + t * (0.7107068705 + t * (-0.7265760135 + t * 0.5307027145)))
    )
    tail = poly * e
    cdf = jnp.where(z >= 0.0, 1.0 - tail, tail)
    return z * cdf, cdf + z * (e * 0.3989422804014327)


def ffn_up(hb, we, vec, g, gp, b, tile=128):
    @pl.loop(0, T // tile)
    def _(i):
        r = rows_at(i, tile)
        z = nn(hb[r, :], we[b]) + vec[8 + b : 9 + b, :]
        act, der = gelu_parts(z)
        g[b, r, :] = act.astype(BF)
        gp[b, r, :] = der.astype(BF)


def ffn_down(g, ws, vec, h, n2, r2, x_out, xb_out, tile=128):
    @pl.loop(0, T // tile)
    def _(i):
        r = rows_at(i, tile)
        u = h[r, :] + vec[6:7, :]
        for b in range(4):
            u = u + nn(g[b, r, :], ws[b])
        n, inv = norm_parts(u)
        y = n * vec[1:2, :] + vec[7:8, :]
        n2[r, :] = n.astype(n2.dtype)
        r2[r, :] = jnp.broadcast_to(inv, (tile, 128))
        if x_out is not None:
            x_out[r, :] = y
        xb_out[r, :] = y.astype(BF)


def sum8(v):
    return jnp.sum(v.reshape(v.shape[0] // 8, 8, v.shape[1]), axis=0)


def norm_backward(dy, n, r, gain_row, du, dub, sums, rows, tile=128):
    def step(i, carry):
        s = rows_at(i, tile)
        g = dy[s, :].astype(F32)
        nv = n[s, :].astype(F32)
        inv = r[s, 0:1]
        e = g * gain_row
        m1 = jnp.mean(e, axis=-1, keepdims=True)
        m2 = jnp.mean(e * nv, axis=-1, keepdims=True)
        d = inv * (e - m1 - nv * m2)
        db = d.astype(BF)
        du[s, :] = d
        dub[s, :] = db
        return (
            carry[0] + sum8(g * nv),
            carry[1] + sum8(g),
            carry[2] + sum8(db.astype(F32)),
        )

    zero = jnp.zeros((8, D), F32)
    out = lax.fori_loop(0, T // tile, step, (zero, zero, zero))
    for k in range(3):
        sums[rows[k] : rows[k] + 1, :] = jnp.sum(out[k], axis=0, keepdims=True)


def transpose_into(src, dst, tile=128):
    @pl.loop(0, T // tile)
    def _(i):
        dst[:, rows_at(i, tile)] = src[rows_at(i, tile), :].T


def weight_grad(at, bmat, out, tile=256):
    @pl.loop(0, D // tile)
    def _(i):
        r = rows_at(i, tile)
        out[r, :] = nn(at[r, :], bmat[...]).astype(BF)


def ffn_back_block(dob, ws, g, gp, dz, sums, b, tile=128):
    def step(i, acc):
        r = rows_at(i, tile)
        v = (nt(dob[r, :], ws[b]) * gp[b, r, :].astype(F32)).astype(BF)
        dz[b, r, :] = v
        return acc + sum8(v.astype(F32))

    acc = lax.fori_loop(0, T // tile, step, jnp.zeros((8, D), F32))
    sums[8 + b : 9 + b, :] = jnp.sum(acc, axis=0, keepdims=True)


def ffn_back_input(dz, we, du, tile=128):
    @pl.loop(0, T // tile)
    def _(i):
        r = rows_at(i, tile)
        u = du[r, :]
        for b in range(4):
            u = u + nt(dz[b, r, :], we[b])
        du[r, :] = u


def context_back(dab, wo, dc, tile=256):
    @pl.loop(0, T // tile)
    def _(i):
        r = rows_at(i, tile)
        dc[r, :] = nt(dab[r, :], wo[...]).astype(BF)


def attend_backward_pair(p, joint, bias, logsum, dc, dj):
    lanes = pl.ds(pl.multiple_of(p * 128, 128), 128)
    masks = head_masks()
    q2 = joint[0, :, lanes]
    k2 = joint[1, :, lanes]
    v2 = joint[2, :, lanes]
    d2 = dc[:, lanes]
    kt = k2.T
    ls = logsum[p]
    dk = jnp.zeros((T, 128), F32)
    dv = jnp.zeros((T, 128), F32)
    dqt = []
    for h in range(2):
        qm = q2 * (masks[h] * 0.125).astype(BF)
        dm = d2 * masks[h].astype(BF)
        prob = jnp.exp(nt(k2, qm) + bias[...] - ls[h : h + 1, :])
        dp = nt(v2, dm)
        delta = jnp.sum(prob * dp, axis=0, keepdims=True)
        ds = (prob * (dp - delta)).astype(BF)
        dv = dv + nn(prob.astype(BF), dm)
        dk = dk + nn(ds, qm)
        dqt.append(nn(kt[64 * h : 64 * h + 64, :], ds))
    dj[0, :, lanes] = (jnp.concatenate(dqt, axis=0) * 0.125).T.astype(BF)
    dj[1, :, lanes] = dk.astype(BF)
    dj[2, :, lanes] = dv.astype(BF)


def input_back(dj, wa, du, dx, sums, tile=128):
    def step(i, carry):
        r = rows_at(i, tile)
        u = du[r, :]
        for b in range(3):
            u = u + nt(dj[b, r, :], wa[b])
        dx[r, :] = u.astype(dx.dtype)
        return (carry[0] + sum8(dj[0, r, :].astype(F32)), carry[1] + sum8(dj[2, r, :].astype(F32)))

    zero = jnp.zeros((8, D), F32)
    out = lax.fori_loop(0, T // tile, step, (zero, zero))
    sums[2:3, :] = jnp.sum(out[0], axis=0, keepdims=True)
    sums[3:4, :] = jnp.sum(out[1], axis=0, keepdims=True)


MESH = pl.DeviceIdType.MESH
PAIRS = 6
PIECE = 96
GROUPS = 6


def place():
    q = lax.axis_index("dp")
    f = lax.axis_index("fsdp")
    z = f // 2
    c = f % 2
    x_side = (q + 1 - 2 * (q % 2), f)
    y_side = ((q + 2) % 4, f)
    sibling = (q, f + 1 - 2 * c)
    planes = [(q, (f + 2 * k) % 8) for k in range(1, 4)]
    return q, z, c, x_side, y_side, sibling, planes


def greet(peers):
    barrier = pltpu.get_barrier_semaphore()
    for peer in peers:
        pl.semaphore_signal(barrier, inc=1, device_id=peer, device_id_type=MESH)
    pl.semaphore_wait(barrier, len(peers))


def hidden_piece(kind, b, zz, c, first, count):
    if kind < 2:
        start = 192 * zz + 96 * c + first
        return b, pl.ds(pl.multiple_of(start, 16), count)
    start = 384 * c + 96 * b + first
    return zz, pl.ds(pl.multiple_of(start, 16), count)


PARTS = [(g, first, 32) for g in range(6) for first in (0, 32, 64)]


class Gather:
    def __init__(self, whole, sbuf, sems):
        self.whole, self.sbuf, self.sems = whole, sbuf, sems
        q, z, c, self.x_side, self.y_side, self.sibling, self.planes = place()
        self.q, self.z, self.c = q, z, c
        self.qx = q + 1 - 2 * (q % 2)
        self.qy = (q + 2) % 4
        self.qd = (self.qx + 2) % 4
        self.others = [(z + k) % 4 for k in range(1, 4)]

    def spot(self, k, b, zz, cols=None):
        g, first, count = PARTS[k]
        lead, rows = hidden_piece(g % 3, b, zz, self.c, first, count)
        if cols is None:
            return self.whole.at[g, lead, rows, :]
        return self.whole.at[g, lead, rows, pl.ds(384 * cols, 384)]

    def send(self, k, src, dst, slot, peer):
        pltpu.make_async_remote_copy(
            src_ref=src, dst_ref=dst, send_sem=self.sems.at[k, slot], recv_sem=self.sems.at[k, slot + 1],
            device_id=peer, device_id_type=MESH,
        ).start()

    def total(self, k, slot, rows, cols=768):
        lead = self.whole.at[0, 0, pl.ds(0, rows), pl.ds(0, cols)] if rows <= 768 else self.whole.at[0, pl.ds(0, rows // 768)]
        pltpu.make_async_copy(lead, lead, self.sems.at[k, slot]).wait()

    def z_send(self, k):
        g, first, count = PARTS[k]
        src = self.sbuf.at[g, self.q, pl.ds(first, count), :]
        for peer in self.planes:
            self.send(k, src, self.spot(k, self.q, self.z), 0, peer)
        for b in range(4):
            mine = self.sbuf.at[g, b, pl.ds(first, count), :]
            self.send(k, mine, self.spot(k, b, self.z), 10, self.sibling)
            pltpu.make_async_copy(mine, self.spot(k, b, self.z), self.sems.at[k, 12]).start()

    def xy_send(self, k):
        count = PARTS[k][2]
        self.total(k, 1, 3 * count)
        for zz in self.others:
            spot = self.spot(k, self.q, zz)
            self.send(k, spot, spot, 2, self.x_side)
            self.send(k, spot, spot, 4, self.y_side)
        for zz in self.others:
            spot = self.spot(k, self.q, zz)
            self.send(k, spot, spot, 10, self.sibling)

    def diagonal_send(self, k):
        count = PARTS[k][2]
        self.total(k, 3, 3 * count)
        self.total(k, 5, 3 * count)
        for zz in self.others:
            spot = self.spot(k, self.qy, zz, 0)
            self.send(k, spot, spot, 6, self.x_side)
            spot = self.spot(k, self.qx, zz, 1)
            self.send(k, spot, spot, 8, self.y_side)
        for zz in self.others:
            for b in (self.qx, self.qy):
                spot = self.spot(k, b, zz)
                self.send(k, spot, spot, 10, self.sibling)

    def last_send(self, k):
        count = PARTS[k][2]
        self.total(k, 7, 3 * count, 384)
        self.total(k, 9, 3 * count, 384)
        for zz in self.others:
            spot = self.spot(k, self.qd, zz)
            self.send(k, spot, spot, 10, self.sibling)

    def finish(self, k):
        count = PARTS[k][2]
        self.total(k, 11, 16 * count)
        self.total(k, 12, 4 * count)

    def drain(self, k):
        count = PARTS[k][2]
        self.total(k, 0, 3 * count)
        self.total(k, 2, 3 * count)
        self.total(k, 4, 3 * count)
        self.total(k, 6, 3 * count, 384)
        self.total(k, 8, 3 * count, 384)
        self.total(k, 10, 16 * count)


UNIT_TIMES = (("joint", 3.0),) + tuple((f"att{p}", 1.4) for p in range(6)) + (("out", 2.0),) + tuple(
    (f"up{b}", 1.7) for b in range(4)
) + (("down", 3.0),)


def forward_plan():
    events = []
    z_free = 5.0
    xy_free = 0.0
    ready = {}
    jobs = []
    for k, (g, first, count) in enumerate(PARTS):
        share = count / 96.0
        z_start = z_free
        z_free = z_start + 12.6 * share
        jobs.append([z_free + 1.5, k, "xy", 9.9 * share])
        events.append((z_start if k else 0.0, 0, "z", k))
    done = []
    jobs.sort()
    while jobs:
        jobs.sort(key=lambda j: (max(j[0], xy_free), 0 if j[2] == "dg" else 1, j[1]))
        at, k, kind, cost = jobs.pop(0)
        start = max(at, xy_free)
        xy_free = start + cost
        share = PARTS[k][2] / 96.0
        if kind == "xy":
            events.append((at, 1, "xy", k))
            jobs.append([xy_free + 1.5, k, "dg", 5.1 * share])
        else:
            events.append((at, 2, "dg", k))
            events.append((xy_free + 1.5, 3, "last", k))
            events.append((xy_free + 1.5 + 2.0, 4, "fin", k))
            ready[PARTS[k][0]] = xy_free + 3.5 + 2.0
    events.sort()
    order, now, pos = [], 0.0, 0
    for layer in range(2):
        for name, cost in UNIT_TIMES:
            need = {"joint": 0, "up0": 1, "down": 2}.get(name)
            start = now
            if need is not None:
                start = max(now, ready[3 * layer + need])
            while pos < len(events) and events[pos][0] <= start + 0.3:
                order.append(events[pos][2:])
                pos += 1
            order.append(("run", layer, name))
            now = start + cost
    assert pos == len(events)
    return order


def forward_kernel(
    tokens, seg, vecs, joint_w, output_w, expand_w, shrink_w,
    whole, vec_out, x_saved, j_saved, c_saved, l_saved, n1_saved, r1_saved, g_saved, gp_saved, n2_saved, r2_saved, final, squares,
    stage, sbuf, wv, bias, x1, h, hb, xb, joint, ctx, logsum, n1, r1, g, gp, n2, r2, vg, vec,
    sems, stage_sems, wv_sems, vec_sems, out_sems,
):
    masters = (joint_w, output_w, expand_w, shrink_w)
    gather = Gather(whole, sbuf, sems)
    q, z, c = gather.q, gather.z, gather.c

    def stage_copies(grp):
        layer, kind = divmod(grp, 3)
        slot = grp % 2
        out = []
        for b in range(4):
            if kind == 0:
                src = output_w.at[layer] if b == 3 else joint_w.at[layer, :, pl.ds(768 * b, 768)]
            elif kind == 1:
                src = expand_w.at[layer, :, pl.ds(768 * b, 768)]
            else:
                src = shrink_w.at[layer, pl.ds(96 * b, 96), :]
            out.append(pltpu.make_async_copy(src, stage.at[slot, b], stage_sems.at[slot, b]))
        return out

    def take(grp):
        layer, kind = divmod(grp, 3)
        slot = grp % 2
        for cp in stage_copies(grp):
            cp.wait()
        sums = []
        for b in range(4):
            value = stage[slot, b]
            sbuf[grp, b] = value.astype(BF)
            sums.append(jnp.sum(value * value, axis=0, keepdims=True))
        if kind == 0:
            squares[4 * layer : 4 * layer + 1, :] = sums[0] + sums[1] + sums[2]
            squares[4 * layer + 1 : 4 * layer + 2, :] = sums[3]
        else:
            row = 4 * layer + 1 + kind
            squares[row : row + 1, :] = sums[0] + sums[1] + sums[2] + sums[3]
        if grp + 2 < GROUPS:
            for cp in stage_copies(grp + 2):
                cp.start()

    for grp in range(2):
        for cp in stage_copies(grp):
            cp.start()
    take(0)
    greet([gather.x_side, gather.y_side, gather.sibling] + gather.planes)
    gather.z_send(0)

    vg[z, c] = vecs[...]

    def vec_copy(zz, peer, slot):
        return pltpu.make_async_remote_copy(
            src_ref=vg.at[zz, c], dst_ref=vg.at[zz, c], send_sem=vec_sems.at[2 * slot], recv_sem=vec_sems.at[2 * slot + 1],
            device_id=peer, device_id_type=MESH,
        )

    def vec_total(slot, count):
        ref = vg.at[0, pl.ds(0, 1)] if count == 1 else (vg.at[0, pl.ds(0, 2)] if count == 2 else vg.at[pl.ds(0, 2)])
        pltpu.make_async_copy(ref, ref, vec_sems.at[slot]).wait()

    for k, peer in enumerate(gather.planes):
        vec_copy(z, peer, k).start()
    take(1)
    take(2)
    take(3)
    for k in range(3):
        vec_copy((z + 3 - k) % 4, gather.planes[0], k).wait_recv()
    for zz in range(4):
        vec_copy(zz, gather.sibling, 3 + zz).start()
    gather.z_send(1)
    take(4)
    take(5)
    build_mask(seg, bias)
    for zz in range(4):
        vec_copy(zz, gather.sibling, 3 + zz).wait_recv()
    lane = lax.broadcasted_iota(jnp.int32, (128, 768), 1)
    spot = lax.broadcasted_iota(jnp.int32, (128, 768), 0)
    for layer in range(2):
        acc = jnp.zeros((16, 768), F32)
        for m in range(8):
            pick = jnp.where((lane == spot + 96 * m) & (spot < 96), 1.0, 0.0).astype(BF)
            first = vg[m // 2, m % 2, 16 * layer : 16 * layer + 8, :]
            rest = [vg[b, m // 4, 16 * layer + 8 + m % 4 : 16 * layer + 9 + m % 4, :] for b in range(4)]
            left = jnp.concatenate([first] + rest + [jnp.zeros((4, 128), F32)], axis=0)
            acc = acc + nn(left.astype(BF), pick)
        vec[layer] = acc

    state = {"sent": 2}
    started = []

    def save(src, dst):
        n = len(started)
        cp = pltpu.make_async_copy(src, dst, out_sems.at[n])
        cp.start()
        started.append(cp)

    def load(grp):
        return pltpu.make_async_copy(whole.at[grp], wv.at[grp % 3], wv_sems.at[grp % 3])

    def event(kind, k):
        if kind == "z":
            return
        if kind == "xy":
            gather.xy_send(k)
            if k + 2 < len(PARTS):
                gather.z_send(k + 2)
        elif kind == "dg":
            gather.diagonal_send(k)
        elif kind == "last":
            gather.last_send(k)
        elif kind == "fin":
            gather.finish(k)
            grp, first, count = PARTS[k]
            if first + count == 96:
                load(grp).start()

    order = forward_plan()
    pos = 0
    while pos < len(order):
        item = order[pos]
        if item[0] != "run":
            event(*item)
            pos += 1
            continue
        _, layer, name = item
        vl = vec.at[layer]
        x_in = tokens if layer == 0 else x1
        xb_in = tokens if layer == 0 else xb
        if name == "joint":
            load(3 * layer).wait()
            joint_forward(xb_in, wv.at[0], vl, joint.at[layer])
            save(joint.at[layer], j_saved.at[layer])
        elif name.startswith("att"):
            hooks, first = {}, int(name[3:])
            p, look = first, pos
            while True:
                it = order[look]
                if it[0] == "run":
                    if not it[2].startswith("att"):
                        break
                    p = int(it[2][3:]) + 1
                else:
                    hooks.setdefault(p, []).append(it)
                look += 1
            tail = hooks.pop(6, [])

            @pl.loop(0, PAIRS)
            def _(p):
                for at, items in hooks.items():
                    @pl.when(p == at)
                    def _():
                        for it in items:
                            event(*it)
                attend_forward_pair(p, joint.at[layer], bias, ctx.at[layer], logsum.at[layer])

            for it in tail:
                event(*it)
            save(ctx.at[layer], c_saved.at[layer])
            save(logsum.at[layer], l_saved.at[layer])
            pos = look
            continue
        elif name == "out":
            out_forward(ctx.at[layer], x_in, wv.at[0, 3], vl, n1.at[layer], r1.at[layer], h, hb)
            save(n1.at[layer], n1_saved.at[layer])
            save(r1.at[layer], r1_saved.at[layer])
        elif name.startswith("up"):
            b = int(name[2:])
            if b == 0:
                load(3 * layer + 1).wait()
            ffn_up(hb, wv.at[1], vl, g.at[layer], gp.at[layer], b)
            if b == 3:
                save(g.at[layer], g_saved.at[layer])
                save(gp.at[layer], gp_saved.at[layer])
        else:
            load(3 * layer + 2).wait()
            ffn_down(g.at[layer], wv.at[2], vl, h, n2.at[layer], r2.at[layer], x1 if layer == 0 else None, xb if layer == 0 else hb)
            save(n2.at[layer], n2_saved.at[layer])
            save(r2.at[layer], r2_saved.at[layer])
            if layer == 0:
                save(xb, x_saved)
            else:
                save(hb, final)
        pos += 1
    save(vec, vec_out)
    for k in range(len(PARTS)):
        gather.drain(k)
    for k in range(3):
        vec_copy(z, gather.planes[k], k).wait_send()
    for zz in range(4):
        vec_copy(zz, gather.sibling, 3 + zz).wait_send()
    for cp in started:
        cp.wait()


def forward_call(tokens, seg, vecs, joint_w, output_w, expand_w, shrink_w):
    sd = jax.ShapeDtypeStruct
    any_spec = pl.BlockSpec(memory_space=pl.ANY)
    vm = pl.BlockSpec(memory_space=pltpu.VMEM)
    V = pltpu.VMEM
    saved = [
        sd((6, 4, 768, 768), BF),
        sd((2, 16, 768), F32),
        sd((T, D), BF),
        sd((2, 3, T, D), BF),
        sd((2, T, D), BF),
        sd((2, 6, 2, T), F32),
        sd((2, T, D), BF),
        sd((2, T, 128), F32),
        sd((2, 4, T, D), BF),
        sd((2, 4, T, D), BF),
        sd((2, T, D), BF),
        sd((2, T, 128), F32),
        sd((T, D), BF),
        sd((8, 768), F32),
    ]
    scratch = [
        V((2, 4, 96, 768), F32),
        V((6, 4, 96, 768), BF),
        V((3, 4, 768, 768), BF),
        V((T, T), F32),
        V((T, D), F32),
        V((T, D), F32),
        V((T, D), BF),
        V((T, D), BF),
        V((2, 3, T, D), BF),
        V((2, T, D), BF),
        V((2, 6, 2, T), F32),
        V((2, T, D), BF),
        V((2, T, 128), F32),
        V((2, 4, T, D), BF),
        V((2, 4, T, D), BF),
        V((2, T, D), BF),
        V((2, T, 128), F32),
        V((4, 2, 32, 128), F32),
        V((2, 16, 768), F32),
        pltpu.SemaphoreType.DMA((len(PARTS), 13)),
        pltpu.SemaphoreType.DMA((2, 4)),
        pltpu.SemaphoreType.DMA((3,)),
        pltpu.SemaphoreType.DMA((14,)),
        pltpu.SemaphoreType.DMA((24,)),
    ]
    return pl.pallas_call(
        forward_kernel,
        out_shape=saved,
        in_specs=[vm, vm, vm] + [any_spec] * 4,
        out_specs=[any_spec] * 13 + [vm],
        scratch_shapes=scratch,
        compiler_params=pltpu.CompilerParams(
            collective_id=0, has_side_effects=True, vmem_limit_bytes=62 << 20
        ),
        name="forward",
    )(tokens, seg, vecs, joint_w, output_w, expand_w, shrink_w)


def pack_vectors(norm_gains, biases, hidden_bias):
    parts = []
    for layer in range(2):
        parts.append(norm_gains[layer])
        parts.append(biases[layer])
        parts.append(hidden_bias[layer].reshape(4, 96))
        parts.append(jnp.zeros((4, 96), F32))
    rows = jnp.concatenate(parts, axis=0)
    return jnp.pad(rows, ((0, 0), (0, 32)))


def backward_call(dy, xb, seg, whole, layer, vec, saved):
    joint, ctx, logsum, n1, r1, g, gp, n2, r2 = saved

    def kernel(dy, xb, seg, whole, vec, joint, ctx, logsum, n1, r1, g, gp, n2, r2, dx, ga, ge, gs, sums, bias, du, dob, at, hb, dz, dc, dj):
        wa, we, ws = whole.at[0], whole.at[1], whole.at[2]
        build_mask(seg, bias)
        sums[...] = jnp.zeros_like(sums)
        norm_backward(dy, n2, r2, vec[1:2, :], du, dob, sums, (1, 7, 6))
        for b in range(4):
            ffn_back_block(dob, ws, g, gp, dz, sums, b)
            transpose_into(g.at[b], at)
            weight_grad(at, dob, gs.at[b])
        hb[...] = (n1[...].astype(F32) * vec[0:1, :] + vec[5:6, :]).astype(BF)
        transpose_into(hb, at)
        for b in range(4):
            weight_grad(at, dz.at[b], ge.at[b])
        ffn_back_input(dz, we, du)
        norm_backward(du, n1, r1, vec[0:1, :], du, dob, sums, (0, 5, 4))
        transpose_into(ctx, at)
        weight_grad(at, dob, ga.at[3])
        context_back(dob, wa.at[3], dc)

        @pl.loop(0, PAIRS)
        def _(p):
            attend_backward_pair(p, joint, bias, logsum, dc, dj)

        transpose_into(xb, at)
        for b in range(3):
            weight_grad(at, dj.at[b], ga.at[b])
        input_back(dj, wa, du, dx, sums)

    sd = jax.ShapeDtypeStruct
    V = pltpu.VMEM
    VM = pl.BlockSpec(memory_space=pltpu.VMEM)
    return pl.pallas_call(
        kernel,
        out_shape=[sd((512, 768), F32), sd((4, 768, 768), BF), sd((4, 768, 768), BF), sd((4, 768, 768), BF), sd((16, 768), F32)],
        in_specs=[VM] * 14,
        out_specs=[VM] * 5,
        scratch_shapes=[V((512, 512), F32), V((512, 768), F32), V((512, 768), BF), V((768, 512), BF), V((512, 768), BF), V((4, 512, 768), BF), V((512, 768), BF), V((3, 512, 768), BF)],
        compiler_params=pltpu.CompilerParams(vmem_limit_bytes=63 << 20),
        name="backward",
    )(dy, xb, seg, whole, vec, joint, ctx, logsum, n1, r1, g, gp, n2, r2)


def local_kernels(
    tokens,
    segments,
    cotangent,
    joint_weight,
    output_weight,
    expand_weight,
    shrink_weight,
    norm_gains,
    biases,
    hidden_bias,
    joint_rows,
    joint_columns,
    output_rows,
    output_columns,
    expand_rows,
    expand_columns,
    shrink_rows,
    shrink_columns,
    gain_moments,
    bias_moments,
    hidden_moments,
):
    row_count, slot_count, features = tokens.shape
    vecs = pack_vectors(norm_gains, biases, hidden_bias)
    (whole, vec, x_saved, j_s, c_s, l_s, n1_s, r1_s, g_s, gp_s, n2_s, r2_s, final, squares) = forward_call(
        tokens[0], segments, vecs, joint_weight, output_weight, expand_weight, shrink_weight
    )
    activations = final[None]
    grad = cotangent[0]
    blocks, sums_list = [], []
    for number in (1, 0):
        saved = (j_s[number], c_s[number], l_s[number], n1_s[number], r1_s[number], g_s[number], gp_s[number], n2_s[number], r2_s[number])
        grad, ga, ge, gs, sums = backward_call(
            grad, tokens[0] if number == 0 else x_saved, segments, whole[3 * number : 3 * number + 3], number, vec[number], saved
        )
        blocks.append((
            lax.psum(lax.psum_scatter(ga, "fsdp", scatter_dimension=1, tiled=True), "dp"),
            lax.psum(lax.psum_scatter(ge, "fsdp", scatter_dimension=1, tiled=True), "dp"),
            lax.psum(lax.psum_scatter(gs.reshape(3072, 768), "fsdp", scatter_dimension=0, tiled=True), "dp"),
        ))
        sums_list.append(sums)
    sums = lax.psum(jnp.stack(sums_list[::-1]), ("dp", "fsdp"))
    f = lax.axis_index("fsdp")
    mine = lax.dynamic_slice_in_dim(sums[:, :8], f * 96, 96, axis=2)
    hidden_mine = lax.dynamic_slice_in_dim(sums[:, 8:12].reshape(2, 3072), f * 384, 384, axis=1)
    collected = []
    for number in range(2):
        ga, ge, gs = blocks[1 - number]
        collected.append((
            ga[:3].transpose(1, 0, 2).reshape(96, 2304).astype(jnp.float32),
            ga[3].astype(jnp.float32),
            ge.transpose(1, 0, 2).reshape(96, 3072).astype(jnp.float32),
            gs.astype(jnp.float32),
            mine[number, :2],
            mine[number, 2:8],
            hidden_mine[number],
        ))
    input_gradient = grad.astype(jnp.bfloat16)[None]
    fsdp_count = lax.axis_size("fsdp")
    token_total = row_count * slot_count * lax.axis_size("dp") * fsdp_count
    root_scale = 1.0 / math.sqrt(token_total)
    stacked_grads = [
        jnp.stack([entry[index] for entry in collected]) * root_scale for index in range(7)
    ]
    matrices = (
        (stacked_grads[0], joint_weight, joint_rows, joint_columns),
        (stacked_grads[1], output_weight, output_rows, output_columns),
        (stacked_grads[2], expand_weight, expand_rows, expand_columns),
        (stacked_grads[3], shrink_weight, shrink_rows, shrink_columns),
    )
    partial_list = [factored_partials(item[0], item[1], item[2]) for item in matrices]
    vectors = (
        (stacked_grads[4], norm_gains, gain_moments),
        (stacked_grads[5], biases, bias_moments),
        (stacked_grads[6][:, None, :], hidden_bias[:, None, :], hidden_moments[:, None, :]),
    )
    vector_list = [vector_partials(item[0], item[2]) for item in vectors]
    vector_squares = jnp.concatenate(
        [jnp.sum(item[1] * item[1], axis=2) for item in vectors], axis=1
    )
    statistics = lax.psum(
        (
            partial_list[0][1],
            partial_list[1][1],
            partial_list[2][1],
            partial_list[3][1],
            jnp.stack([item[2] for item in partial_list], axis=1),
            jnp.stack([item[3] for item in partial_list], axis=1),
            vector_squares,
        ),
        "fsdp",
    )
    updates = []
    columns_list = []
    for index in range(4):
        gradient = matrices[index][0]
        total_rows = gradient.shape[1] * fsdp_count
        rows_next = partial_list[index][0]
        columns_next = DECAY_RATE * matrices[index][3] + (1.0 - DECAY_RATE) * (
            statistics[index] / total_rows
        )
        row_average = statistics[4][:, index] / total_rows
        estimate = rows_next[:, :, None] * columns_next[:, None, :] / row_average[:, None, None]
        updates.append(gradient * lax.rsqrt(estimate))
        columns_list.append(columns_next)
    matrix_squares = jnp.stack([jnp.sum(item * item, axis=(1, 2)) for item in updates], axis=1)
    vector_updates = jnp.concatenate(
        [jnp.sum(item[1] * item[1], axis=2) for item in vector_list], axis=1
    )
    norms = lax.psum((matrix_squares, vector_updates), "fsdp")
    matrix_next = []
    for index in range(4):
        gradient = matrices[index][0]
        entry_count = gradient.shape[1] * fsdp_count * gradient.shape[2]
        clip_ratio = jnp.sqrt(norms[0][:, index] / entry_count) / CLIP_LIMIT
        update = updates[index] / jnp.maximum(clip_ratio, 1.0)[:, None, None]
        stride = STEP_RATE * jnp.maximum(
            FLOOR_SCALE, jnp.sqrt(statistics[5][:, index] / entry_count)
        )
        matrix_next.append(matrices[index][1] - stride[:, None, None] * update)
    vector_next = []
    offset = 0
    for index in range(3):
        gradient = vectors[index][0]
        kinds = gradient.shape[1]
        entry_count = gradient.shape[2] * fsdp_count
        clip_ratio = jnp.sqrt(norms[1][:, offset : offset + kinds] / entry_count) / CLIP_LIMIT
        update = vector_list[index][1] / jnp.maximum(clip_ratio, 1.0)[:, :, None]
        stride = STEP_RATE * jnp.maximum(
            FLOOR_SCALE, jnp.sqrt(statistics[6][:, offset : offset + kinds] / entry_count)
        )
        vector_next.append(vectors[index][1] - stride[:, :, None] * update)
        offset = offset + kinds
    return (
        activations,
        input_gradient,
        stacked_grads[0],
        stacked_grads[1],
        stacked_grads[2],
        stacked_grads[3],
        stacked_grads[4],
        stacked_grads[5],
        stacked_grads[6],
        matrix_next[0],
        matrix_next[1],
        matrix_next[2],
        matrix_next[3],
        vector_next[0],
        vector_next[1],
        vector_next[2][:, 0, :],
        matrix_next[0].astype(jnp.bfloat16),
        matrix_next[1].astype(jnp.bfloat16),
        matrix_next[2].astype(jnp.bfloat16),
        matrix_next[3].astype(jnp.bfloat16),
        partial_list[0][0],
        columns_list[0],
        partial_list[1][0],
        columns_list[1],
        partial_list[2][0],
        columns_list[2],
        partial_list[3][0],
        columns_list[3],
        vector_list[0][0],
        vector_list[1][0],
        vector_list[2][0][:, 0, :],
    )


def solution(mesh):
    placed = (
        P(("dp", "fsdp"), None, None),
        P(("dp", "fsdp"), None),
        P(("dp", "fsdp"), None, None),
        P(None, "fsdp", None),
        P(None, "fsdp", None),
        P(None, "fsdp", None),
        P(None, "fsdp", None),
        P(None, None, "fsdp"),
        P(None, None, "fsdp"),
        P(None, "fsdp"),
        P(None, "fsdp"),
        P(),
        P(None, "fsdp"),
        P(),
        P(None, "fsdp"),
        P(),
        P(None, "fsdp"),
        P(),
        P(None, None, "fsdp"),
        P(None, None, "fsdp"),
        P(None, "fsdp"),
    )
    known = dict(mesh.shape) == {"dp": 4, "fsdp": 8}
    return jax.shard_map(
        local_kernels if known else local_plain,
        mesh=mesh,
        in_specs=placed,
        out_specs=(
            P(("dp", "fsdp"), None, None),
            P(("dp", "fsdp"), None, None),
            P(None, "fsdp", None),
            P(None, "fsdp", None),
            P(None, "fsdp", None),
            P(None, "fsdp", None),
            P(None, None, "fsdp"),
            P(None, None, "fsdp"),
            P(None, "fsdp"),
            P(None, "fsdp", None),
            P(None, "fsdp", None),
            P(None, "fsdp", None),
            P(None, "fsdp", None),
            P(None, None, "fsdp"),
            P(None, None, "fsdp"),
            P(None, "fsdp"),
            P(None, "fsdp", None),
            P(None, "fsdp", None),
            P(None, "fsdp", None),
            P(None, "fsdp", None),
            P(None, "fsdp"),
            P(),
            P(None, "fsdp"),
            P(),
            P(None, "fsdp"),
            P(),
            P(None, "fsdp"),
            P(),
            P(None, None, "fsdp"),
            P(None, None, "fsdp"),
            P(None, "fsdp"),
        ),
        check_vma=False,
    )
```

```python
from functools import partial
import math

import jax
import jax.numpy as jnp
from jax import lax
from jax.sharding import PartitionSpec as P
from jax.experimental import pallas as pl
from jax.experimental.pallas import tpu as pltpu

HEADS = 12
HEAD_SIZE = 64


NORM_EPSILON = 1e-12
SCORE_SCALE = 0.125
MASK_VALUE = -1e30
FLOOR_SQUARE = 1e-30
FLOOR_SCALE = 0.001
DECAY_RATE = 0.5
CLIP_LIMIT = 0.25
STEP_RATE = 4.0


def product(left, right):
    return jnp.dot(left, right, preferred_element_type=jnp.float32)


def product_left(left, right):
    return lax.dot_general(
        left, right, (((0,), (0,)), ((), ())), preferred_element_type=jnp.float32
    )


def product_right(left, right):
    return lax.dot_general(
        left, right, (((1,), (1,)), ((), ())), preferred_element_type=jnp.float32
    )


def normalize(values):
    average = jnp.mean(values, axis=-1, keepdims=True)
    centered = values - average
    variance = jnp.mean(centered * centered, axis=-1, keepdims=True)
    inverse = lax.rsqrt(variance + NORM_EPSILON)
    return (centered * inverse, inverse)


def normalize_back(grad_scaled, scaled, inverse):
    first_mean = jnp.mean(grad_scaled, axis=-1, keepdims=True)
    second_mean = jnp.mean(grad_scaled * scaled, axis=-1, keepdims=True)
    return inverse * (grad_scaled - first_mean - scaled * second_mean)


def split_heads(joint_row):
    slot_count = joint_row.shape[0]
    shaped = joint_row.reshape(slot_count, 3, HEADS, HEAD_SIZE)
    return (shaped[:, 0], shaped[:, 1], shaped[:, 2])


def masked_scores(query_rows, key_rows, segment_row):
    scores = (
        jnp.einsum("qhe,khe->hqk", query_rows, key_rows, preferred_element_type=jnp.float32)
        * SCORE_SCALE
    )
    allowed = segment_row[:, None] == segment_row[None, :]
    return jnp.where(allowed[None], scores, MASK_VALUE)


def attend_forward(packed):
    joint_row, segment_row = packed
    query_rows, key_rows, value_rows = split_heads(joint_row)
    scores = masked_scores(query_rows, key_rows, segment_row)
    highest = jnp.max(scores, axis=-1, keepdims=True)
    raised = jnp.exp(scores - highest)
    denominator = jnp.sum(raised, axis=-1, keepdims=True)
    weights = (raised / denominator).astype(jnp.bfloat16)
    context = jnp.einsum("hqk,khe->qhe", weights, value_rows, preferred_element_type=jnp.float32)
    logsum = (highest + jnp.log(denominator))[:, :, 0]
    return (context.astype(jnp.bfloat16).reshape(joint_row.shape[0], HEADS * HEAD_SIZE), logsum)


def attend_backward(packed):
    joint_row, segment_row, logsum, grad_row = packed
    slot_count = joint_row.shape[0]
    query_rows, key_rows, value_rows = split_heads(joint_row)
    scores = masked_scores(query_rows, key_rows, segment_row)
    probabilities = jnp.exp(scores - logsum[:, :, None])
    upstream = grad_row.reshape(slot_count, HEADS, HEAD_SIZE)
    grad_probs = jnp.einsum(
        "qhe,khe->hqk", upstream, value_rows, preferred_element_type=jnp.float32
    )
    row_delta = jnp.sum(probabilities * grad_probs, axis=-1, keepdims=True)
    grad_scores = (probabilities * (grad_probs - row_delta)).astype(jnp.bfloat16)
    grad_query = (
        jnp.einsum("hqk,khe->qhe", grad_scores, key_rows, preferred_element_type=jnp.float32)
        * SCORE_SCALE
    )
    grad_key = (
        jnp.einsum("hqk,qhe->khe", grad_scores, query_rows, preferred_element_type=jnp.float32)
        * SCORE_SCALE
    )
    grad_value = jnp.einsum(
        "hqk,qhe->khe",
        probabilities.astype(jnp.bfloat16),
        upstream,
        preferred_element_type=jnp.float32,
    )
    stacked = jnp.stack([grad_query, grad_key, grad_value], axis=1)
    return stacked.reshape(slot_count, 3 * HEADS * HEAD_SIZE).astype(jnp.bfloat16)


def block_forward(hidden_in, segments, weights):
    joint_matrix, output_matrix, expand_matrix, shrink_matrix, gain_rows, bias_rows, inner_bias = (
        weights
    )
    gain_values = gain_rows.astype(jnp.float32)
    bias_values = bias_rows.astype(jnp.float32)
    row_count, slot_count = segments.shape
    zero_block = jnp.zeros_like(bias_values[0])
    joint_bias = jnp.concatenate([bias_values[0], zero_block, bias_values[1]])
    joint_out = (product(hidden_in.astype(jnp.bfloat16), joint_matrix) + joint_bias).astype(
        jnp.bfloat16
    )
    context, logsum = lax.map(
        attend_forward, (joint_out.reshape(row_count, slot_count, -1), segments)
    )
    context = context.reshape(row_count * slot_count, -1)
    attended = product(context, output_matrix) + bias_values[2]
    first_scaled, first_inverse = normalize(hidden_in + attended)
    first_norm = first_scaled * gain_values[0] + bias_values[3]
    pre_active = product(first_norm.astype(jnp.bfloat16), expand_matrix) + inner_bias.astype(
        jnp.float32
    )
    active = jax.nn.gelu(pre_active, approximate=False).astype(jnp.bfloat16)
    branch = product(active, shrink_matrix) + bias_values[4]
    second_scaled, second_inverse = normalize(first_norm + branch)
    result = second_scaled * gain_values[1] + bias_values[5]
    stored = (
        hidden_in,
        joint_out,
        context,
        logsum,
        first_scaled,
        first_inverse,
        pre_active,
        second_scaled,
        second_inverse,
    )
    return (result, stored)


def block_backward(grad_out, segments, weights, stored):
    joint_matrix, output_matrix, expand_matrix, shrink_matrix, gain_rows, bias_rows, inner_bias = (
        weights
    )
    (
        hidden_in,
        joint_out,
        context,
        logsum,
        first_scaled,
        first_inverse,
        pre_active,
        second_scaled,
        second_inverse,
    ) = stored
    gain_values = gain_rows.astype(jnp.float32)
    bias_values = bias_rows.astype(jnp.float32)
    row_count, slot_count = segments.shape
    features = hidden_in.shape[1]
    grad_second_bias = jnp.sum(grad_out, axis=0)
    grad_second_gain = jnp.sum(grad_out * second_scaled, axis=0)
    grad_sum = normalize_back(grad_out * gain_values[1], second_scaled, second_inverse)
    grad_branch = grad_sum.astype(jnp.bfloat16)
    active, gelu_back = jax.vjp(partial(jax.nn.gelu, approximate=False), pre_active)
    grad_shrink = product_left(active.astype(jnp.bfloat16), grad_branch)
    grad_active = product_right(grad_branch, shrink_matrix)
    grad_pre = gelu_back(grad_active)[0].astype(jnp.bfloat16)
    first_norm = first_scaled * gain_values[0] + bias_values[3]
    grad_expand = product_left(first_norm.astype(jnp.bfloat16), grad_pre)
    grad_first = grad_sum + product_right(grad_pre, expand_matrix)
    grad_first_bias = jnp.sum(grad_first, axis=0)
    grad_first_gain = jnp.sum(grad_first * first_scaled, axis=0)
    grad_middle = normalize_back(grad_first * gain_values[0], first_scaled, first_inverse)
    grad_attended = grad_middle.astype(jnp.bfloat16)
    grad_output = product_left(context, grad_attended)
    grad_context = product_right(grad_attended, output_matrix).astype(jnp.bfloat16)
    grad_joint_out = lax.map(
        attend_backward,
        (
            joint_out.reshape(row_count, slot_count, -1),
            segments,
            logsum,
            grad_context.reshape(row_count, slot_count, -1),
        ),
    )
    grad_joint_out = grad_joint_out.reshape(row_count * slot_count, -1)
    grad_joint = product_left(hidden_in.astype(jnp.bfloat16), grad_joint_out)
    grad_input = grad_middle + product_right(grad_joint_out, joint_matrix)
    joint_sums = jnp.sum(grad_joint_out, axis=0, dtype=jnp.float32)
    bias_grads = jnp.stack(
        [
            joint_sums[:features],
            joint_sums[2 * features :],
            jnp.sum(grad_attended, axis=0, dtype=jnp.float32),
            grad_first_bias,
            jnp.sum(grad_branch, axis=0, dtype=jnp.float32),
            grad_second_bias,
        ]
    )
    gain_grads = jnp.stack([grad_first_gain, grad_second_gain])
    inner_grad = jnp.sum(grad_pre, axis=0, dtype=jnp.float32)
    return (
        grad_input,
        (grad_joint, grad_output, grad_expand, grad_shrink, gain_grads, bias_grads, inner_grad),
    )


def factored_partials(gradient, weight, rows_old):
    squared = gradient * gradient + FLOOR_SQUARE
    rows_next = DECAY_RATE * rows_old + (1.0 - DECAY_RATE) * jnp.mean(squared, axis=2)
    return (
        rows_next,
        jnp.sum(squared, axis=1),
        jnp.sum(rows_next, axis=1),
        jnp.sum(weight * weight, axis=(1, 2)),
    )


def vector_partials(gradient, moments_old):
    moments_next = DECAY_RATE * moments_old + (1.0 - DECAY_RATE) * (
        gradient * gradient + FLOOR_SQUARE
    )
    return (moments_next, gradient * lax.rsqrt(moments_next))


def local_plain(
    tokens,
    segments,
    cotangent,
    joint_weight,
    output_weight,
    expand_weight,
    shrink_weight,
    norm_gains,
    biases,
    hidden_bias,
    joint_rows,
    joint_columns,
    output_rows,
    output_columns,
    expand_rows,
    expand_columns,
    shrink_rows,
    shrink_columns,
    gain_moments,
    bias_moments,
    hidden_moments,
):
    layers = joint_weight.shape[0]
    row_count, slot_count, features = tokens.shape
    hidden = tokens.astype(jnp.float32).reshape(row_count * slot_count, features)
    gathered_list = []
    stored_list = []
    for number in range(layers):
        weights = (
            lax.all_gather(joint_weight[number].astype(jnp.bfloat16), "fsdp", axis=0, tiled=True),
            lax.all_gather(output_weight[number].astype(jnp.bfloat16), "fsdp", axis=0, tiled=True),
            lax.all_gather(expand_weight[number].astype(jnp.bfloat16), "fsdp", axis=0, tiled=True),
            lax.all_gather(shrink_weight[number].astype(jnp.bfloat16), "fsdp", axis=0, tiled=True),
            lax.all_gather(norm_gains[number].astype(jnp.bfloat16), "fsdp", axis=1, tiled=True),
            lax.all_gather(biases[number].astype(jnp.bfloat16), "fsdp", axis=1, tiled=True),
            lax.all_gather(hidden_bias[number].astype(jnp.bfloat16), "fsdp", axis=0, tiled=True),
        )
        hidden, stored = block_forward(hidden, segments, weights)
        gathered_list.append(weights)
        stored_list.append(stored)
    activations = hidden.reshape(row_count, slot_count, features).astype(jnp.bfloat16)
    grad_hidden = cotangent.astype(jnp.float32).reshape(row_count * slot_count, features)
    collected = []
    for number in reversed(range(layers)):
        weights = (
            lax.all_gather(joint_weight[number].astype(jnp.bfloat16), "fsdp", axis=0, tiled=True),
            lax.all_gather(output_weight[number].astype(jnp.bfloat16), "fsdp", axis=0, tiled=True),
            lax.all_gather(expand_weight[number].astype(jnp.bfloat16), "fsdp", axis=0, tiled=True),
            lax.all_gather(shrink_weight[number].astype(jnp.bfloat16), "fsdp", axis=0, tiled=True),
            lax.all_gather(norm_gains[number].astype(jnp.bfloat16), "fsdp", axis=1, tiled=True),
            lax.all_gather(biases[number].astype(jnp.bfloat16), "fsdp", axis=1, tiled=True),
            lax.all_gather(hidden_bias[number].astype(jnp.bfloat16), "fsdp", axis=0, tiled=True),
        )
        grad_hidden, local_grads = block_backward(
            grad_hidden, segments, weights, stored_list[number]
        )
        grad_joint, grad_output, grad_expand, grad_shrink, gain_grads, bias_grads, inner_grad = (
            local_grads
        )
        shards = (
            lax.psum_scatter(grad_joint, "fsdp", scatter_dimension=0, tiled=True),
            lax.psum_scatter(grad_output, "fsdp", scatter_dimension=0, tiled=True),
            lax.psum_scatter(grad_expand, "fsdp", scatter_dimension=0, tiled=True),
            lax.psum_scatter(grad_shrink, "fsdp", scatter_dimension=0, tiled=True),
            lax.psum_scatter(gain_grads, "fsdp", scatter_dimension=1, tiled=True),
            lax.psum_scatter(bias_grads, "fsdp", scatter_dimension=1, tiled=True),
            lax.psum_scatter(inner_grad, "fsdp", scatter_dimension=0, tiled=True),
        )
        summed = (
            lax.psum(shards[0].astype(jnp.bfloat16), "dp").astype(jnp.float32),
            lax.psum(shards[1].astype(jnp.bfloat16), "dp").astype(jnp.float32),
            lax.psum(shards[2].astype(jnp.bfloat16), "dp").astype(jnp.float32),
            lax.psum(shards[3].astype(jnp.bfloat16), "dp").astype(jnp.float32),
            lax.psum(shards[4].astype(jnp.bfloat16), "dp").astype(jnp.float32),
            lax.psum(shards[5].astype(jnp.bfloat16), "dp").astype(jnp.float32),
            lax.psum(shards[6].astype(jnp.bfloat16), "dp").astype(jnp.float32),
        )
        collected.append(summed)
    collected = collected[::-1]
    input_gradient = grad_hidden.reshape(row_count, slot_count, features).astype(jnp.bfloat16)
    fsdp_count = lax.axis_size("fsdp")
    token_total = row_count * slot_count * lax.axis_size("dp") * fsdp_count
    root_scale = 1.0 / math.sqrt(token_total)
    stacked_grads = [
        jnp.stack([entry[index] for entry in collected]) * root_scale for index in range(7)
    ]
    matrices = (
        (stacked_grads[0], joint_weight, joint_rows, joint_columns),
        (stacked_grads[1], output_weight, output_rows, output_columns),
        (stacked_grads[2], expand_weight, expand_rows, expand_columns),
        (stacked_grads[3], shrink_weight, shrink_rows, shrink_columns),
    )
    partial_list = [factored_partials(item[0], item[1], item[2]) for item in matrices]
    vectors = (
        (stacked_grads[4], norm_gains, gain_moments),
        (stacked_grads[5], biases, bias_moments),
        (stacked_grads[6][:, None, :], hidden_bias[:, None, :], hidden_moments[:, None, :]),
    )
    vector_list = [vector_partials(item[0], item[2]) for item in vectors]
    vector_squares = jnp.concatenate(
        [jnp.sum(item[1] * item[1], axis=2) for item in vectors], axis=1
    )
    statistics = lax.psum(
        (
            partial_list[0][1],
            partial_list[1][1],
            partial_list[2][1],
            partial_list[3][1],
            jnp.stack([item[2] for item in partial_list], axis=1),
            jnp.stack([item[3] for item in partial_list], axis=1),
            vector_squares,
        ),
        "fsdp",
    )
    updates = []
    columns_list = []
    for index in range(4):
        gradient = matrices[index][0]
        total_rows = gradient.shape[1] * fsdp_count
        rows_next = partial_list[index][0]
        columns_next = DECAY_RATE * matrices[index][3] + (1.0 - DECAY_RATE) * (
            statistics[index] / total_rows
        )
        row_average = statistics[4][:, index] / total_rows
        estimate = rows_next[:, :, None] * columns_next[:, None, :] / row_average[:, None, None]
        updates.append(gradient * lax.rsqrt(estimate))
        columns_list.append(columns_next)
    matrix_squares = jnp.stack([jnp.sum(item * item, axis=(1, 2)) for item in updates], axis=1)
    vector_updates = jnp.concatenate(
        [jnp.sum(item[1] * item[1], axis=2) for item in vector_list], axis=1
    )
    norms = lax.psum((matrix_squares, vector_updates), "fsdp")
    matrix_next = []
    for index in range(4):
        gradient = matrices[index][0]
        entry_count = gradient.shape[1] * fsdp_count * gradient.shape[2]
        clip_ratio = jnp.sqrt(norms[0][:, index] / entry_count) / CLIP_LIMIT
        update = updates[index] / jnp.maximum(clip_ratio, 1.0)[:, None, None]
        stride = STEP_RATE * jnp.maximum(
            FLOOR_SCALE, jnp.sqrt(statistics[5][:, index] / entry_count)
        )
        matrix_next.append(matrices[index][1] - stride[:, None, None] * update)
    vector_next = []
    offset = 0
    for index in range(3):
        gradient = vectors[index][0]
        kinds = gradient.shape[1]
        entry_count = gradient.shape[2] * fsdp_count
        clip_ratio = jnp.sqrt(norms[1][:, offset : offset + kinds] / entry_count) / CLIP_LIMIT
        update = vector_list[index][1] / jnp.maximum(clip_ratio, 1.0)[:, :, None]
        stride = STEP_RATE * jnp.maximum(
            FLOOR_SCALE, jnp.sqrt(statistics[6][:, offset : offset + kinds] / entry_count)
        )
        vector_next.append(vectors[index][1] - stride[:, :, None] * update)
        offset = offset + kinds
    return (
        activations,
        input_gradient,
        stacked_grads[0],
        stacked_grads[1],
        stacked_grads[2],
        stacked_grads[3],
        stacked_grads[4],
        stacked_grads[5],
        stacked_grads[6],
        matrix_next[0],
        matrix_next[1],
        matrix_next[2],
        matrix_next[3],
        vector_next[0],
        vector_next[1],
        vector_next[2][:, 0, :],
        matrix_next[0].astype(jnp.bfloat16),
        matrix_next[1].astype(jnp.bfloat16),
        matrix_next[2].astype(jnp.bfloat16),
        matrix_next[3].astype(jnp.bfloat16),
        partial_list[0][0],
        columns_list[0],
        partial_list[1][0],
        columns_list[1],
        partial_list[2][0],
        columns_list[2],
        partial_list[3][0],
        columns_list[3],
        vector_list[0][0],
        vector_list[1][0],
        vector_list[2][0][:, 0, :],
    )


F32 = jnp.float32
BF = jnp.bfloat16
T = 512
D = 768


def nn(a, b):
    return lax.dot_general(a, b, (((1,), (0,)), ((), ())), preferred_element_type=F32)


def nt(a, b):
    return lax.dot_general(a, b, (((1,), (1,)), ((), ())), preferred_element_type=F32)


def rows_at(i, n):
    return pl.ds(pl.multiple_of(i * n, n), n)


def build_mask(seg_ref, bias_ref):
    row = seg_ref[...]
    wide = jnp.broadcast_to(row, (128, T)).T
    for j in range(T // 128):
        bias_ref[:, j * 128 : (j + 1) * 128] = jnp.where(
            wide == row[:, j * 128 : (j + 1) * 128], 0.0, MASK_VALUE
        ).astype(F32)


def joint_forward(xb, wa, vec, joint, tile=256):
    for b in range(3):
        @pl.loop(0, T // tile)
        def _(i, b=b):
            r = rows_at(i, tile)
            out = nn(xb[r, :], wa[b])
            if b == 0:
                out = out + vec[2:3, :]
            if b == 2:
                out = out + vec[3:4, :]
            joint[b, r, :] = out.astype(BF)


def head_masks():
    lane = lax.broadcasted_iota(jnp.int32, (1, 128), 1)
    return [
        jnp.where(lane < 64, 1.0, 0.0).astype(F32),
        jnp.where(lane >= 64, 1.0, 0.0).astype(F32),
    ]


def attend_forward_pair(p, joint, bias, ctx, logsum):
    lanes = pl.ds(pl.multiple_of(p * 128, 128), 128)
    masks = head_masks()
    q2 = joint[0, :, lanes]
    k2 = joint[1, :, lanes]
    vt = joint[2, :, lanes].T
    outs, sums = [], []
    for h in range(2):
        qm = q2 * (masks[h] * 0.125).astype(BF)
        st = nt(k2, qm) + bias[...]
        top = jnp.max(st, axis=0, keepdims=True)
        e = jnp.exp(st - top)
        total = jnp.sum(e, axis=0, keepdims=True)
        ct = nn(vt[64 * h : 64 * h + 64, :], e.astype(BF))
        outs.append(ct * (1.0 / total))
        sums.append(top + jnp.log(total))
    ctx[:, lanes] = jnp.concatenate(outs, axis=0).T.astype(BF)
    logsum[p] = jnp.concatenate(sums, axis=0)


def norm_parts(u):
    avg = jnp.mean(u, axis=-1, keepdims=True)
    c = u - avg
    var = jnp.mean(c * c, axis=-1, keepdims=True)
    inv = lax.rsqrt(var + NORM_EPSILON)
    return c * inv, inv


def out_forward(ctx, x, wo, vec, n1, r1, h, hb, tile=128):
    @pl.loop(0, T // tile)
    def _(i):
        r = rows_at(i, tile)
        u = nn(ctx[r, :], wo[...]) + vec[4:5, :] + x[r, :].astype(F32)
        n, inv = norm_parts(u)
        y = n * vec[0:1, :] + vec[5:6, :]
        n1[r, :] = n.astype(n1.dtype)
        r1[r, :] = jnp.broadcast_to(inv, (tile, 128))
        h[r, :] = y
        hb[r, :] = y.astype(BF)


def gelu_parts(z):
    a = jnp.abs(z)
    e = jnp.exp(z * z * -0.5)
    t = 1.0 / (1.0 + 0.23164189 * a)
    poly = t * (
        0.127414796 + t * (-0.142248368 + t * (0.7107068705 + t * (-0.7265760135 + t * 0.5307027145)))
    )
    tail = poly * e
    cdf = jnp.where(z >= 0.0, 1.0 - tail, tail)
    return z * cdf, cdf + z * (e * 0.3989422804014327)


def ffn_up(hb, we, vec, g, gp, b, tile=128):
    @pl.loop(0, T // tile)
    def _(i):
        r = rows_at(i, tile)
        z = nn(hb[r, :], we[b]) + vec[8 + b : 9 + b, :]
        act, der = gelu_parts(z)
        g[b, r, :] = act.astype(BF)
        gp[b, r, :] = der.astype(BF)


def ffn_down(g, ws, vec, h, n2, r2, x_out, xb_out, tile=128):
    @pl.loop(0, T // tile)
    def _(i):
        r = rows_at(i, tile)
        u = h[r, :] + vec[6:7, :]
        for b in range(4):
            u = u + nn(g[b, r, :], ws[b])
        n, inv = norm_parts(u)
        y = n * vec[1:2, :] + vec[7:8, :]
        n2[r, :] = n.astype(n2.dtype)
        r2[r, :] = jnp.broadcast_to(inv, (tile, 128))
        if x_out is not None:
            x_out[r, :] = y
        xb_out[r, :] = y.astype(BF)


def sum8(v):
    return jnp.sum(v.reshape(v.shape[0] // 8, 8, v.shape[1]), axis=0)


def norm_backward(dy, n, r, gain_row, du, dub, sums, rows, tile=128):
    def step(i, carry):
        s = rows_at(i, tile)
        g = dy[s, :].astype(F32)
        nv = n[s, :].astype(F32)
        inv = r[s, 0:1]
        e = g * gain_row
        m1 = jnp.mean(e, axis=-1, keepdims=True)
        m2 = jnp.mean(e * nv, axis=-1, keepdims=True)
        d = inv * (e - m1 - nv * m2)
        db = d.astype(BF)
        du[s, :] = d
        dub[s, :] = db
        return (
            carry[0] + sum8(g * nv),
            carry[1] + sum8(g),
            carry[2] + sum8(db.astype(F32)),
        )

    zero = jnp.zeros((8, D), F32)
    out = lax.fori_loop(0, T // tile, step, (zero, zero, zero))
    for k in range(3):
        sums[rows[k] : rows[k] + 1, :] = jnp.sum(out[k], axis=0, keepdims=True)


def transpose_into(src, dst, tile=128):
    @pl.loop(0, T // tile)
    def _(i):
        dst[:, rows_at(i, tile)] = src[rows_at(i, tile), :].T


def weight_grad(at, bmat, out, tile=256):
    @pl.loop(0, D // tile)
    def _(i):
        r = rows_at(i, tile)
        out[r, :] = nn(at[r, :], bmat[...]).astype(BF)


def ffn_back_block(dob, ws, gp, dz, sums, b, tile=128):
    def step(i, acc):
        r = rows_at(i, tile)
        v = (nt(dob[r, :], ws[b]) * gp[b, r, :].astype(F32)).astype(BF)
        dz[b, r, :] = v
        return acc + sum8(v.astype(F32))

    acc = lax.fori_loop(0, T // tile, step, jnp.zeros((8, D), F32))
    sums[8 + b : 9 + b, :] = jnp.sum(acc, axis=0, keepdims=True)


def ffn_back_input(dz, we, du, tile=128):
    @pl.loop(0, T // tile)
    def _(i):
        r = rows_at(i, tile)
        u = du[r, :]
        for b in range(4):
            u = u + nt(dz[b, r, :], we[b])
        du[r, :] = u


def context_back(dab, wo, dc, tile=256):
    @pl.loop(0, T // tile)
    def _(i):
        r = rows_at(i, tile)
        dc[r, :] = nt(dab[r, :], wo[...]).astype(BF)


def attend_backward_pair(p, joint, bias, logsum, dc, dj):
    lanes = pl.ds(pl.multiple_of(p * 128, 128), 128)
    masks = head_masks()
    q2 = joint[0, :, lanes]
    k2 = joint[1, :, lanes]
    v2 = joint[2, :, lanes]
    d2 = dc[:, lanes]
    kt = k2.T
    ls = logsum[p]
    dk = jnp.zeros((T, 128), F32)
    dv = jnp.zeros((T, 128), F32)
    dqt = []
    for h in range(2):
        qm = q2 * (masks[h] * 0.125).astype(BF)
        dm = d2 * masks[h].astype(BF)
        prob = jnp.exp(nt(k2, qm) + bias[...] - ls[h : h + 1, :])
        dp = nt(v2, dm)
        delta = jnp.sum(prob * dp, axis=0, keepdims=True)
        ds = (prob * (dp - delta)).astype(BF)
        dv = dv + nn(prob.astype(BF), dm)
        dk = dk + nn(ds, qm)
        dqt.append(nn(kt[64 * h : 64 * h + 64, :], ds))
    dj[0, :, lanes] = (jnp.concatenate(dqt, axis=0) * 0.125).T.astype(BF)
    dj[1, :, lanes] = dk.astype(BF)
    dj[2, :, lanes] = dv.astype(BF)


def input_back(dj, wa, du, dx, sums, tile=128):
    def step(i, carry):
        r = rows_at(i, tile)
        u = du[r, :]
        for b in range(3):
            u = u + nt(dj[b, r, :], wa[b])
        dx[r, :] = u.astype(dx.dtype)
        return (carry[0] + sum8(dj[0, r, :].astype(F32)), carry[1] + sum8(dj[2, r, :].astype(F32)))

    zero = jnp.zeros((8, D), F32)
    out = lax.fori_loop(0, T // tile, step, (zero, zero))
    sums[2:3, :] = jnp.sum(out[0], axis=0, keepdims=True)
    sums[3:4, :] = jnp.sum(out[1], axis=0, keepdims=True)


MESH = pl.DeviceIdType.MESH
PAIRS = 6
PIECE = 96
GROUPS = 6


def place():
    q = lax.axis_index("dp")
    f = lax.axis_index("fsdp")
    z = f // 2
    c = f % 2
    x_side = (q + 1 - 2 * (q % 2), f)
    y_side = ((q + 2) % 4, f)
    sibling = (q, f + 1 - 2 * c)
    planes = [(q, (f + 2 * k) % 8) for k in range(1, 4)]
    return q, z, c, x_side, y_side, sibling, planes


def greet(peers):
    barrier = pltpu.get_barrier_semaphore()
    for peer in peers:
        pl.semaphore_signal(barrier, inc=1, device_id=peer, device_id_type=MESH)
    pl.semaphore_wait(barrier, len(peers))


def hidden_piece(kind, b, zz, c, first, count):
    if kind < 2:
        start = 192 * zz + 96 * c + first
        return b, pl.ds(pl.multiple_of(start, 16), count)
    start = 384 * c + 96 * b + first
    return zz, pl.ds(pl.multiple_of(start, 16), count)


PARTS = [(g, first, 32) for g in range(6) for first in (0, 32, 64)]


class Gather:
    def __init__(self, whole, sbuf, sems):
        self.whole, self.sbuf, self.sems = whole, sbuf, sems
        q, z, c, self.x_side, self.y_side, self.sibling, self.planes = place()
        self.q, self.z, self.c = q, z, c
        self.qx = q + 1 - 2 * (q % 2)
        self.qy = (q + 2) % 4
        self.qd = (self.qx + 2) % 4
        self.others = [(z + k) % 4 for k in range(1, 4)]

    def spot(self, k, b, zz, cols=None):
        g, first, count = PARTS[k]
        lead, rows = hidden_piece(g % 3, b, zz, self.c, first, count)
        if cols is None:
            return self.whole.at[g, lead, rows, :]
        return self.whole.at[g, lead, rows, pl.ds(384 * cols, 384)]

    def send(self, k, src, dst, slot, peer):
        pltpu.make_async_remote_copy(
            src_ref=src, dst_ref=dst, send_sem=self.sems.at[k, slot], recv_sem=self.sems.at[k, slot + 1],
            device_id=peer, device_id_type=MESH,
        ).start()

    def total(self, k, slot, rows, cols=768):
        lead = self.whole.at[0, 0, pl.ds(0, rows), pl.ds(0, cols)] if rows <= 768 else self.whole.at[0, pl.ds(0, rows // 768)]
        pltpu.make_async_copy(lead, lead, self.sems.at[k, slot]).wait()

    def z_send(self, k):
        g, first, count = PARTS[k]
        src = self.sbuf.at[g, self.q, pl.ds(first, count), :]
        for peer in self.planes:
            self.send(k, src, self.spot(k, self.q, self.z), 0, peer)
        for b in range(4):
            mine = self.sbuf.at[g, b, pl.ds(first, count), :]
            self.send(k, mine, self.spot(k, b, self.z), 10, self.sibling)
            pltpu.make_async_copy(mine, self.spot(k, b, self.z), self.sems.at[k, 12]).start()

    def xy_send(self, k):
        count = PARTS[k][2]
        self.total(k, 1, 3 * count)
        for zz in self.others:
            spot = self.spot(k, self.q, zz)
            self.send(k, spot, spot, 2, self.x_side)
            self.send(k, spot, spot, 4, self.y_side)
        for zz in self.others:
            spot = self.spot(k, self.q, zz)
            self.send(k, spot, spot, 10, self.sibling)

    def diagonal_send(self, k):
        count = PARTS[k][2]
        self.total(k, 3, 3 * count)
        self.total(k, 5, 3 * count)
        for zz in self.others:
            spot = self.spot(k, self.qy, zz, 0)
            self.send(k, spot, spot, 6, self.x_side)
            spot = self.spot(k, self.qx, zz, 1)
            self.send(k, spot, spot, 8, self.y_side)
        for zz in self.others:
            for b in (self.qx, self.qy):
                spot = self.spot(k, b, zz)
                self.send(k, spot, spot, 10, self.sibling)

    def last_send(self, k):
        count = PARTS[k][2]
        self.total(k, 7, 3 * count, 384)
        self.total(k, 9, 3 * count, 384)
        for zz in self.others:
            spot = self.spot(k, self.qd, zz)
            self.send(k, spot, spot, 10, self.sibling)

    def finish(self, k):
        count = PARTS[k][2]
        self.total(k, 11, 16 * count)
        self.total(k, 12, 4 * count)

    def drain(self, k):
        count = PARTS[k][2]
        self.total(k, 0, 3 * count)
        self.total(k, 2, 3 * count)
        self.total(k, 4, 3 * count)
        self.total(k, 6, 3 * count, 384)
        self.total(k, 8, 3 * count, 384)
        self.total(k, 10, 16 * count)


UNIT_TIMES = (("joint", 3.0),) + tuple((f"att{p}", 1.4) for p in range(6)) + (("out", 2.0),) + tuple(
    (f"up{b}", 1.7) for b in range(4)
) + (("down", 3.0),)


def forward_plan():
    events = []
    z_free = 5.0
    xy_free = 0.0
    ready = {}
    jobs = []
    for k, (g, first, count) in enumerate(PARTS):
        share = count / 96.0
        z_start = z_free
        z_free = z_start + 12.6 * share
        jobs.append([z_free + 1.5, k, "xy", 9.9 * share])
        events.append((z_start if k else 0.0, 0, "z", k))
    done = []
    jobs.sort()
    while jobs:
        jobs.sort(key=lambda j: (max(j[0], xy_free), 0 if j[2] == "dg" else 1, j[1]))
        at, k, kind, cost = jobs.pop(0)
        start = max(at, xy_free)
        xy_free = start + cost
        share = PARTS[k][2] / 96.0
        if kind == "xy":
            events.append((at, 1, "xy", k))
            jobs.append([xy_free + 1.5, k, "dg", 5.1 * share])
        else:
            events.append((at, 2, "dg", k))
            events.append((xy_free + 1.5, 3, "last", k))
            events.append((xy_free + 1.5 + 2.0, 4, "fin", k))
            ready[PARTS[k][0]] = xy_free + 3.5 + 2.0
    events.sort()
    order, now, pos = [], 0.0, 0
    for layer in range(2):
        for name, cost in UNIT_TIMES:
            need = {"joint": 0, "up0": 1, "down": 2}.get(name)
            start = now
            if need is not None:
                start = max(now, ready[3 * layer + need])
            while pos < len(events) and events[pos][0] <= start + 0.3:
                order.append(events[pos][2:])
                pos += 1
            order.append(("run", layer, name))
            now = start + cost
    assert pos == len(events)
    return order


def forward_kernel(
    tokens, seg, vecs, joint_w, output_w, expand_w, shrink_w,
    whole, vec_out, x_saved, j_saved, c_saved, l_saved, n1_saved, r1_saved, g_saved, gp_saved, n2_saved, r2_saved, final, squares,
    stage, sbuf, wv, bias, x1, h, hb, xb, joint, ctx, logsum, n1, r1, g, gp, n2, r2, vg, vec,
    sems, stage_sems, wv_sems, vec_sems, out_sems,
):
    masters = (joint_w, output_w, expand_w, shrink_w)
    gather = Gather(whole, sbuf, sems)
    q, z, c = gather.q, gather.z, gather.c

    def stage_copies(grp):
        layer, kind = divmod(grp, 3)
        slot = grp % 2
        out = []
        for b in range(4):
            if kind == 0:
                src = output_w.at[layer] if b == 3 else joint_w.at[layer, :, pl.ds(768 * b, 768)]
            elif kind == 1:
                src = expand_w.at[layer, :, pl.ds(768 * b, 768)]
            else:
                src = shrink_w.at[layer, pl.ds(96 * b, 96), :]
            out.append(pltpu.make_async_copy(src, stage.at[slot, b], stage_sems.at[slot, b]))
        return out

    def take(grp):
        layer, kind = divmod(grp, 3)
        slot = grp % 2
        for cp in stage_copies(grp):
            cp.wait()
        sums = []
        for b in range(4):
            value = stage[slot, b]
            sbuf[grp, b] = value.astype(BF)
            sums.append(jnp.sum(value * value, axis=0, keepdims=True))
        if kind == 0:
            squares[4 * layer : 4 * layer + 1, :] = sums[0] + sums[1] + sums[2]
            squares[4 * layer + 1 : 4 * layer + 2, :] = sums[3]
        else:
            row = 4 * layer + 1 + kind
            squares[row : row + 1, :] = sums[0] + sums[1] + sums[2] + sums[3]
        if grp + 2 < GROUPS:
            for cp in stage_copies(grp + 2):
                cp.start()

    for grp in range(2):
        for cp in stage_copies(grp):
            cp.start()
    take(0)
    greet([gather.x_side, gather.y_side, gather.sibling] + gather.planes)
    gather.z_send(0)

    vg[z, c] = vecs[...]

    def vec_copy(zz, peer, slot):
        return pltpu.make_async_remote_copy(
            src_ref=vg.at[zz, c], dst_ref=vg.at[zz, c], send_sem=vec_sems.at[2 * slot], recv_sem=vec_sems.at[2 * slot + 1],
            device_id=peer, device_id_type=MESH,
        )

    def vec_total(slot, count):
        ref = vg.at[0, pl.ds(0, 1)] if count == 1 else (vg.at[0, pl.ds(0, 2)] if count == 2 else vg.at[pl.ds(0, 2)])
        pltpu.make_async_copy(ref, ref, vec_sems.at[slot]).wait()

    for k, peer in enumerate(gather.planes):
        vec_copy(z, peer, k).start()
    take(1)
    take(2)
    take(3)
    for k in range(3):
        vec_copy((z + 3 - k) % 4, gather.planes[0], k).wait_recv()
    for zz in range(4):
        vec_copy(zz, gather.sibling, 3 + zz).start()
    gather.z_send(1)
    take(4)
    take(5)
    build_mask(seg, bias)
    for zz in range(4):
        vec_copy(zz, gather.sibling, 3 + zz).wait_recv()
    lane = lax.broadcasted_iota(jnp.int32, (128, 768), 1)
    spot = lax.broadcasted_iota(jnp.int32, (128, 768), 0)
    for layer in range(2):
        acc = jnp.zeros((16, 768), F32)
        for m in range(8):
            pick = jnp.where((lane == spot + 96 * m) & (spot < 96), 1.0, 0.0).astype(BF)
            first = vg[m // 2, m % 2, 16 * layer : 16 * layer + 8, :]
            rest = [vg[b, m // 4, 16 * layer + 8 + m % 4 : 16 * layer + 9 + m % 4, :] for b in range(4)]
            left = jnp.concatenate([first] + rest + [jnp.zeros((4, 128), F32)], axis=0)
            acc = acc + nn(left.astype(BF), pick)
        vec[layer] = acc

    state = {"sent": 2}
    started = []

    def save(src, dst):
        n = len(started)
        cp = pltpu.make_async_copy(src, dst, out_sems.at[n])
        cp.start()
        started.append(cp)

    def load(grp):
        return pltpu.make_async_copy(whole.at[grp], wv.at[grp % 3], wv_sems.at[grp % 3])

    def event(kind, k):
        if kind == "z":
            return
        if kind == "xy":
            gather.xy_send(k)
            if k + 2 < len(PARTS):
                gather.z_send(k + 2)
        elif kind == "dg":
            gather.diagonal_send(k)
        elif kind == "last":
            gather.last_send(k)
        elif kind == "fin":
            gather.finish(k)
            grp, first, count = PARTS[k]
            if first + count == 96:
                load(grp).start()

    order = forward_plan()
    pos = 0
    while pos < len(order):
        item = order[pos]
        if item[0] != "run":
            event(*item)
            pos += 1
            continue
        _, layer, name = item
        vl = vec.at[layer]
        x_in = tokens if layer == 0 else x1
        xb_in = tokens if layer == 0 else xb
        if name == "joint":
            load(3 * layer).wait()
            joint_forward(xb_in, wv.at[0], vl, joint.at[layer])
            save(joint.at[layer], j_saved.at[layer])
        elif name.startswith("att"):
            hooks, first = {}, int(name[3:])
            p, look = first, pos
            while True:
                it = order[look]
                if it[0] == "run":
                    if not it[2].startswith("att"):
                        break
                    p = int(it[2][3:]) + 1
                else:
                    hooks.setdefault(p, []).append(it)
                look += 1
            tail = hooks.pop(6, [])

            @pl.loop(0, PAIRS)
            def _(p):
                for at, items in hooks.items():
                    @pl.when(p == at)
                    def _():
                        for it in items:
                            event(*it)
                attend_forward_pair(p, joint.at[layer], bias, ctx.at[layer], logsum.at[layer])

            for it in tail:
                event(*it)
            save(ctx.at[layer], c_saved.at[layer])
            save(logsum.at[layer], l_saved.at[layer])
            pos = look
            continue
        elif name == "out":
            out_forward(ctx.at[layer], x_in, wv.at[0, 3], vl, n1.at[layer], r1.at[layer], h, hb)
            save(n1.at[layer], n1_saved.at[layer])
            save(r1.at[layer], r1_saved.at[layer])
        elif name.startswith("up"):
            b = int(name[2:])
            if b == 0:
                load(3 * layer + 1).wait()
            ffn_up(hb, wv.at[1], vl, g.at[layer], gp.at[layer], b)
            if b == 3:
                save(g.at[layer], g_saved.at[layer])
                save(gp.at[layer], gp_saved.at[layer])
        else:
            load(3 * layer + 2).wait()
            ffn_down(g.at[layer], wv.at[2], vl, h, n2.at[layer], r2.at[layer], x1 if layer == 0 else None, xb if layer == 0 else hb)
            save(n2.at[layer], n2_saved.at[layer])
            save(r2.at[layer], r2_saved.at[layer])
            if layer == 0:
                save(xb, x_saved)
            else:
                save(hb, final)
        pos += 1
    save(vec, vec_out)
    for k in range(len(PARTS)):
        gather.drain(k)
    for k in range(3):
        vec_copy(z, gather.planes[k], k).wait_send()
    for zz in range(4):
        vec_copy(zz, gather.sibling, 3 + zz).wait_send()
    for cp in started:
        cp.wait()


def forward_call(tokens, seg, vecs, joint_w, output_w, expand_w, shrink_w):
    sd = jax.ShapeDtypeStruct
    any_spec = pl.BlockSpec(memory_space=pl.ANY)
    vm = pl.BlockSpec(memory_space=pltpu.VMEM)
    V = pltpu.VMEM
    saved = [
        sd((6, 4, 768, 768), BF),
        sd((2, 16, 768), F32),
        sd((T, D), BF),
        sd((2, 3, T, D), BF),
        sd((2, T, D), BF),
        sd((2, 6, 2, T), F32),
        sd((2, T, D), BF),
        sd((2, T, 128), F32),
        sd((2, 4, T, D), BF),
        sd((2, 4, T, D), BF),
        sd((2, T, D), BF),
        sd((2, T, 128), F32),
        sd((T, D), BF),
        sd((8, 768), F32),
    ]
    scratch = [
        V((2, 4, 96, 768), F32),
        V((6, 4, 96, 768), BF),
        V((3, 4, 768, 768), BF),
        V((T, T), F32),
        V((T, D), F32),
        V((T, D), F32),
        V((T, D), BF),
        V((T, D), BF),
        V((2, 3, T, D), BF),
        V((2, T, D), BF),
        V((2, 6, 2, T), F32),
        V((2, T, D), BF),
        V((2, T, 128), F32),
        V((2, 4, T, D), BF),
        V((2, 4, T, D), BF),
        V((2, T, D), BF),
        V((2, T, 128), F32),
        V((4, 2, 32, 128), F32),
        V((2, 16, 768), F32),
        pltpu.SemaphoreType.DMA((len(PARTS), 13)),
        pltpu.SemaphoreType.DMA((2, 4)),
        pltpu.SemaphoreType.DMA((3,)),
        pltpu.SemaphoreType.DMA((14,)),
        pltpu.SemaphoreType.DMA((24,)),
    ]
    return pl.pallas_call(
        forward_kernel,
        out_shape=saved,
        in_specs=[vm, vm, vm] + [any_spec] * 4,
        out_specs=[any_spec] * 13 + [vm],
        scratch_shapes=scratch,
        compiler_params=pltpu.CompilerParams(
            collective_id=0, has_side_effects=True, vmem_limit_bytes=62 << 20
        ),
        name="forward",
    )(tokens, seg, vecs, joint_w, output_w, expand_w, shrink_w)


def pack_vectors(norm_gains, biases, hidden_bias):
    parts = []
    for layer in range(2):
        parts.append(norm_gains[layer])
        parts.append(biases[layer])
        parts.append(hidden_bias[layer].reshape(4, 96))
        parts.append(jnp.zeros((4, 96), F32))
    rows = jnp.concatenate(parts, axis=0)
    return jnp.pad(rows, ((0, 0), (0, 32)))


BACK_UNITS = (
    (("ln2", 3.5),)
    + tuple((f"s{i}", 2.0) for i in range(4))
    + tuple((f"dz{i}", 2.0) for i in range(4))
    + (("ht", 1.2), ("e0", 3.5), ("e1", 3.5), ("dh", 4.5), ("ln1", 3.5), ("o", 3.5))
    + tuple((f"att{p}", 2.6) for p in range(6))
    + (("xt", 0.8), ("q0", 2.8), ("q1", 2.8), ("dx", 3.5))
)
GROUP_OF = {"s": 0, "e": 1, "o": 2, "q": 2}
PARTS_OF = {"s0": (0,), "s1": (1,), "s2": (2,), "s3": (3,), "e0": (0, 1), "e1": (2, 3), "q0": (0, 1), "q1": (2, 3)}


def backward_plan():
    now, xy_free, z_free, core_free = 0.0, 0.0, 0.0, 0.0
    pending, order, summed = [], [], set()

    def emit(entry):
        nonlocal now, xy_free, z_free
        ready, name, t, zz = entry
        now = max(now, ready) + 0.4
        order.append((name, t, zz))
        if name == "xy1":
            xy_free = max(xy_free, now) + 3.2
            pending.append((xy_free + 1.5, "xy2", t, zz))
        elif name == "xy2":
            xy_free = max(xy_free, now) + 1.6
            pending.append((xy_free + 1.5, "z", t, zz))
        elif name == "z":
            z_free = max(z_free, now) + 3.2
            if sum(1 for o in order if o[0] == "z" and o[1] == t) == 4:
                pending.append((z_free + 1.5, "sum", t, 0))
        elif name == "sum":
            summed.add(t)
            xy_free = max(xy_free, now) + 3.2
            pending.append((xy_free + 1.5, "ag", t, 0))
        elif name == "ag":
            xy_free = max(xy_free, now) + 1.6
            pending.append((xy_free + 1.5, "fin", t, 0))

    def step(limit):
        pending.sort()
        if pending and pending[0][0] <= limit:
            emit(pending.pop(0))
            return True
        return False

    for layer in (1, 0):
        for name, cost in BACK_UNITS:
            while step(now):
                pass
            if name[0] in GROUP_OF and name != "ln2":
                t = 3 * (1 - layer) + GROUP_OF[name[0]]
                while t >= 3 and t - 3 not in summed:
                    step(1e9)
            order.append(("run", layer, name))
            now += cost
            for zz in PARTS_OF.get(name, ()):
                core_free = max(core_free, now) + 1.0
                pending.append((core_free + 1.5, "xy1", 3 * (1 - layer) + GROUP_OF[name[0]], zz))
    while step(1e9):
        pass
    return order


class Reduce:
    def __init__(self, gb, rc, rx1, ry1, rx2, ry2, rz, fin, sems, group_sems, credits):
        self.gb, self.rc, self.rx1, self.ry1, self.rx2, self.ry2, self.rz, self.fin = gb, rc, rx1, ry1, rx2, ry2, rz, fin
        self.sems, self.group_sems, self.credits = sems, group_sems, credits
        q, z, c, self.x_side, self.y_side, self.sibling, self.planes = place()
        self.q, self.z, self.c = q, z, c
        self.ax, self.ay = q % 2, q // 2

    def send(self, src, dst, sem, peer):
        pltpu.make_async_remote_copy(
            src_ref=src, dst_ref=dst, send_sem=sem[0], recv_sem=sem[1], device_id=peer, device_id_type=MESH
        ).start()

    def pair(self, t, zz, slot):
        return self.sems.at[4 * t + zz, 2 * slot], self.sems.at[4 * t + zz, 2 * slot + 1]

    def group_pair(self, t, slot):
        return self.group_sems.at[t, 2 * slot], self.group_sems.at[t, 2 * slot + 1]

    def wait(self, ref, sem):
        pltpu.make_async_copy(ref, ref, sem).wait()

    def credit_wait(self, t, phase, zz):
        if t > 0:
            pl.semaphore_wait(self.credits.at[phase, zz], 1)

    def credit_give(self, t, phase, zz, peer):
        if t < 5:
            pl.semaphore_signal(self.credits.at[phase, zz], inc=1, device_id=peer, device_id_type=MESH)

    def core_send(self, t, zz):
        self.credit_wait(t, 0, zz)
        self.send(self.gb.at[t % 3, :, :, zz, 1 - self.c], self.rc.at[zz], self.pair(t, zz, 0), self.sibling)

    def add(self, ref, other):
        ref[...] = (ref[...].astype(F32) + other[...].astype(F32)).astype(BF)

    def xy1(self, t, zz):
        gb, c = self.gb.at[t % 3], self.c
        self.wait(self.rc.at[0], self.pair(t, zz, 0)[1])
        for by in range(2):
            for bx in range(2):
                self.add(gb.at[by, bx, zz, c], self.rc.at[zz, by, bx])
        self.credit_give(t, 0, zz, self.sibling)
        self.credit_wait(t, 1, zz)
        self.send(gb.at[:, 1 - self.ax, zz, c, pl.ds(0, 48)], self.rx1.at[zz], self.pair(t, zz, 1), self.x_side)
        self.credit_wait(t, 2, zz)
        self.send(gb.at[1 - self.ay, :, zz, c, pl.ds(48, 48)], self.ry1.at[zz], self.pair(t, zz, 2), self.y_side)

    def xy2(self, t, zz):
        gb, c = self.gb.at[t % 3], self.c
        self.wait(self.rx1.at[0], self.pair(t, zz, 1)[1])
        self.wait(self.ry1.at[0], self.pair(t, zz, 2)[1])
        for k in range(2):
            self.add(gb.at[k, self.ax, zz, c, pl.ds(0, 48)], self.rx1.at[zz, k])
            self.add(gb.at[self.ay, k, zz, c, pl.ds(48, 48)], self.ry1.at[zz, k])
        self.credit_give(t, 1, zz, self.x_side)
        self.credit_give(t, 2, zz, self.y_side)
        self.credit_wait(t, 3, zz)
        self.send(gb.at[self.ay, 1 - self.ax, zz, c, pl.ds(48, 48)], self.rx2.at[zz], self.pair(t, zz, 3), self.x_side)
        self.credit_wait(t, 4, zz)
        self.send(gb.at[1 - self.ay, self.ax, zz, c, pl.ds(0, 48)], self.ry2.at[zz], self.pair(t, zz, 4), self.y_side)

    def z_send(self, t, zz):
        gb, c = self.gb.at[t % 3], self.c
        self.wait(self.rx2.at[0], self.pair(t, zz, 3)[1])
        self.wait(self.ry2.at[0], self.pair(t, zz, 4)[1])
        self.add(gb.at[self.ay, self.ax, zz, c, pl.ds(48, 48)], self.rx2.at[zz])
        self.add(gb.at[self.ay, self.ax, zz, c, pl.ds(0, 48)], self.ry2.at[zz])
        self.credit_give(t, 3, zz, self.x_side)
        self.credit_give(t, 4, zz, self.y_side)

        @pl.when(self.z != zz)
        def _():
            self.send(
                gb.at[self.ay, self.ax, zz, c], self.rz.at[t, (self.z + 3 - zz) % 4], self.group_pair(t, 0),
                (self.q, 2 * zz + c),
            )

    def total(self, t):
        gb, c = self.gb.at[t % 3], self.c
        self.wait(self.rz.at[0], self.group_pair(t, 0)[1])
        own = gb[self.ay, self.ax, self.z, c].astype(F32)
        for k in range(3):
            own = own + self.rz[t, k].astype(F32)
        self.fin[t, self.q] = own.astype(BF)
        spot = self.fin.at[t, self.q]
        self.send(spot, spot, self.group_pair(t, 1), self.x_side)
        self.send(spot, spot, self.group_pair(t, 2), self.y_side)

    def share(self, t):
        self.wait(self.fin.at[0, 0], self.group_pair(t, 1)[1])
        self.wait(self.fin.at[0, 0], self.group_pair(t, 2)[1])
        qx = self.q + 1 - 2 * self.ax
        qy = (self.q + 2) % 4
        spot = self.fin.at[t, qy, pl.ds(0, 48)]
        self.send(spot, spot, self.group_pair(t, 3), self.x_side)
        spot = self.fin.at[t, qx, pl.ds(48, 48)]
        self.send(spot, spot, self.group_pair(t, 4), self.y_side)

    def finish(self, t):
        self.wait(self.fin.at[0, 0, pl.ds(0, 48)], self.group_pair(t, 3)[1])
        self.wait(self.fin.at[0, 0, pl.ds(0, 48)], self.group_pair(t, 4)[1])

    def drain(self, t):
        for zz in range(4):
            self.wait(self.rc.at[0], self.pair(t, zz, 0)[0])
            self.wait(self.rx1.at[0], self.pair(t, zz, 1)[0])
            self.wait(self.ry1.at[0], self.pair(t, zz, 2)[0])
            self.wait(self.rx2.at[0], self.pair(t, zz, 3)[0])
            self.wait(self.ry2.at[0], self.pair(t, zz, 4)[0])
        self.wait(self.rz.at[0], self.group_pair(t, 0)[0])

    def drain_share(self, t):
        self.wait(self.fin.at[0, 0], self.group_pair(t, 1)[0])
        self.wait(self.fin.at[0, 0], self.group_pair(t, 2)[0])
        self.wait(self.fin.at[0, 0, pl.ds(0, 48)], self.group_pair(t, 3)[0])
        self.wait(self.fin.at[0, 0, pl.ds(0, 48)], self.group_pair(t, 4)[0])


def backward_kernel(
    cot, seg, vec, tokens, x_saved, whole, j_saved, c_saved, l_saved, n1_saved, r1_saved, g_saved, gp_saved, n2_saved, r2_saved,
    fin, total, grad_in,
    gb, rc, rx1, ry1, rx2, ry2, rz, wv, g, dz, dj, ctx, n1, n2, r1, r2, logsum, xb, dob, at, hb, bias, du, sums, vr, va,
    sems, group_sems, credits, load_sems, vec_sems,
):
    red = Reduce(gb, rc, rx1, ry1, rx2, ry2, rz, fin, sems, group_sems, credits)
    q, z, c = red.q, red.z, red.c
    sources = {
        "n2": (n2_saved, n2), "r2": (r2_saved, r2), "g": (g_saved, g), "dz": (gp_saved, dz), "n1": (n1_saved, n1),
        "r1": (r1_saved, r1), "ctx": (c_saved, ctx), "dj": (j_saved, dj), "logsum": (l_saved, logsum), "xb": (None, xb),
    }
    names = list(sources)

    def load(name, layer):
        src, dst = sources[name]
        if name == "xb":
            src = x_saved if layer == 1 else tokens
        else:
            src = src.at[layer]
        return pltpu.make_async_copy(src, dst, load_sems.at[names.index(name)])

    def weights(t):
        layer, kind = 1 - t // 3, (2, 1, 0)[t % 3]
        return pltpu.make_async_copy(whole.at[3 * layer + kind], wv.at[t % 2], load_sems.at[10 + t % 2])

    def need(layer, *which):
        for name in which:
            load(name, layer).wait()

    def release(layer, *which):
        if layer == 1:
            for name in which:
                load(name, 0).start()

    def next_weights(t):
        if t + 2 < 6:
            weights(t + 2).start()

    for name in ("n2", "r2", "g"):
        load(name, 1).start()
    weights(0).start()
    load("dz", 1).start()
    weights(1).start()
    for name in ("n1", "r1", "ctx", "dj", "logsum", "xb"):
        load(name, 1).start()
    build_mask(seg, bias)
    sums[...] = jnp.zeros_like(sums)
    greet([red.x_side, red.y_side, red.sibling] + red.planes)

    def blocks_pair(slot, b, pair, left):
        out = nn(at[pl.ds(384 * pair, 384), :], left).astype(BF)
        gb[slot, b // 2, b % 2, pl.ds(2 * pair, 2)] = out.reshape(2, 2, 96, 768)

    def unit(layer, name):
        base = 3 * (1 - layer)
        vl, sl = vec.at[layer], sums.at[layer]
        if name == "ln2":
            need(layer, "n2", "r2")
            norm_backward(cot if layer == 1 else du, n2, r2, vl[1:2, :], du, dob, sl, (1, 7, 6))
            release(layer, "n2", "r2")
        elif name[0] == "s":
            zz = int(name[1])
            if zz == 0:
                need(layer, "g")
                if base >= 3:
                    red.drain(base - 3)
            transpose_into(g.at[zz], at)
            for cc in range(2):
                out = nn(at[pl.ds(384 * cc, 384), :], dob[...]).astype(BF)
                gb[base % 3, :, :, zz, cc] = out.reshape(2, 2, 96, 768)
            red.core_send(base, zz)
            if zz == 3:
                release(layer, "g")
        elif name.startswith("dz"):
            b = int(name[2])
            if b == 0:
                need(layer, "dz")
                weights(base).wait()
            ffn_back_block(dob, wv.at[base % 2], dz, dz, sl, b)
            if b == 3:
                next_weights(base)
        elif name == "ht":
            need(layer, "n1", "r1")
            hb[...] = (n1[...].astype(F32) * vl[0:1, :] + vl[5:6, :]).astype(BF)
            transpose_into(hb, at)
        elif name[0] == "e":
            pair = int(name[1])
            if pair == 0 and base >= 3:
                red.drain(base - 2)
            for b in range(4):
                blocks_pair((base + 1) % 3, b, pair, dz[b])
            for zz in (2 * pair, 2 * pair + 1):
                red.core_send(base + 1, zz)
        elif name == "dh":
            weights(base + 1).wait()
            ffn_back_input(dz, wv.at[(base + 1) % 2], du)
            release(layer, "dz")
            next_weights(base + 1)
        elif name == "ln1":
            norm_backward(du, n1, r1, vl[0:1, :], du, dob, sl, (0, 5, 4))
            release(layer, "n1", "r1")
        elif name == "o":
            need(layer, "ctx")
            weights(base + 2).wait()
            if base >= 3:
                red.drain(base - 1)
            transpose_into(ctx, at)
            for pair in range(2):
                blocks_pair((base + 2) % 3, 3, pair, dob[...])
            context_back(dob, wv.at[(base + 2) % 2, 3], hb)
            release(layer, "ctx")
        elif name == "xt":
            need(layer, "xb")
            transpose_into(xb, at)
            release(layer, "xb", "logsum")
        elif name[0] == "q":
            pair = int(name[1])
            for b in range(3):
                blocks_pair((base + 2) % 3, b, pair, dj[b])
            for zz in (2 * pair, 2 * pair + 1):
                red.core_send(base + 2, zz)
        elif name == "dx":
            input_back(dj, wv.at[(base + 2) % 2], du, du, sl)
            release(layer, "dj")
            next_weights(base + 2)

    def event(name, t, zz):
        if name == "xy1":
            red.xy1(t, zz)
        elif name == "xy2":
            red.xy2(t, zz)
        elif name == "z":
            red.z_send(t, zz)
        elif name == "sum":
            red.total(t)
        elif name == "ag":
            red.share(t)
        else:
            red.finish(t)

    def vec_copy(src, dst, k, peer):
        return pltpu.make_async_remote_copy(
            src_ref=src, dst_ref=dst, send_sem=vec_sems.at[2 * k], recv_sem=vec_sems.at[2 * k + 1],
            device_id=peer, device_id_type=MESH,
        )

    def vec_hop(k, src, peer, out):
        cp = vec_copy(src, vr.at[k], k, peer)
        cp.start()
        cp.wait()
        out[...] = src[...] + vr[k]

    order = backward_plan()
    pos = 0
    done_units = False
    while pos < len(order):
        item = order[pos]
        if item[0] != "run":
            event(*item)
            pos += 1
            continue
        _, layer, name = item
        if not name.startswith("att"):
            unit(layer, name)
            pos += 1
            continue
        hooks, look, p = {}, pos, 0
        while True:
            it = order[look]
            if it[0] == "run":
                if not it[2].startswith("att"):
                    break
                p = int(it[2][3:]) + 1
            else:
                hooks.setdefault(p, []).append(it)
            look += 1
        tail = hooks.pop(6, [])
        need(layer, "dj", "logsum")

        @pl.loop(0, PAIRS)
        def _(p):
            for at_pair, items in hooks.items():
                @pl.when(p == at_pair)
                def _():
                    for it in items:
                        event(*it)
            attend_backward_pair(p, dj, bias, logsum, hb, dj)

        for it in tail:
            event(*it)
        pos = look

    grad_in[...] = du[...].astype(BF)
    vec_hop(0, sums, red.sibling, va.at[0])
    vec_hop(1, va.at[0], red.x_side, va.at[1])
    vec_hop(2, va.at[1], red.y_side, va.at[2])
    for k, peer in enumerate(red.planes):
        vec_copy(va.at[2], vr.at[3 + k], 3 + k, peer).start()
    for k, peer in enumerate(red.planes):
        vec_copy(va.at[2], vr.at[3 + k], 3 + k, peer).wait()
    acc = jnp.zeros((2, 16, 768), F32)
    for plane in range(4):
        part = jnp.where(z == plane, va[2], 0.0)
        for k in range(3):
            part = jnp.where((z + 3 - k) % 4 == plane, vr[3 + k], part)
        acc = acc + part
    total[...] = acc
    for t in range(3, 6):
        red.drain(t)
    for t in range(6):
        red.drain_share(t)


def backward_call(cot, seg, vec, tokens, x_saved, whole, j_s, c_s, l_s, n1_s, r1_s, g_s, gp_s, n2_s, r2_s):
    sd = jax.ShapeDtypeStruct
    any_spec = pl.BlockSpec(memory_space=pl.ANY)
    vm = pl.BlockSpec(memory_space=pltpu.VMEM)
    V = pltpu.VMEM
    dma = pltpu.SemaphoreType.DMA
    return pl.pallas_call(
        backward_kernel,
        out_shape=[sd((6, 4, 96, 768), BF), sd((2, 16, 768), F32), sd((T, D), BF)],
        in_specs=[vm, vm, vm] + [any_spec] * 12,
        out_specs=[vm] * 3,
        scratch_shapes=[
            V((3, 2, 2, 4, 2, 96, 768), BF),
            V((4, 2, 2, 96, 768), BF),
            V((4, 2, 48, 768), BF),
            V((4, 2, 48, 768), BF),
            V((4, 48, 768), BF),
            V((4, 48, 768), BF),
            V((6, 3, 96, 768), BF),
            V((2, 4, 768, 768), BF),
            V((4, T, D), BF),
            V((4, T, D), BF),
            V((3, T, D), BF),
            V((T, D), BF),
            V((T, D), BF),
            V((T, D), BF),
            V((T, 128), F32),
            V((T, 128), F32),
            V((6, 2, T), F32),
            V((T, D), BF),
            V((T, D), BF),
            V((D, T), BF),
            V((T, D), BF),
            V((T, T), F32),
            V((T, D), F32),
            V((2, 16, 768), F32),
            V((6, 2, 16, 768), F32),
            V((3, 2, 16, 768), F32),
            dma((24, 10)),
            dma((6, 10)),
            pltpu.SemaphoreType.REGULAR((5, 4)),
            dma((12,)),
            dma((12,)),
        ],
        compiler_params=pltpu.CompilerParams(
            collective_id=1, has_side_effects=True, vmem_limit_bytes=63 << 20
        ),
        name="backward",
    )(cot, seg, vec, tokens, x_saved, whole, j_s, c_s, l_s, n1_s, r1_s, g_s, gp_s, n2_s, r2_s)


def local_kernels(
    tokens,
    segments,
    cotangent,
    joint_weight,
    output_weight,
    expand_weight,
    shrink_weight,
    norm_gains,
    biases,
    hidden_bias,
    joint_rows,
    joint_columns,
    output_rows,
    output_columns,
    expand_rows,
    expand_columns,
    shrink_rows,
    shrink_columns,
    gain_moments,
    bias_moments,
    hidden_moments,
):
    row_count, slot_count, features = tokens.shape
    vecs = pack_vectors(norm_gains, biases, hidden_bias)
    (whole, vec, x_saved, j_s, c_s, l_s, n1_s, r1_s, g_s, gp_s, n2_s, r2_s, final, squares) = forward_call(
        tokens[0], segments, vecs, joint_weight, output_weight, expand_weight, shrink_weight
    )
    activations = final[None]
    blocks, sums, grad = backward_call(
        cotangent[0], segments, vec, tokens[0], x_saved, whole, j_s, c_s, l_s, n1_s, r1_s, g_s, gp_s, n2_s, r2_s
    )
    f = lax.axis_index("fsdp")
    mine = lax.dynamic_slice_in_dim(sums[:, :8], f * 96, 96, axis=2)
    hidden_mine = lax.dynamic_slice_in_dim(sums[:, 8:12].reshape(2, 3072), f * 384, 384, axis=1)
    collected = []
    for number in range(2):
        gs, ge, ga = blocks[3 * (1 - number)], blocks[3 * (1 - number) + 1], blocks[3 * (1 - number) + 2]
        collected.append((
            ga[:3].transpose(1, 0, 2).reshape(96, 2304).astype(jnp.float32),
            ga[3].astype(jnp.float32),
            ge.transpose(1, 0, 2).reshape(96, 3072).astype(jnp.float32),
            gs.reshape(384, 768).astype(jnp.float32),
            mine[number, :2],
            mine[number, 2:8],
            hidden_mine[number],
        ))
    input_gradient = grad[None]
    fsdp_count = lax.axis_size("fsdp")
    token_total = row_count * slot_count * lax.axis_size("dp") * fsdp_count
    root_scale = 1.0 / math.sqrt(token_total)
    stacked_grads = [
        jnp.stack([entry[index] for entry in collected]) * root_scale for index in range(7)
    ]
    matrices = (
        (stacked_grads[0], joint_weight, joint_rows, joint_columns),
        (stacked_grads[1], output_weight, output_rows, output_columns),
        (stacked_grads[2], expand_weight, expand_rows, expand_columns),
        (stacked_grads[3], shrink_weight, shrink_rows, shrink_columns),
    )
    partial_list = [factored_partials(item[0], item[1], item[2]) for item in matrices]
    vectors = (
        (stacked_grads[4], norm_gains, gain_moments),
        (stacked_grads[5], biases, bias_moments),
        (stacked_grads[6][:, None, :], hidden_bias[:, None, :], hidden_moments[:, None, :]),
    )
    vector_list = [vector_partials(item[0], item[2]) for item in vectors]
    vector_squares = jnp.concatenate(
        [jnp.sum(item[1] * item[1], axis=2) for item in vectors], axis=1
    )
    statistics = lax.psum(
        (
            partial_list[0][1],
            partial_list[1][1],
            partial_list[2][1],
            partial_list[3][1],
            jnp.stack([item[2] for item in partial_list], axis=1),
            jnp.stack([item[3] for item in partial_list], axis=1),
            vector_squares,
        ),
        "fsdp",
    )
    updates = []
    columns_list = []
    for index in range(4):
        gradient = matrices[index][0]
        total_rows = gradient.shape[1] * fsdp_count
        rows_next = partial_list[index][0]
        columns_next = DECAY_RATE * matrices[index][3] + (1.0 - DECAY_RATE) * (
            statistics[index] / total_rows
        )
        row_average = statistics[4][:, index] / total_rows
        estimate = rows_next[:, :, None] * columns_next[:, None, :] / row_average[:, None, None]
        updates.append(gradient * lax.rsqrt(estimate))
        columns_list.append(columns_next)
    matrix_squares = jnp.stack([jnp.sum(item * item, axis=(1, 2)) for item in updates], axis=1)
    vector_updates = jnp.concatenate(
        [jnp.sum(item[1] * item[1], axis=2) for item in vector_list], axis=1
    )
    norms = lax.psum((matrix_squares, vector_updates), "fsdp")
    matrix_next = []
    for index in range(4):
        gradient = matrices[index][0]
        entry_count = gradient.shape[1] * fsdp_count * gradient.shape[2]
        clip_ratio = jnp.sqrt(norms[0][:, index] / entry_count) / CLIP_LIMIT
        update = updates[index] / jnp.maximum(clip_ratio, 1.0)[:, None, None]
        stride = STEP_RATE * jnp.maximum(
            FLOOR_SCALE, jnp.sqrt(statistics[5][:, index] / entry_count)
        )
        matrix_next.append(matrices[index][1] - stride[:, None, None] * update)
    vector_next = []
    offset = 0
    for index in range(3):
        gradient = vectors[index][0]
        kinds = gradient.shape[1]
        entry_count = gradient.shape[2] * fsdp_count
        clip_ratio = jnp.sqrt(norms[1][:, offset : offset + kinds] / entry_count) / CLIP_LIMIT
        update = vector_list[index][1] / jnp.maximum(clip_ratio, 1.0)[:, :, None]
        stride = STEP_RATE * jnp.maximum(
            FLOOR_SCALE, jnp.sqrt(statistics[6][:, offset : offset + kinds] / entry_count)
        )
        vector_next.append(vectors[index][1] - stride[:, :, None] * update)
        offset = offset + kinds
    return (
        activations,
        input_gradient,
        stacked_grads[0],
        stacked_grads[1],
        stacked_grads[2],
        stacked_grads[3],
        stacked_grads[4],
        stacked_grads[5],
        stacked_grads[6],
        matrix_next[0],
        matrix_next[1],
        matrix_next[2],
        matrix_next[3],
        vector_next[0],
        vector_next[1],
        vector_next[2][:, 0, :],
        matrix_next[0].astype(jnp.bfloat16),
        matrix_next[1].astype(jnp.bfloat16),
        matrix_next[2].astype(jnp.bfloat16),
        matrix_next[3].astype(jnp.bfloat16),
        partial_list[0][0],
        columns_list[0],
        partial_list[1][0],
        columns_list[1],
        partial_list[2][0],
        columns_list[2],
        partial_list[3][0],
        columns_list[3],
        vector_list[0][0],
        vector_list[1][0],
        vector_list[2][0][:, 0, :],
    )


def solution(mesh):
    placed = (
        P(("dp", "fsdp"), None, None),
        P(("dp", "fsdp"), None),
        P(("dp", "fsdp"), None, None),
        P(None, "fsdp", None),
        P(None, "fsdp", None),
        P(None, "fsdp", None),
        P(None, "fsdp", None),
        P(None, None, "fsdp"),
        P(None, None, "fsdp"),
        P(None, "fsdp"),
        P(None, "fsdp"),
        P(),
        P(None, "fsdp"),
        P(),
        P(None, "fsdp"),
        P(),
        P(None, "fsdp"),
        P(),
        P(None, None, "fsdp"),
        P(None, None, "fsdp"),
        P(None, "fsdp"),
    )
    known = dict(mesh.shape) == {"dp": 4, "fsdp": 8}
    return jax.shard_map(
        local_kernels if known else local_plain,
        mesh=mesh,
        in_specs=placed,
        out_specs=(
            P(("dp", "fsdp"), None, None),
            P(("dp", "fsdp"), None, None),
            P(None, "fsdp", None),
            P(None, "fsdp", None),
            P(None, "fsdp", None),
            P(None, "fsdp", None),
            P(None, None, "fsdp"),
            P(None, None, "fsdp"),
            P(None, "fsdp"),
            P(None, "fsdp", None),
            P(None, "fsdp", None),
            P(None, "fsdp", None),
            P(None, "fsdp", None),
            P(None, None, "fsdp"),
            P(None, None, "fsdp"),
            P(None, "fsdp"),
            P(None, "fsdp", None),
            P(None, "fsdp", None),
            P(None, "fsdp", None),
            P(None, "fsdp", None),
            P(None, "fsdp"),
            P(),
            P(None, "fsdp"),
            P(),
            P(None, "fsdp"),
            P(),
            P(None, "fsdp"),
            P(),
            P(None, None, "fsdp"),
            P(None, None, "fsdp"),
            P(None, "fsdp"),
        ),
        check_vma=False,
    )
```

```python
from functools import partial
import math

import jax
import jax.numpy as jnp
from jax import lax
from jax.sharding import PartitionSpec as P
from jax.experimental import pallas as pl
from jax.experimental.pallas import tpu as pltpu

HEADS = 12
HEAD_SIZE = 64


NORM_EPSILON = 1e-12
SCORE_SCALE = 0.125
MASK_VALUE = -1e30
FLOOR_SQUARE = 1e-30
FLOOR_SCALE = 0.001
DECAY_RATE = 0.5
CLIP_LIMIT = 0.25
STEP_RATE = 4.0


def product(left, right):
    return jnp.dot(left, right, preferred_element_type=jnp.float32)


def product_left(left, right):
    return lax.dot_general(
        left, right, (((0,), (0,)), ((), ())), preferred_element_type=jnp.float32
    )


def product_right(left, right):
    return lax.dot_general(
        left, right, (((1,), (1,)), ((), ())), preferred_element_type=jnp.float32
    )


def normalize(values):
    average = jnp.mean(values, axis=-1, keepdims=True)
    centered = values - average
    variance = jnp.mean(centered * centered, axis=-1, keepdims=True)
    inverse = lax.rsqrt(variance + NORM_EPSILON)
    return (centered * inverse, inverse)


def normalize_back(grad_scaled, scaled, inverse):
    first_mean = jnp.mean(grad_scaled, axis=-1, keepdims=True)
    second_mean = jnp.mean(grad_scaled * scaled, axis=-1, keepdims=True)
    return inverse * (grad_scaled - first_mean - scaled * second_mean)


def split_heads(joint_row):
    slot_count = joint_row.shape[0]
    shaped = joint_row.reshape(slot_count, 3, HEADS, HEAD_SIZE)
    return (shaped[:, 0], shaped[:, 1], shaped[:, 2])


def masked_scores(query_rows, key_rows, segment_row):
    scores = (
        jnp.einsum("qhe,khe->hqk", query_rows, key_rows, preferred_element_type=jnp.float32)
        * SCORE_SCALE
    )
    allowed = segment_row[:, None] == segment_row[None, :]
    return jnp.where(allowed[None], scores, MASK_VALUE)


def attend_forward(packed):
    joint_row, segment_row = packed
    query_rows, key_rows, value_rows = split_heads(joint_row)
    scores = masked_scores(query_rows, key_rows, segment_row)
    highest = jnp.max(scores, axis=-1, keepdims=True)
    raised = jnp.exp(scores - highest)
    denominator = jnp.sum(raised, axis=-1, keepdims=True)
    weights = (raised / denominator).astype(jnp.bfloat16)
    context = jnp.einsum("hqk,khe->qhe", weights, value_rows, preferred_element_type=jnp.float32)
    logsum = (highest + jnp.log(denominator))[:, :, 0]
    return (context.astype(jnp.bfloat16).reshape(joint_row.shape[0], HEADS * HEAD_SIZE), logsum)


def attend_backward(packed):
    joint_row, segment_row, logsum, grad_row = packed
    slot_count = joint_row.shape[0]
    query_rows, key_rows, value_rows = split_heads(joint_row)
    scores = masked_scores(query_rows, key_rows, segment_row)
    probabilities = jnp.exp(scores - logsum[:, :, None])
    upstream = grad_row.reshape(slot_count, HEADS, HEAD_SIZE)
    grad_probs = jnp.einsum(
        "qhe,khe->hqk", upstream, value_rows, preferred_element_type=jnp.float32
    )
    row_delta = jnp.sum(probabilities * grad_probs, axis=-1, keepdims=True)
    grad_scores = (probabilities * (grad_probs - row_delta)).astype(jnp.bfloat16)
    grad_query = (
        jnp.einsum("hqk,khe->qhe", grad_scores, key_rows, preferred_element_type=jnp.float32)
        * SCORE_SCALE
    )
    grad_key = (
        jnp.einsum("hqk,qhe->khe", grad_scores, query_rows, preferred_element_type=jnp.float32)
        * SCORE_SCALE
    )
    grad_value = jnp.einsum(
        "hqk,qhe->khe",
        probabilities.astype(jnp.bfloat16),
        upstream,
        preferred_element_type=jnp.float32,
    )
    stacked = jnp.stack([grad_query, grad_key, grad_value], axis=1)
    return stacked.reshape(slot_count, 3 * HEADS * HEAD_SIZE).astype(jnp.bfloat16)


def block_forward(hidden_in, segments, weights):
    joint_matrix, output_matrix, expand_matrix, shrink_matrix, gain_rows, bias_rows, inner_bias = (
        weights
    )
    gain_values = gain_rows.astype(jnp.float32)
    bias_values = bias_rows.astype(jnp.float32)
    row_count, slot_count = segments.shape
    zero_block = jnp.zeros_like(bias_values[0])
    joint_bias = jnp.concatenate([bias_values[0], zero_block, bias_values[1]])
    joint_out = (product(hidden_in.astype(jnp.bfloat16), joint_matrix) + joint_bias).astype(
        jnp.bfloat16
    )
    context, logsum = lax.map(
        attend_forward, (joint_out.reshape(row_count, slot_count, -1), segments)
    )
    context = context.reshape(row_count * slot_count, -1)
    attended = product(context, output_matrix) + bias_values[2]
    first_scaled, first_inverse = normalize(hidden_in + attended)
    first_norm = first_scaled * gain_values[0] + bias_values[3]
    pre_active = product(first_norm.astype(jnp.bfloat16), expand_matrix) + inner_bias.astype(
        jnp.float32
    )
    active = jax.nn.gelu(pre_active, approximate=False).astype(jnp.bfloat16)
    branch = product(active, shrink_matrix) + bias_values[4]
    second_scaled, second_inverse = normalize(first_norm + branch)
    result = second_scaled * gain_values[1] + bias_values[5]
    stored = (
        hidden_in,
        joint_out,
        context,
        logsum,
        first_scaled,
        first_inverse,
        pre_active,
        second_scaled,
        second_inverse,
    )
    return (result, stored)


def block_backward(grad_out, segments, weights, stored):
    joint_matrix, output_matrix, expand_matrix, shrink_matrix, gain_rows, bias_rows, inner_bias = (
        weights
    )
    (
        hidden_in,
        joint_out,
        context,
        logsum,
        first_scaled,
        first_inverse,
        pre_active,
        second_scaled,
        second_inverse,
    ) = stored
    gain_values = gain_rows.astype(jnp.float32)
    bias_values = bias_rows.astype(jnp.float32)
    row_count, slot_count = segments.shape
    features = hidden_in.shape[1]
    grad_second_bias = jnp.sum(grad_out, axis=0)
    grad_second_gain = jnp.sum(grad_out * second_scaled, axis=0)
    grad_sum = normalize_back(grad_out * gain_values[1], second_scaled, second_inverse)
    grad_branch = grad_sum.astype(jnp.bfloat16)
    active, gelu_back = jax.vjp(partial(jax.nn.gelu, approximate=False), pre_active)
    grad_shrink = product_left(active.astype(jnp.bfloat16), grad_branch)
    grad_active = product_right(grad_branch, shrink_matrix)
    grad_pre = gelu_back(grad_active)[0].astype(jnp.bfloat16)
    first_norm = first_scaled * gain_values[0] + bias_values[3]
    grad_expand = product_left(first_norm.astype(jnp.bfloat16), grad_pre)
    grad_first = grad_sum + product_right(grad_pre, expand_matrix)
    grad_first_bias = jnp.sum(grad_first, axis=0)
    grad_first_gain = jnp.sum(grad_first * first_scaled, axis=0)
    grad_middle = normalize_back(grad_first * gain_values[0], first_scaled, first_inverse)
    grad_attended = grad_middle.astype(jnp.bfloat16)
    grad_output = product_left(context, grad_attended)
    grad_context = product_right(grad_attended, output_matrix).astype(jnp.bfloat16)
    grad_joint_out = lax.map(
        attend_backward,
        (
            joint_out.reshape(row_count, slot_count, -1),
            segments,
            logsum,
            grad_context.reshape(row_count, slot_count, -1),
        ),
    )
    grad_joint_out = grad_joint_out.reshape(row_count * slot_count, -1)
    grad_joint = product_left(hidden_in.astype(jnp.bfloat16), grad_joint_out)
    grad_input = grad_middle + product_right(grad_joint_out, joint_matrix)
    joint_sums = jnp.sum(grad_joint_out, axis=0, dtype=jnp.float32)
    bias_grads = jnp.stack(
        [
            joint_sums[:features],
            joint_sums[2 * features :],
            jnp.sum(grad_attended, axis=0, dtype=jnp.float32),
            grad_first_bias,
            jnp.sum(grad_branch, axis=0, dtype=jnp.float32),
            grad_second_bias,
        ]
    )
    gain_grads = jnp.stack([grad_first_gain, grad_second_gain])
    inner_grad = jnp.sum(grad_pre, axis=0, dtype=jnp.float32)
    return (
        grad_input,
        (grad_joint, grad_output, grad_expand, grad_shrink, gain_grads, bias_grads, inner_grad),
    )


def factored_partials(gradient, weight, rows_old):
    squared = gradient * gradient + FLOOR_SQUARE
    rows_next = DECAY_RATE * rows_old + (1.0 - DECAY_RATE) * jnp.mean(squared, axis=2)
    return (
        rows_next,
        jnp.sum(squared, axis=1),
        jnp.sum(rows_next, axis=1),
        jnp.sum(weight * weight, axis=(1, 2)),
    )


def vector_partials(gradient, moments_old):
    moments_next = DECAY_RATE * moments_old + (1.0 - DECAY_RATE) * (
        gradient * gradient + FLOOR_SQUARE
    )
    return (moments_next, gradient * lax.rsqrt(moments_next))


def local_plain(
    tokens,
    segments,
    cotangent,
    joint_weight,
    output_weight,
    expand_weight,
    shrink_weight,
    norm_gains,
    biases,
    hidden_bias,
    joint_rows,
    joint_columns,
    output_rows,
    output_columns,
    expand_rows,
    expand_columns,
    shrink_rows,
    shrink_columns,
    gain_moments,
    bias_moments,
    hidden_moments,
):
    layers = joint_weight.shape[0]
    row_count, slot_count, features = tokens.shape
    hidden = tokens.astype(jnp.float32).reshape(row_count * slot_count, features)
    gathered_list = []
    stored_list = []
    for number in range(layers):
        weights = (
            lax.all_gather(joint_weight[number].astype(jnp.bfloat16), "fsdp", axis=0, tiled=True),
            lax.all_gather(output_weight[number].astype(jnp.bfloat16), "fsdp", axis=0, tiled=True),
            lax.all_gather(expand_weight[number].astype(jnp.bfloat16), "fsdp", axis=0, tiled=True),
            lax.all_gather(shrink_weight[number].astype(jnp.bfloat16), "fsdp", axis=0, tiled=True),
            lax.all_gather(norm_gains[number].astype(jnp.bfloat16), "fsdp", axis=1, tiled=True),
            lax.all_gather(biases[number].astype(jnp.bfloat16), "fsdp", axis=1, tiled=True),
            lax.all_gather(hidden_bias[number].astype(jnp.bfloat16), "fsdp", axis=0, tiled=True),
        )
        hidden, stored = block_forward(hidden, segments, weights)
        gathered_list.append(weights)
        stored_list.append(stored)
    activations = hidden.reshape(row_count, slot_count, features).astype(jnp.bfloat16)
    grad_hidden = cotangent.astype(jnp.float32).reshape(row_count * slot_count, features)
    collected = []
    for number in reversed(range(layers)):
        weights = (
            lax.all_gather(joint_weight[number].astype(jnp.bfloat16), "fsdp", axis=0, tiled=True),
            lax.all_gather(output_weight[number].astype(jnp.bfloat16), "fsdp", axis=0, tiled=True),
            lax.all_gather(expand_weight[number].astype(jnp.bfloat16), "fsdp", axis=0, tiled=True),
            lax.all_gather(shrink_weight[number].astype(jnp.bfloat16), "fsdp", axis=0, tiled=True),
            lax.all_gather(norm_gains[number].astype(jnp.bfloat16), "fsdp", axis=1, tiled=True),
            lax.all_gather(biases[number].astype(jnp.bfloat16), "fsdp", axis=1, tiled=True),
            lax.all_gather(hidden_bias[number].astype(jnp.bfloat16), "fsdp", axis=0, tiled=True),
        )
        grad_hidden, local_grads = block_backward(
            grad_hidden, segments, weights, stored_list[number]
        )
        grad_joint, grad_output, grad_expand, grad_shrink, gain_grads, bias_grads, inner_grad = (
            local_grads
        )
        shards = (
            lax.psum_scatter(grad_joint, "fsdp", scatter_dimension=0, tiled=True),
            lax.psum_scatter(grad_output, "fsdp", scatter_dimension=0, tiled=True),
            lax.psum_scatter(grad_expand, "fsdp", scatter_dimension=0, tiled=True),
            lax.psum_scatter(grad_shrink, "fsdp", scatter_dimension=0, tiled=True),
            lax.psum_scatter(gain_grads, "fsdp", scatter_dimension=1, tiled=True),
            lax.psum_scatter(bias_grads, "fsdp", scatter_dimension=1, tiled=True),
            lax.psum_scatter(inner_grad, "fsdp", scatter_dimension=0, tiled=True),
        )
        summed = (
            lax.psum(shards[0].astype(jnp.bfloat16), "dp").astype(jnp.float32),
            lax.psum(shards[1].astype(jnp.bfloat16), "dp").astype(jnp.float32),
            lax.psum(shards[2].astype(jnp.bfloat16), "dp").astype(jnp.float32),
            lax.psum(shards[3].astype(jnp.bfloat16), "dp").astype(jnp.float32),
            lax.psum(shards[4].astype(jnp.bfloat16), "dp").astype(jnp.float32),
            lax.psum(shards[5].astype(jnp.bfloat16), "dp").astype(jnp.float32),
            lax.psum(shards[6].astype(jnp.bfloat16), "dp").astype(jnp.float32),
        )
        collected.append(summed)
    collected = collected[::-1]
    input_gradient = grad_hidden.reshape(row_count, slot_count, features).astype(jnp.bfloat16)
    fsdp_count = lax.axis_size("fsdp")
    token_total = row_count * slot_count * lax.axis_size("dp") * fsdp_count
    root_scale = 1.0 / math.sqrt(token_total)
    stacked_grads = [
        jnp.stack([entry[index] for entry in collected]) * root_scale for index in range(7)
    ]
    matrices = (
        (stacked_grads[0], joint_weight, joint_rows, joint_columns),
        (stacked_grads[1], output_weight, output_rows, output_columns),
        (stacked_grads[2], expand_weight, expand_rows, expand_columns),
        (stacked_grads[3], shrink_weight, shrink_rows, shrink_columns),
    )
    partial_list = [factored_partials(item[0], item[1], item[2]) for item in matrices]
    vectors = (
        (stacked_grads[4], norm_gains, gain_moments),
        (stacked_grads[5], biases, bias_moments),
        (stacked_grads[6][:, None, :], hidden_bias[:, None, :], hidden_moments[:, None, :]),
    )
    vector_list = [vector_partials(item[0], item[2]) for item in vectors]
    vector_squares = jnp.concatenate(
        [jnp.sum(item[1] * item[1], axis=2) for item in vectors], axis=1
    )
    statistics = lax.psum(
        (
            partial_list[0][1],
            partial_list[1][1],
            partial_list[2][1],
            partial_list[3][1],
            jnp.stack([item[2] for item in partial_list], axis=1),
            jnp.stack([item[3] for item in partial_list], axis=1),
            vector_squares,
        ),
        "fsdp",
    )
    updates = []
    columns_list = []
    for index in range(4):
        gradient = matrices[index][0]
        total_rows = gradient.shape[1] * fsdp_count
        rows_next = partial_list[index][0]
        columns_next = DECAY_RATE * matrices[index][3] + (1.0 - DECAY_RATE) * (
            statistics[index] / total_rows
        )
        row_average = statistics[4][:, index] / total_rows
        estimate = rows_next[:, :, None] * columns_next[:, None, :] / row_average[:, None, None]
        updates.append(gradient * lax.rsqrt(estimate))
        columns_list.append(columns_next)
    matrix_squares = jnp.stack([jnp.sum(item * item, axis=(1, 2)) for item in updates], axis=1)
    vector_updates = jnp.concatenate(
        [jnp.sum(item[1] * item[1], axis=2) for item in vector_list], axis=1
    )
    norms = lax.psum((matrix_squares, vector_updates), "fsdp")
    matrix_next = []
    for index in range(4):
        gradient = matrices[index][0]
        entry_count = gradient.shape[1] * fsdp_count * gradient.shape[2]
        clip_ratio = jnp.sqrt(norms[0][:, index] / entry_count) / CLIP_LIMIT
        update = updates[index] / jnp.maximum(clip_ratio, 1.0)[:, None, None]
        stride = STEP_RATE * jnp.maximum(
            FLOOR_SCALE, jnp.sqrt(statistics[5][:, index] / entry_count)
        )
        matrix_next.append(matrices[index][1] - stride[:, None, None] * update)
    vector_next = []
    offset = 0
    for index in range(3):
        gradient = vectors[index][0]
        kinds = gradient.shape[1]
        entry_count = gradient.shape[2] * fsdp_count
        clip_ratio = jnp.sqrt(norms[1][:, offset : offset + kinds] / entry_count) / CLIP_LIMIT
        update = vector_list[index][1] / jnp.maximum(clip_ratio, 1.0)[:, :, None]
        stride = STEP_RATE * jnp.maximum(
            FLOOR_SCALE, jnp.sqrt(statistics[6][:, offset : offset + kinds] / entry_count)
        )
        vector_next.append(vectors[index][1] - stride[:, :, None] * update)
        offset = offset + kinds
    return (
        activations,
        input_gradient,
        stacked_grads[0],
        stacked_grads[1],
        stacked_grads[2],
        stacked_grads[3],
        stacked_grads[4],
        stacked_grads[5],
        stacked_grads[6],
        matrix_next[0],
        matrix_next[1],
        matrix_next[2],
        matrix_next[3],
        vector_next[0],
        vector_next[1],
        vector_next[2][:, 0, :],
        matrix_next[0].astype(jnp.bfloat16),
        matrix_next[1].astype(jnp.bfloat16),
        matrix_next[2].astype(jnp.bfloat16),
        matrix_next[3].astype(jnp.bfloat16),
        partial_list[0][0],
        columns_list[0],
        partial_list[1][0],
        columns_list[1],
        partial_list[2][0],
        columns_list[2],
        partial_list[3][0],
        columns_list[3],
        vector_list[0][0],
        vector_list[1][0],
        vector_list[2][0][:, 0, :],
    )


F32 = jnp.float32
BF = jnp.bfloat16
T = 512
D = 768


def nn(a, b):
    return lax.dot_general(a, b, (((1,), (0,)), ((), ())), preferred_element_type=F32)


def nt(a, b):
    return lax.dot_general(a, b, (((1,), (1,)), ((), ())), preferred_element_type=F32)


def rows_at(i, n):
    return pl.ds(pl.multiple_of(i * n, n), n)


def build_mask(seg_ref, bias_ref):
    row = seg_ref[...]
    wide = jnp.broadcast_to(row, (128, T)).T
    for j in range(T // 128):
        bias_ref[:, j * 128 : (j + 1) * 128] = jnp.where(
            wide == row[:, j * 128 : (j + 1) * 128], 0.0, MASK_VALUE
        ).astype(F32)


def joint_forward(xb, wa, vec, joint, tile=256):
    for b in range(3):
        @pl.loop(0, T // tile)
        def _(i, b=b):
            r = rows_at(i, tile)
            out = nn(xb[r, :], wa[b])
            if b == 0:
                out = out + vec[2:3, :]
            if b == 2:
                out = out + vec[3:4, :]
            joint[b, r, :] = out.astype(BF)


def head_masks():
    lane = lax.broadcasted_iota(jnp.int32, (1, 128), 1)
    return [
        jnp.where(lane < 64, 1.0, 0.0).astype(F32),
        jnp.where(lane >= 64, 1.0, 0.0).astype(F32),
    ]


def attend_forward_pair(p, joint, bias, ctx, logsum):
    lanes = pl.ds(pl.multiple_of(p * 128, 128), 128)
    masks = head_masks()
    q2 = joint[0, :, lanes]
    k2 = joint[1, :, lanes]
    vt = joint[2, :, lanes].T
    outs, sums = [], []
    for h in range(2):
        qm = q2 * (masks[h] * 0.125).astype(BF)
        st = nt(k2, qm) + bias[...]
        top = jnp.max(st, axis=0, keepdims=True)
        e = jnp.exp(st - top)
        total = jnp.sum(e, axis=0, keepdims=True)
        ct = nn(vt[64 * h : 64 * h + 64, :], e.astype(BF))
        outs.append(ct * (1.0 / total))
        sums.append(top + jnp.log(total))
    ctx[:, lanes] = jnp.concatenate(outs, axis=0).T.astype(BF)
    logsum[p] = jnp.concatenate(sums, axis=0)


def norm_parts(u):
    avg = jnp.mean(u, axis=-1, keepdims=True)
    c = u - avg
    var = jnp.mean(c * c, axis=-1, keepdims=True)
    inv = lax.rsqrt(var + NORM_EPSILON)
    return c * inv, inv


def out_forward(ctx, x, wo, vec, n1, r1, h, hb, tile=128):
    @pl.loop(0, T // tile)
    def _(i):
        r = rows_at(i, tile)
        u = nn(ctx[r, :], wo[...]) + vec[4:5, :] + x[r, :].astype(F32)
        n, inv = norm_parts(u)
        y = n * vec[0:1, :] + vec[5:6, :]
        n1[r, :] = n.astype(n1.dtype)
        r1[r, :] = jnp.broadcast_to(inv, (tile, 128))
        h[r, :] = y
        hb[r, :] = y.astype(BF)


def gelu_parts(z):
    a = jnp.abs(z)
    e = jnp.exp(z * z * -0.5)
    t = 1.0 / (1.0 + 0.23164189 * a)
    poly = t * (
        0.127414796 + t * (-0.142248368 + t * (0.7107068705 + t * (-0.7265760135 + t * 0.5307027145)))
    )
    tail = poly * e
    cdf = jnp.where(z >= 0.0, 1.0 - tail, tail)
    return z * cdf, cdf + z * (e * 0.3989422804014327)


def ffn_up(hb, we, vec, g, gp, b, tile=128):
    @pl.loop(0, T // tile)
    def _(i):
        r = rows_at(i, tile)
        z = nn(hb[r, :], we[b]) + vec[8 + b : 9 + b, :]
        act, der = gelu_parts(z)
        g[b, r, :] = act.astype(BF)
        gp[b, r, :] = der.astype(BF)


def ffn_down(g, ws, vec, h, n2, r2, x_out, xb_out, tile=128):
    @pl.loop(0, T // tile)
    def _(i):
        r = rows_at(i, tile)
        u = h[r, :] + vec[6:7, :]
        for b in range(4):
            u = u + nn(g[b, r, :], ws[b])
        n, inv = norm_parts(u)
        y = n * vec[1:2, :] + vec[7:8, :]
        n2[r, :] = n.astype(n2.dtype)
        r2[r, :] = jnp.broadcast_to(inv, (tile, 128))
        if x_out is not None:
            x_out[r, :] = y
        xb_out[r, :] = y.astype(BF)


def sum8(v):
    return jnp.sum(v.reshape(v.shape[0] // 8, 8, v.shape[1]), axis=0)


def norm_backward(dy, n, r, gain_row, du, dub, sums, rows, tile=128):
    def step(i, carry):
        s = rows_at(i, tile)
        g = dy[s, :].astype(F32)
        nv = n[s, :].astype(F32)
        inv = r[s, 0:1]
        e = g * gain_row
        m1 = jnp.mean(e, axis=-1, keepdims=True)
        m2 = jnp.mean(e * nv, axis=-1, keepdims=True)
        d = inv * (e - m1 - nv * m2)
        db = d.astype(BF)
        du[s, :] = d
        dub[s, :] = db
        return (
            carry[0] + sum8(g * nv),
            carry[1] + sum8(g),
            carry[2] + sum8(db.astype(F32)),
        )

    zero = jnp.zeros((8, D), F32)
    out = lax.fori_loop(0, T // tile, step, (zero, zero, zero))
    for k in range(3):
        sums[rows[k] : rows[k] + 1, :] = jnp.sum(out[k], axis=0, keepdims=True)


def transpose_into(src, dst, tile=128):
    @pl.loop(0, T // tile)
    def _(i):
        dst[:, rows_at(i, tile)] = src[rows_at(i, tile), :].T


def weight_grad(at, bmat, out, tile=256):
    @pl.loop(0, D // tile)
    def _(i):
        r = rows_at(i, tile)
        out[r, :] = nn(at[r, :], bmat[...]).astype(BF)


def ffn_back_block(dob, ws, gp, dz, sums, b, tile=128):
    def step(i, acc):
        r = rows_at(i, tile)
        v = (nt(dob[r, :], ws[b]) * gp[b, r, :].astype(F32)).astype(BF)
        dz[b, r, :] = v
        return acc + sum8(v.astype(F32))

    acc = lax.fori_loop(0, T // tile, step, jnp.zeros((8, D), F32))
    sums[8 + b : 9 + b, :] = jnp.sum(acc, axis=0, keepdims=True)


def ffn_back_input(dz, we, du, tile=128):
    @pl.loop(0, T // tile)
    def _(i):
        r = rows_at(i, tile)
        u = du[r, :]
        for b in range(4):
            u = u + nt(dz[b, r, :], we[b])
        du[r, :] = u


def context_back(dab, wo, dc, tile=256):
    @pl.loop(0, T // tile)
    def _(i):
        r = rows_at(i, tile)
        dc[r, :] = nt(dab[r, :], wo[...]).astype(BF)


def attend_backward_pair(p, joint, bias, logsum, dc, dj):
    lanes = pl.ds(pl.multiple_of(p * 128, 128), 128)
    masks = head_masks()
    q2 = joint[0, :, lanes]
    k2 = joint[1, :, lanes]
    v2 = joint[2, :, lanes]
    d2 = dc[:, lanes]
    kt = k2.T
    ls = logsum[p]
    dk = jnp.zeros((T, 128), F32)
    dv = jnp.zeros((T, 128), F32)
    dqt = []
    for h in range(2):
        qm = q2 * (masks[h] * 0.125).astype(BF)
        dm = d2 * masks[h].astype(BF)
        prob = jnp.exp(nt(k2, qm) + bias[...] - ls[h : h + 1, :])
        dp = nt(v2, dm)
        delta = jnp.sum(prob * dp, axis=0, keepdims=True)
        ds = (prob * (dp - delta)).astype(BF)
        dv = dv + nn(prob.astype(BF), dm)
        dk = dk + nn(ds, qm)
        dqt.append(nn(kt[64 * h : 64 * h + 64, :], ds))
    dj[0, :, lanes] = (jnp.concatenate(dqt, axis=0) * 0.125).T.astype(BF)
    dj[1, :, lanes] = dk.astype(BF)
    dj[2, :, lanes] = dv.astype(BF)


def input_back(dj, wa, du, dx, sums, tile=128):
    def step(i, carry):
        r = rows_at(i, tile)
        u = du[r, :]
        for b in range(3):
            u = u + nt(dj[b, r, :], wa[b])
        dx[r, :] = u.astype(dx.dtype)
        return (carry[0] + sum8(dj[0, r, :].astype(F32)), carry[1] + sum8(dj[2, r, :].astype(F32)))

    zero = jnp.zeros((8, D), F32)
    out = lax.fori_loop(0, T // tile, step, (zero, zero))
    sums[2:3, :] = jnp.sum(out[0], axis=0, keepdims=True)
    sums[3:4, :] = jnp.sum(out[1], axis=0, keepdims=True)


MESH = pl.DeviceIdType.MESH
PAIRS = 6
PIECE = 96
GROUPS = 6


def place():
    q = lax.axis_index("dp")
    f = lax.axis_index("fsdp")
    z = f // 2
    c = f % 2
    x_side = (q + 1 - 2 * (q % 2), f)
    y_side = ((q + 2) % 4, f)
    sibling = (q, f + 1 - 2 * c)
    planes = [(q, (f + 2 * k) % 8) for k in range(1, 4)]
    return q, z, c, x_side, y_side, sibling, planes


def greet(peers):
    barrier = pltpu.get_barrier_semaphore()
    for peer in peers:
        pl.semaphore_signal(barrier, inc=1, device_id=peer, device_id_type=MESH)
    pl.semaphore_wait(barrier, len(peers))


def hidden_piece(kind, b, zz, c, first, count):
    if kind < 2:
        start = 192 * zz + 96 * c + first
        return b, pl.ds(pl.multiple_of(start, 16), count)
    start = 384 * c + 96 * b + first
    return zz, pl.ds(pl.multiple_of(start, 16), count)


PARTS = [(g, first, 32) for g in range(6) for first in (0, 32, 64)]


class Gather:
    def __init__(self, whole, sbuf, sems):
        self.whole, self.sbuf, self.sems = whole, sbuf, sems
        q, z, c, self.x_side, self.y_side, self.sibling, self.planes = place()
        self.q, self.z, self.c = q, z, c
        self.qx = q + 1 - 2 * (q % 2)
        self.qy = (q + 2) % 4
        self.qd = (self.qx + 2) % 4
        self.others = [(z + k) % 4 for k in range(1, 4)]

    def spot(self, k, b, zz, cols=None):
        g, first, count = PARTS[k]
        lead, rows = hidden_piece(g % 3, b, zz, self.c, first, count)
        if cols is None:
            return self.whole.at[g, lead, rows, :]
        return self.whole.at[g, lead, rows, pl.ds(384 * cols, 384)]

    def send(self, k, src, dst, slot, peer):
        pltpu.make_async_remote_copy(
            src_ref=src, dst_ref=dst, send_sem=self.sems.at[k, slot], recv_sem=self.sems.at[k, slot + 1],
            device_id=peer, device_id_type=MESH,
        ).start()

    def total(self, k, slot, rows, cols=768):
        lead = self.whole.at[0, 0, pl.ds(0, rows), pl.ds(0, cols)] if rows <= 768 else self.whole.at[0, pl.ds(0, rows // 768)]
        pltpu.make_async_copy(lead, lead, self.sems.at[k, slot]).wait()

    def z_send(self, k):
        g, first, count = PARTS[k]
        src = self.sbuf.at[g, self.q, pl.ds(first, count), :]
        for peer in self.planes:
            self.send(k, src, self.spot(k, self.q, self.z), 0, peer)
        for b in range(4):
            mine = self.sbuf.at[g, b, pl.ds(first, count), :]
            self.send(k, mine, self.spot(k, b, self.z), 10, self.sibling)
            pltpu.make_async_copy(mine, self.spot(k, b, self.z), self.sems.at[k, 12]).start()

    def xy_send(self, k):
        count = PARTS[k][2]
        self.total(k, 1, 3 * count)
        for zz in self.others:
            spot = self.spot(k, self.q, zz)
            self.send(k, spot, spot, 2, self.x_side)
            self.send(k, spot, spot, 4, self.y_side)
        for zz in self.others:
            spot = self.spot(k, self.q, zz)
            self.send(k, spot, spot, 10, self.sibling)

    def diagonal_send(self, k):
        count = PARTS[k][2]
        self.total(k, 3, 3 * count)
        self.total(k, 5, 3 * count)
        for zz in self.others:
            spot = self.spot(k, self.qy, zz, 0)
            self.send(k, spot, spot, 6, self.x_side)
            spot = self.spot(k, self.qx, zz, 1)
            self.send(k, spot, spot, 8, self.y_side)
        for zz in self.others:
            for b in (self.qx, self.qy):
                spot = self.spot(k, b, zz)
                self.send(k, spot, spot, 10, self.sibling)

    def last_send(self, k):
        count = PARTS[k][2]
        self.total(k, 7, 3 * count, 384)
        self.total(k, 9, 3 * count, 384)
        for zz in self.others:
            spot = self.spot(k, self.qd, zz)
            self.send(k, spot, spot, 10, self.sibling)

    def finish(self, k):
        count = PARTS[k][2]
        self.total(k, 11, 16 * count)
        self.total(k, 12, 4 * count)

    def drain(self, k):
        count = PARTS[k][2]
        self.total(k, 0, 3 * count)
        self.total(k, 2, 3 * count)
        self.total(k, 4, 3 * count)
        self.total(k, 6, 3 * count, 384)
        self.total(k, 8, 3 * count, 384)
        self.total(k, 10, 16 * count)


UNIT_TIMES = (("joint", 3.0),) + tuple((f"att{p}", 1.4) for p in range(6)) + (("out", 2.0),) + tuple(
    (f"up{b}", 1.7) for b in range(4)
) + (("down", 3.0),)


SPREAD = 0.85


def forward_plan():
    count = len(PARTS)
    steps = []
    for i in range(count + 3):
        for lag, kind in enumerate(("xy", "dg", "last", "fin")):
            if 0 <= i - lag < count:
                steps.append((kind, i - lag))
    units = [(layer, name, cost) for layer in range(2) for name, cost in UNIT_TIMES]
    last = {PARTS[k][0]: k for k in range(count)}
    need = {"joint": 0, "up0": 1, "down": 2}
    order, finished, at, budget = [], set(), 0, 0.0
    for step in steps:
        order.append(step)
        if step[0] == "fin":
            finished.add(step[1])
        budget += SPREAD
        while at < len(units):
            layer, name, cost = units[at]
            if name in need and last[3 * layer + need[name]] not in finished:
                budget = min(budget, 0.0)
                break
            if cost > budget + 0.5:
                break
            budget -= cost
            order.append(("run", layer, name))
            at += 1
    return order + [("run", layer, name) for layer, name, cost in units[at:]]


def forward_kernel(
    tokens, seg, vecs, joint_w, output_w, expand_w, shrink_w,
    whole, vec_out, x_saved, j_saved, c_saved, l_saved, n1_saved, r1_saved, g_saved, gp_saved, n2_saved, r2_saved, final, squares,
    stage, sbuf, wv, bias, x1, h, hb, xb, joint, ctx, logsum, n1, r1, g, gp, n2, r2, vg, vec,
    sems, stage_sems, wv_sems, vec_sems, out_sems,
):
    masters = (joint_w, output_w, expand_w, shrink_w)
    gather = Gather(whole, sbuf, sems)
    q, z, c = gather.q, gather.z, gather.c

    def stage_copies(grp):
        layer, kind = divmod(grp, 3)
        slot = grp % 2
        out = []
        for b in range(4):
            if kind == 0:
                src = output_w.at[layer] if b == 3 else joint_w.at[layer, :, pl.ds(768 * b, 768)]
            elif kind == 1:
                src = expand_w.at[layer, :, pl.ds(768 * b, 768)]
            else:
                src = shrink_w.at[layer, pl.ds(96 * b, 96), :]
            out.append(pltpu.make_async_copy(src, stage.at[slot, b], stage_sems.at[slot, b]))
        return out

    def take(grp):
        layer, kind = divmod(grp, 3)
        slot = grp % 2
        for cp in stage_copies(grp):
            cp.wait()
        sums = []
        for b in range(4):
            value = stage[slot, b]
            sbuf[grp, b] = value.astype(BF)
            sums.append(jnp.sum(value * value, axis=0, keepdims=True))
        if kind == 0:
            squares[4 * layer : 4 * layer + 1, :] = sums[0] + sums[1] + sums[2]
            squares[4 * layer + 1 : 4 * layer + 2, :] = sums[3]
        else:
            row = 4 * layer + 1 + kind
            squares[row : row + 1, :] = sums[0] + sums[1] + sums[2] + sums[3]
        if grp + 2 < GROUPS:
            for cp in stage_copies(grp + 2):
                cp.start()

    for grp in range(2):
        for cp in stage_copies(grp):
            cp.start()
    take(0)
    greet([gather.x_side, gather.y_side, gather.sibling] + gather.planes)
    gather.z_send(0)

    vg[z, c] = vecs[...].reshape(32, 128)

    def vec_copy(zz, peer, slot):
        return pltpu.make_async_remote_copy(
            src_ref=vg.at[zz, c], dst_ref=vg.at[zz, c], send_sem=vec_sems.at[2 * slot], recv_sem=vec_sems.at[2 * slot + 1],
            device_id=peer, device_id_type=MESH,
        )

    def vec_total(slot, count):
        ref = vg.at[0, pl.ds(0, 1)] if count == 1 else (vg.at[0, pl.ds(0, 2)] if count == 2 else vg.at[pl.ds(0, 2)])
        pltpu.make_async_copy(ref, ref, vec_sems.at[slot]).wait()

    for k, peer in enumerate(gather.planes):
        vec_copy(z, peer, k).start()
    take(1)
    gather.z_send(1)
    take(2)
    take(3)
    for k in range(3):
        vec_copy((z + 3 - k) % 4, gather.planes[0], k).wait_recv()
    for zz in range(4):
        vec_copy(zz, gather.sibling, 3 + zz).start()
    take(4)
    take(5)
    build_mask(seg, bias)
    for zz in range(4):
        vec_copy(zz, gather.sibling, 3 + zz).wait_recv()
    lane = lax.broadcasted_iota(jnp.int32, (128, 768), 1)
    spot = lax.broadcasted_iota(jnp.int32, (128, 768), 0)
    for layer in range(2):
        acc = jnp.zeros((8, 768), F32)
        for m in range(8):
            pick = jnp.where((lane == spot + 96 * m) & (spot < 96), 1.0, 0.0).astype(BF)
            acc = acc + nn(vg[m // 2, m % 2, 16 * layer : 16 * layer + 8, :].astype(BF), pick)
            for k in range(3):
                row = vg[m // 2, m % 2, 16 * layer + 8 + k : 16 * layer + 9 + k, :].astype(BF).astype(F32)
                start = 384 * (m % 2) + 128 * k
                vec[layer, 8 + m // 2 : 9 + m // 2, start : start + 128] = row
        vec[layer, 0:8, :] = acc
        vec[layer, 12:16, :] = jnp.zeros((4, 768), F32)

    started = []

    def save(src, dst):
        n = len(started)
        cp = pltpu.make_async_copy(src, dst, out_sems.at[n])
        cp.start()
        started.append(cp)

    def load(grp):
        return pltpu.make_async_copy(whole.at[grp], wv.at[grp % 3], wv_sems.at[grp % 3])

    def event(kind, k):
        if kind == "xy":
            gather.xy_send(k)
            if k + 2 < len(PARTS):
                gather.z_send(k + 2)
        elif kind == "dg":
            gather.diagonal_send(k)
        elif kind == "last":
            gather.last_send(k)
        elif kind == "fin":
            gather.finish(k)
            grp, first, count = PARTS[k]
            if first + count == 96:
                load(grp).start()

    order = forward_plan()
    pos = 0
    while pos < len(order):
        item = order[pos]
        if item[0] != "run":
            event(*item)
            pos += 1
            continue
        _, layer, name = item
        vl = vec.at[layer]
        x_in = tokens if layer == 0 else x1
        xb_in = tokens if layer == 0 else xb
        if name == "joint":
            load(3 * layer).wait()
            joint_forward(xb_in, wv.at[0], vl, joint.at[layer])
            save(joint.at[layer], j_saved.at[layer])
        elif name.startswith("att"):
            hooks, first = {}, int(name[3:])
            p, look = first, pos
            while True:
                it = order[look]
                if it[0] == "run":
                    if not it[2].startswith("att"):
                        break
                    p = int(it[2][3:]) + 1
                else:
                    hooks.setdefault(p, []).append(it)
                look += 1
            tail = hooks.pop(6, [])

            @pl.loop(0, PAIRS)
            def _(p):
                for at, items in hooks.items():
                    @pl.when(p == at)
                    def _():
                        for it in items:
                            event(*it)
                attend_forward_pair(p, joint.at[layer], bias, ctx.at[layer], logsum.at[layer])

            for it in tail:
                event(*it)
            save(ctx.at[layer], c_saved.at[layer])
            save(logsum.at[layer], l_saved.at[layer])
            pos = look
            continue
        elif name == "out":
            out_forward(ctx.at[layer], x_in, wv.at[0, 3], vl, n1.at[layer], r1.at[layer], h, hb)
            save(n1.at[layer], n1_saved.at[layer])
            save(r1.at[layer], r1_saved.at[layer])
        elif name.startswith("up"):
            b = int(name[2:])
            if b == 0:
                load(3 * layer + 1).wait()
            ffn_up(hb, wv.at[1], vl, g.at[layer], gp.at[layer], b)
            if b == 3:
                save(g.at[layer], g_saved.at[layer])
                save(gp.at[layer], gp_saved.at[layer])
        else:
            load(3 * layer + 2).wait()
            ffn_down(g.at[layer], wv.at[2], vl, h, n2.at[layer], r2.at[layer], x1 if layer == 0 else None, xb if layer == 0 else hb)
            save(n2.at[layer], n2_saved.at[layer])
            save(r2.at[layer], r2_saved.at[layer])
            if layer == 0:
                save(xb, x_saved)
            else:
                save(hb, final)
        pos += 1
    save(vec, vec_out)
    for k in range(len(PARTS)):
        gather.drain(k)
    for k in range(3):
        vec_copy(z, gather.planes[k], k).wait_send()
    for zz in range(4):
        vec_copy(zz, gather.sibling, 3 + zz).wait_send()
    for cp in started:
        cp.wait()


def forward_call(tokens, seg, vecs, joint_w, output_w, expand_w, shrink_w):
    sd = jax.ShapeDtypeStruct
    any_spec = pl.BlockSpec(memory_space=pl.ANY)
    vm = pl.BlockSpec(memory_space=pltpu.VMEM)
    V = pltpu.VMEM
    saved = [
        sd((6, 4, 768, 768), BF),
        sd((2, 16, 768), F32),
        sd((T, D), BF),
        sd((2, 3, T, D), BF),
        sd((2, T, D), BF),
        sd((2, 6, 2, T), F32),
        sd((2, T, D), BF),
        sd((2, T, 128), F32),
        sd((2, 4, T, D), BF),
        sd((2, 4, T, D), BF),
        sd((2, T, D), BF),
        sd((2, T, 128), F32),
        sd((T, D), BF),
        sd((8, 768), F32),
    ]
    scratch = [
        V((2, 4, 96, 768), F32),
        V((6, 4, 96, 768), BF),
        V((3, 4, 768, 768), BF),
        V((T, T), F32),
        V((T, D), F32),
        V((T, D), F32),
        V((T, D), BF),
        V((T, D), BF),
        V((2, 3, T, D), BF),
        V((2, T, D), BF),
        V((2, 6, 2, T), F32),
        V((2, T, D), BF),
        V((2, T, 128), F32),
        V((2, 4, T, D), BF),
        V((2, 4, T, D), BF),
        V((2, T, D), BF),
        V((2, T, 128), F32),
        V((4, 2, 32, 128), F32),
        V((2, 16, 768), F32),
        pltpu.SemaphoreType.DMA((len(PARTS), 13)),
        pltpu.SemaphoreType.DMA((2, 4)),
        pltpu.SemaphoreType.DMA((3,)),
        pltpu.SemaphoreType.DMA((14,)),
        pltpu.SemaphoreType.DMA((24,)),
    ]
    return pl.pallas_call(
        forward_kernel,
        out_shape=saved,
        in_specs=[vm, vm, vm] + [any_spec] * 4,
        out_specs=[any_spec] * 13 + [vm],
        scratch_shapes=scratch,
        compiler_params=pltpu.CompilerParams(
            collective_id=0, has_side_effects=True, vmem_limit_bytes=62 << 20
        ),
        name="forward",
    )(tokens, seg, vecs, joint_w, output_w, expand_w, shrink_w)


def pack_vectors(gains, biases, hidden, fill=0.0):
    rows = jnp.pad(jnp.concatenate([gains, biases], axis=1), ((0, 0), (0, 0), (0, 32)), constant_values=fill)
    tail = jnp.concatenate([hidden.reshape(2, 3, 128), jnp.full((2, 5, 128), fill, F32)], axis=1)
    return jnp.concatenate([rows, tail], axis=1)


def pack_rows(joint, output, expand, shrink):
    wide = jnp.pad(jnp.stack([joint, output, expand], axis=1), ((0, 0), (0, 0), (0, 32)), constant_values=1.0)
    rows = jnp.concatenate([wide, shrink.reshape(2, 3, 128)], axis=1).reshape(12, 128)
    return jnp.pad(rows, ((0, 4), (0, 0)), constant_values=1.0)


ROOT_SCALE = 1.0 / math.sqrt(32 * T)

BACK_UNITS = (
    (("ln2", 3.5),)
    + tuple((f"s{i}", 2.0) for i in range(4))
    + tuple((f"dz{i}", 2.0) for i in range(4))
    + (("ht", 1.2), ("e0", 3.5), ("e1", 3.5), ("dh", 4.5), ("ln1", 3.5), ("o", 3.5))
    + tuple((f"att{p}", 2.6) for p in range(6))
    + (("xt", 0.8), ("q0", 2.8), ("q1", 2.8), ("dx", 3.5))
)
GROUP_OF = {"s": 0, "e": 1, "o": 2, "q": 2}
PARTS_OF = {"s0": (0,), "s1": (1,), "s2": (2,), "s3": (3,), "e0": (0, 1), "e1": (2, 3), "q0": (0, 1), "q1": (2, 3)}


def backward_plan():
    now, xy_free, z_free, core_free = 0.0, 0.0, 0.0, 0.0
    pending, order, summed = [], [], set()

    def emit(entry):
        nonlocal now, xy_free, z_free
        ready, name, t, zz = entry
        now = max(now, ready) + 0.4
        order.append((name, t, zz))
        if name == "xy1":
            xy_free = max(xy_free, now) + 3.2
            pending.append((xy_free + 1.5, "xy2", t, zz))
        elif name == "xy2":
            xy_free = max(xy_free, now) + 1.6
            pending.append((xy_free + 1.5, "z", t, zz))
        elif name == "z":
            z_free = max(z_free, now) + 3.2
            if sum(1 for o in order if o[0] == "z" and o[1] == t) == 4:
                pending.append((z_free + 1.5, "sum", t, 0))
        elif name == "sum":
            summed.add(t)
            xy_free = max(xy_free, now) + 3.2
            pending.append((xy_free + 1.5, "ag", t, 0))
        elif name == "ag":
            xy_free = max(xy_free, now) + 1.6
            pending.append((xy_free + 1.5, "fin", t, 0))
        elif name == "fin":
            pending.append((now, "stat", t, 0))
        elif name == "stat":
            now += 1.0
        elif name == "vec" and zz < 4:
            pending.append((now + 2.5, "vec", t, zz + 1))

    def step(limit):
        pending.sort()
        if pending and pending[0][0] <= limit:
            emit(pending.pop(0))
            return True
        return False

    for layer in (1, 0):
        for name, cost in BACK_UNITS:
            while step(now):
                pass
            if name[0] in GROUP_OF and name != "ln2":
                t = 3 * (1 - layer) + GROUP_OF[name[0]]
                while t >= 3 and t - 3 not in summed:
                    step(1e9)
            order.append(("run", layer, name))
            now += cost
            for zz in PARTS_OF.get(name, ()):
                core_free = max(core_free, now) + 1.0
                pending.append((core_free + 1.5, "xy1", 3 * (1 - layer) + GROUP_OF[name[0]], zz))
    pending.append((now, "vec", 0, 0))
    while step(1e9):
        pass
    return order


class Reduce:
    def __init__(self, gb, rc, rx1, ry1, rx2, ry2, rz, fin, sems, group_sems, credits):
        self.gb, self.rc, self.rx1, self.ry1, self.rx2, self.ry2, self.rz, self.fin = gb, rc, rx1, ry1, rx2, ry2, rz, fin
        self.sems, self.group_sems, self.credits = sems, group_sems, credits
        q, z, c, self.x_side, self.y_side, self.sibling, self.planes = place()
        self.q, self.z, self.c = q, z, c
        self.ax, self.ay = q % 2, q // 2

    def send(self, src, dst, sem, peer):
        pltpu.make_async_remote_copy(
            src_ref=src, dst_ref=dst, send_sem=sem[0], recv_sem=sem[1], device_id=peer, device_id_type=MESH
        ).start()

    def pair(self, t, zz, slot):
        return self.sems.at[4 * t + zz, 2 * slot], self.sems.at[4 * t + zz, 2 * slot + 1]

    def group_pair(self, t, slot):
        return self.group_sems.at[t, 2 * slot], self.group_sems.at[t, 2 * slot + 1]

    def wait(self, ref, sem):
        pltpu.make_async_copy(ref, ref, sem).wait()

    def credit_wait(self, t, phase, zz):
        if t > 0:
            pl.semaphore_wait(self.credits.at[phase, zz], 1)

    def credit_give(self, t, phase, zz, peer):
        if t < 5:
            pl.semaphore_signal(self.credits.at[phase, zz], inc=1, device_id=peer, device_id_type=MESH)

    def core_send(self, t, zz):
        self.credit_wait(t, 0, zz)
        self.send(self.gb.at[t % 3, :, :, zz, 1 - self.c], self.rc.at[zz], self.pair(t, zz, 0), self.sibling)

    def add(self, ref, other):
        ref[...] = (ref[...].astype(F32) + other[...].astype(F32)).astype(BF)

    def xy1(self, t, zz):
        gb, c = self.gb.at[t % 3], self.c
        self.wait(self.rc.at[0], self.pair(t, zz, 0)[1])
        for by in range(2):
            for bx in range(2):
                self.add(gb.at[by, bx, zz, c], self.rc.at[zz, by, bx])
        self.credit_give(t, 0, zz, self.sibling)
        self.credit_wait(t, 1, zz)
        self.send(gb.at[:, 1 - self.ax, zz, c, pl.ds(0, 48)], self.rx1.at[zz], self.pair(t, zz, 1), self.x_side)
        self.credit_wait(t, 2, zz)
        self.send(gb.at[1 - self.ay, :, zz, c, pl.ds(48, 48)], self.ry1.at[zz], self.pair(t, zz, 2), self.y_side)

    def xy2(self, t, zz):
        gb, c = self.gb.at[t % 3], self.c
        self.wait(self.rx1.at[0], self.pair(t, zz, 1)[1])
        self.wait(self.ry1.at[0], self.pair(t, zz, 2)[1])
        for k in range(2):
            self.add(gb.at[k, self.ax, zz, c, pl.ds(0, 48)], self.rx1.at[zz, k])
            self.add(gb.at[self.ay, k, zz, c, pl.ds(48, 48)], self.ry1.at[zz, k])
        self.credit_give(t, 1, zz, self.x_side)
        self.credit_give(t, 2, zz, self.y_side)
        self.credit_wait(t, 3, zz)
        self.send(gb.at[self.ay, 1 - self.ax, zz, c, pl.ds(48, 48)], self.rx2.at[zz], self.pair(t, zz, 3), self.x_side)
        self.credit_wait(t, 4, zz)
        self.send(gb.at[1 - self.ay, self.ax, zz, c, pl.ds(0, 48)], self.ry2.at[zz], self.pair(t, zz, 4), self.y_side)

    def z_send(self, t, zz):
        gb, c = self.gb.at[t % 3], self.c
        self.wait(self.rx2.at[0], self.pair(t, zz, 3)[1])
        self.wait(self.ry2.at[0], self.pair(t, zz, 4)[1])
        self.add(gb.at[self.ay, self.ax, zz, c, pl.ds(48, 48)], self.rx2.at[zz])
        self.add(gb.at[self.ay, self.ax, zz, c, pl.ds(0, 48)], self.ry2.at[zz])
        self.credit_give(t, 3, zz, self.x_side)
        self.credit_give(t, 4, zz, self.y_side)

        @pl.when(self.z != zz)
        def _():
            self.send(
                gb.at[self.ay, self.ax, zz, c], self.rz.at[t, (self.z + 3 - zz) % 4], self.group_pair(t, 0),
                (self.q, 2 * zz + c),
            )

    def total(self, t):
        gb, c = self.gb.at[t % 3], self.c
        self.wait(self.rz.at[0], self.group_pair(t, 0)[1])
        own = gb[self.ay, self.ax, self.z, c].astype(F32)
        for k in range(3):
            own = own + self.rz[t, k].astype(F32)
        self.fin[t, self.q] = own.astype(BF)
        spot = self.fin.at[t, self.q]
        self.send(spot, spot, self.group_pair(t, 1), self.x_side)
        self.send(spot, spot, self.group_pair(t, 2), self.y_side)

    def share(self, t):
        self.wait(self.fin.at[0, 0], self.group_pair(t, 1)[1])
        self.wait(self.fin.at[0, 0], self.group_pair(t, 2)[1])
        qx = self.q + 1 - 2 * self.ax
        qy = (self.q + 2) % 4
        spot = self.fin.at[t, qy, pl.ds(0, 48)]
        self.send(spot, spot, self.group_pair(t, 3), self.x_side)
        spot = self.fin.at[t, qx, pl.ds(48, 48)]
        self.send(spot, spot, self.group_pair(t, 4), self.y_side)

    def finish(self, t):
        self.wait(self.fin.at[0, 0, pl.ds(0, 48)], self.group_pair(t, 3)[1])
        self.wait(self.fin.at[0, 0, pl.ds(0, 48)], self.group_pair(t, 4)[1])

    def drain(self, t):
        for zz in range(4):
            self.wait(self.rc.at[0], self.pair(t, zz, 0)[0])
            self.wait(self.rx1.at[0], self.pair(t, zz, 1)[0])
            self.wait(self.ry1.at[0], self.pair(t, zz, 2)[0])
            self.wait(self.rx2.at[0], self.pair(t, zz, 3)[0])
            self.wait(self.ry2.at[0], self.pair(t, zz, 4)[0])
        self.wait(self.rz.at[0], self.group_pair(t, 0)[0])

    def drain_share(self, t):
        self.wait(self.fin.at[0, 0], self.group_pair(t, 1)[0])
        self.wait(self.fin.at[0, 0], self.group_pair(t, 2)[0])
        self.wait(self.fin.at[0, 0, pl.ds(0, 48)], self.group_pair(t, 3)[0])
        self.wait(self.fin.at[0, 0, pl.ds(0, 48)], self.group_pair(t, 4)[0])


def backward_kernel(
    cot, seg, vec, squares, rows_old, columns_old, vec_now, vec_old,
    tokens, x_saved, whole, j_saved, c_saved, l_saved, n1_saved, r1_saved, g_saved, gp_saved, n2_saved, r2_saved,
    fin, grad_in, rows_new, columns_new, column_scale, vec_grad, vec_scale,
    gb, rc, rx1, ry1, rx2, ry2, rz, wv, g, dz, dj, ctx, n1, n2, r1, r2, logsum, xb, dob, at, hb, bias, du, sums, vr, va,
    row_cols, pay, pay_in, pay_z, pay_sum,
    sems, group_sems, credits, load_sems, vec_sems, pay_sems,
):
    red = Reduce(gb, rc, rx1, ry1, rx2, ry2, rz, fin, sems, group_sems, credits)
    q, z, c = red.q, red.z, red.c
    sources = {
        "n2": (n2_saved, n2), "r2": (r2_saved, r2), "g": (g_saved, g), "dz": (gp_saved, dz), "n1": (n1_saved, n1),
        "r1": (r1_saved, r1), "ctx": (c_saved, ctx), "dj": (j_saved, dj), "logsum": (l_saved, logsum), "xb": (None, xb),
    }
    names = list(sources)

    def load(name, layer):
        src, dst = sources[name]
        if name == "xb":
            src = x_saved if layer == 1 else tokens
        else:
            src = src.at[layer]
        return pltpu.make_async_copy(src, dst, load_sems.at[names.index(name)])

    def weights(t):
        layer, kind = 1 - t // 3, (2, 1, 0)[t % 3]
        return pltpu.make_async_copy(whole.at[3 * layer + kind], wv.at[t % 2], load_sems.at[10 + t % 2])

    def need(layer, *which):
        for name in which:
            load(name, layer).wait()

    def release(layer, *which):
        if layer == 1:
            for name in which:
                load(name, 0).start()

    def next_weights(t):
        if t + 2 < 6:
            weights(t + 2).start()

    for name in ("n2", "r2", "g"):
        load(name, 1).start()
    weights(0).start()
    load("dz", 1).start()
    weights(1).start()
    for name in ("n1", "r1", "ctx", "dj", "logsum", "xb"):
        load(name, 1).start()
    build_mask(seg, bias)
    sums[...] = jnp.zeros_like(sums)
    greet([red.x_side, red.y_side, red.sibling] + red.planes)

    def blocks_pair(slot, b, pair, left):
        out = nn(at[pl.ds(384 * pair, 384), :], left).astype(BF)
        gb[slot, b // 2, b % 2, pl.ds(2 * pair, 2)] = out.reshape(2, 2, 96, 768)

    def unit(layer, name):
        base = 3 * (1 - layer)
        vl, sl = vec.at[layer], sums.at[layer]
        if name == "ln2":
            need(layer, "n2", "r2")
            norm_backward(cot if layer == 1 else du, n2, r2, vl[1:2, :], du, dob, sl, (1, 7, 6))
            release(layer, "n2", "r2")
        elif name[0] == "s":
            zz = int(name[1])
            if zz == 0:
                need(layer, "g")
                if base >= 3:
                    red.drain(base - 3)
            transpose_into(g.at[zz], at)
            for cc in range(2):
                out = nn(at[pl.ds(384 * cc, 384), :], dob[...]).astype(BF)
                gb[base % 3, :, :, zz, cc] = out.reshape(2, 2, 96, 768)
            red.core_send(base, zz)
            if zz == 3:
                release(layer, "g")
        elif name.startswith("dz"):
            b = int(name[2])
            if b == 0:
                need(layer, "dz")
                weights(base).wait()
            ffn_back_block(dob, wv.at[base % 2], dz, dz, sl, b)
            if b == 3:
                next_weights(base)
        elif name == "ht":
            need(layer, "n1", "r1")
            hb[...] = (n1[...].astype(F32) * vl[0:1, :] + vl[5:6, :]).astype(BF)
            transpose_into(hb, at)
        elif name[0] == "e":
            pair = int(name[1])
            if pair == 0 and base >= 3:
                red.drain(base - 2)
            for b in range(4):
                blocks_pair((base + 1) % 3, b, pair, dz[b])
            for zz in (2 * pair, 2 * pair + 1):
                red.core_send(base + 1, zz)
        elif name == "dh":
            weights(base + 1).wait()
            ffn_back_input(dz, wv.at[(base + 1) % 2], du)
            release(layer, "dz")
            next_weights(base + 1)
        elif name == "ln1":
            norm_backward(du, n1, r1, vl[0:1, :], du, dob, sl, (0, 5, 4))
            release(layer, "n1", "r1")
        elif name == "o":
            need(layer, "ctx")
            weights(base + 2).wait()
            if base >= 3:
                red.drain(base - 1)
            transpose_into(ctx, at)
            for pair in range(2):
                blocks_pair((base + 2) % 3, 3, pair, dob[...])
            context_back(dob, wv.at[(base + 2) % 2, 3], hb)
            release(layer, "ctx")
        elif name == "xt":
            need(layer, "xb")
            transpose_into(xb, at)
            release(layer, "xb", "logsum")
        elif name[0] == "q":
            pair = int(name[1])
            for b in range(3):
                blocks_pair((base + 2) % 3, b, pair, dj[b])
            for zz in (2 * pair, 2 * pair + 1):
                red.core_send(base + 2, zz)
        elif name == "dx":
            input_back(dj, wv.at[(base + 2) % 2], du, du, sl)
            if layer == 0:
                grad_in[...] = du[...].astype(BF)
            release(layer, "dj")
            next_weights(base + 2)

    def event(name, t, zz):
        if name == "xy1":
            red.xy1(t, zz)
        elif name == "xy2":
            red.xy2(t, zz)
        elif name == "z":
            red.z_send(t, zz)
        elif name == "sum":
            red.total(t)
        elif name == "ag":
            red.share(t)
        elif name == "fin":
            red.finish(t)
        elif name == "stat":
            statistics(t)
        else:
            vec_event(zz)

    def vec_copy(src, dst, k, peer):
        return pltpu.make_async_remote_copy(
            src_ref=src, dst_ref=dst, send_sem=vec_sems.at[2 * k], recv_sem=vec_sems.at[2 * k + 1],
            device_id=peer, device_id_type=MESH,
        )

    hops = ((sums, red.sibling), (va.at[0], red.x_side), (va.at[1], red.y_side))

    def vec_event(k):
        if 1 <= k <= 3:
            src, peer = hops[k - 1]
            vec_copy(src, vr.at[k - 1], k - 1, peer).wait()
            va[k - 1] = src[...] + vr[k - 1]
        if k <= 2:
            src, peer = hops[k]
            vec_copy(src, vr.at[k], k, peer).start()
        elif k == 3:
            for j, peer in enumerate(red.planes):
                vec_copy(va.at[2], vr.at[3 + j], 3 + j, peer).start()
        else:
            for j, peer in enumerate(red.planes):
                vec_copy(va.at[2], vr.at[3 + j], 3 + j, peer).wait()
            vec_grads(plane_sum(va[2], [vr[3], vr[4], vr[5]]))

    def plane_sum(own, others):
        acc = jnp.zeros(own.shape, F32)
        for plane in range(4):
            part = jnp.where(z == plane, own, 0.0)
            for k in range(3):
                part = jnp.where((z + 3 - k) % 4 == plane, others[k], part)
            acc = acc + part
        return acc

    f = 2 * z + c

    def vec_grads(total):
        down = lax.broadcasted_iota(jnp.int32, (768, 128), 0)
        across = lax.broadcasted_iota(jnp.int32, (768, 128), 1)
        pick = jnp.where((down == across + 96 * f) & (across < 96), 1.0, 0.0).astype(F32)
        for layer in range(2):
            sums[layer] = total[layer] * ROOT_SCALE
            mine = lax.dot_general(
                sums[layer, 0:8, :], pick, (((1,), (0,)), ((), ())), precision=lax.Precision.HIGHEST, preferred_element_type=F32
            )
            vec_grad[layer] = jnp.zeros((16, 128), F32)
            vec_grad[layer, 0:8, :] = mine
            for k in range(3):
                part = jnp.zeros((1, 128), F32)
                for zz in range(4):
                    for cc in range(2):
                        here = sums[layer, 8 + zz : 9 + zz, 384 * cc + 128 * k : 384 * cc + 128 * k + 128]
                        part = jnp.where(f == 2 * zz + cc, here, part)
                vec_grad[layer, 8 + k : 9 + k, :] = part

    def all_sum(v):
        return jnp.sum(jnp.sum(v, axis=1, keepdims=True), axis=0, keepdims=True)

    lane = lax.broadcasted_iota(jnp.int32, (1, 768), 1)
    lane_c = lax.broadcasted_iota(jnp.int32, (128, 128), 1)

    def row_column(layer, chunk):
        return row_cols[:, 6 * layer + chunk : 6 * layer + chunk + 1]

    def set_row_column(layer, chunk, value):
        if value.shape[0] < 128:
            value = jnp.concatenate([value, jnp.zeros((128 - value.shape[0], 1), F32)], axis=0)
        row_cols[...] = jnp.where(lane_c == 6 * layer + chunk, value, row_cols[...])

    def squared(t, b):
        v = fin[t, b].astype(F32) * ROOT_SCALE
        return v * v

    def put_scalar(layer, index, value):
        pay[layer, 18:19, :] = jnp.where(lane == index, value, pay[layer, 18:19, :])

    def row_sums(sq):
        return jnp.sum(sq + FLOOR_SQUARE, axis=1, keepdims=True)

    def column_sums(sq):
        return jnp.sum(sq + FLOOR_SQUARE, axis=0, keepdims=True)

    def statistics(t):
        layer, kind = 1 - t // 3, (2, 1, 0)[t % 3]
        if kind == 2:
            sums_of = jnp.concatenate([row_sums(squared(t, b)) for b in range(4)], axis=0)
            old = jnp.concatenate([row_column(layer, 3 + k) for k in range(3)], axis=0)
            new = DECAY_RATE * old + (1.0 - DECAY_RATE) * (sums_of / 768.0)
            for k in range(3):
                set_row_column(layer, 3 + k, new[128 * k : 128 * k + 128])
            col, quo = jnp.zeros((1, 768), F32), jnp.zeros((1, 768), F32)
            for b in range(4):
                sq = squared(t, b)
                col = col + column_sums(sq)
                quo = quo + jnp.sum(sq / new[96 * b : 96 * b + 96], axis=0, keepdims=True)
            pay[layer, 8:9, :] = col
            pay[layer, 17:18, :] = quo
            put_scalar(layer, 3, jnp.sum(new, axis=0, keepdims=True))
            return
        sets = (((0, 1, 2), 0, 0, 0), ((3,), 1, 3, 1)) if kind == 0 else (((0, 1, 2, 3), 2, 4, 2),)
        for blocks, chunk, first, index in sets:
            sums_of = jnp.zeros((96, 1), F32)
            for b in blocks:
                sums_of = sums_of + row_sums(squared(t, b))
            old = row_column(layer, chunk)[0:96]
            new = DECAY_RATE * old + (1.0 - DECAY_RATE) * (sums_of / (768.0 * len(blocks)))
            set_row_column(layer, chunk, new)
            for k, b in enumerate(blocks):
                sq = squared(t, b)
                pay[layer, first + k : first + k + 1, :] = column_sums(sq)
                pay[layer, 9 + first + k : 10 + first + k, :] = jnp.sum(sq / new, axis=0, keepdims=True)
            put_scalar(layer, index, jnp.sum(new, axis=0, keepdims=True))

    def vec_moments(layer):
        grad = vec_grad[layer]
        return DECAY_RATE * vec_old[layer] + (1.0 - DECAY_RATE) * (grad * grad + FLOOR_SQUARE)

    def exchange_statistics():
        for layer in range(2):
            for m in range(4):
                put_scalar(layer, 4 + m, all_sum(squares[4 * layer + m : 4 * layer + m + 1, :]))
            grad, now = vec_grad[layer], vec_now[layer]
            step = grad * grad / vec_moments(layer)
            for r in range(9):
                rows = slice(r, r + 1) if r < 8 else slice(8, 11)
                put_scalar(layer, 8 + r, all_sum(now[rows] * now[rows]))
                put_scalar(layer, 17 + r, all_sum(step[rows]))

        def copy(src, dst, k, peer):
            return pltpu.make_async_remote_copy(
                src_ref=src, dst_ref=dst, send_sem=pay_sems.at[2 * k], recv_sem=pay_sems.at[2 * k + 1],
                device_id=peer, device_id_type=MESH,
            )

        cp = copy(pay, pay_in, 0, red.sibling)
        cp.start()
        cp.wait()
        pay_z[3] = pay[c] + pay_in[c]
        copies = [copy(pay_z.at[3], pay_z.at[k], 1 + k, peer) for k, peer in enumerate(red.planes)]
        for cp in copies:
            cp.start()
        for cp in copies:
            cp.wait()
        pay_sum[c] = plane_sum(pay_z[3], [pay_z[0], pay_z[1], pay_z[2]])
        cp = copy(pay_sum.at[c], pay_sum.at[c], 4, red.sibling)
        cp.start()
        cp.wait()

    def finish_statistics():
        rows_new[...] = row_cols[...].T[0:16]
        for layer in range(2):
            scalars = pay_sum[layer, 18:19, :]
            pick = lambda index: scalars[:, index : index + 1]
            for m, (first, count, rows) in enumerate(((0, 3, 768.0), (3, 1, 768.0), (4, 4, 768.0), (8, 1, 3072.0))):
                new = DECAY_RATE * columns_old[layer, first : first + count, :] + (1.0 - DECAY_RATE) * (
                    pay_sum[layer, first : first + count, :] / rows
                )
                columns_new[layer, first : first + count, :] = new
                mean_rows = pick(m) / rows
                entries = rows * 768.0 * count
                energy = mean_rows * all_sum(pay_sum[layer, 9 + first : 9 + first + count, :] / new)
                clip = jnp.sqrt(energy / entries) / CLIP_LIMIT
                stride = STEP_RATE * jnp.maximum(FLOOR_SCALE, jnp.sqrt(pick(4 + m) / entries))
                column_scale[layer, first : first + count, :] = lax.rsqrt(new) * (
                    jnp.sqrt(mean_rows) * stride / jnp.maximum(clip, 1.0)
                )
            vec_scale[layer] = jnp.zeros((16, 128), F32)
            for r in range(9):
                entries = 768.0 if r < 8 else 3072.0
                clip = jnp.sqrt(pick(17 + r) / entries) / CLIP_LIMIT
                stride = STEP_RATE * jnp.maximum(FLOOR_SCALE, jnp.sqrt(pick(8 + r) / entries))
                value = stride / jnp.maximum(clip, 1.0)
                if r < 8:
                    vec_scale[layer, r : r + 1, :] = jnp.broadcast_to(value, (1, 128))
                else:
                    vec_scale[layer, 8:11, :] = jnp.broadcast_to(value, (3, 128))

    row_cols[...] = jnp.concatenate([rows_old[...], jnp.ones((112, 128), F32)], axis=0).T
    pay[...] = jnp.zeros_like(pay)

    order = backward_plan()
    pos = 0
    done_units = False
    while pos < len(order):
        item = order[pos]
        if item[0] != "run":
            event(*item)
            pos += 1
            continue
        _, layer, name = item
        if not name.startswith("att"):
            unit(layer, name)
            pos += 1
            continue
        hooks, look, p = {}, pos, 0
        while True:
            it = order[look]
            if it[0] == "run":
                if not it[2].startswith("att"):
                    break
                p = int(it[2][3:]) + 1
            else:
                hooks.setdefault(p, []).append(it)
            look += 1
        tail = hooks.pop(6, [])
        need(layer, "dj", "logsum")

        @pl.loop(0, PAIRS)
        def _(p):
            for at_pair, items in hooks.items():
                @pl.when(p == at_pair)
                def _():
                    for it in items:
                        event(*it)
            attend_backward_pair(p, dj, bias, logsum, hb, dj)

        for it in tail:
            event(*it)
        pos = look

    exchange_statistics()
    finish_statistics()
    for t in range(3, 6):
        red.drain(t)
    for t in range(6):
        red.drain_share(t)


def backward_call(cot, seg, vec, squares, rows_old, columns_old, vec_now, vec_old, tokens, x_saved, whole, j_s, c_s, l_s, n1_s, r1_s, g_s, gp_s, n2_s, r2_s):
    sd = jax.ShapeDtypeStruct
    any_spec = pl.BlockSpec(memory_space=pl.ANY)
    vm = pl.BlockSpec(memory_space=pltpu.VMEM)
    V = pltpu.VMEM
    dma = pltpu.SemaphoreType.DMA
    return pl.pallas_call(
        backward_kernel,
        out_shape=[
            sd((6, 4, 96, 768), BF), sd((T, D), BF), sd((16, 128), F32), sd((2, 9, 768), F32), sd((2, 9, 768), F32),
            sd((2, 16, 128), F32), sd((2, 16, 128), F32),
        ],
        in_specs=[vm] * 8 + [any_spec] * 12,
        out_specs=[vm] * 7,
        scratch_shapes=[
            V((3, 2, 2, 4, 2, 96, 768), BF),
            V((4, 2, 2, 96, 768), BF),
            V((4, 2, 48, 768), BF),
            V((4, 2, 48, 768), BF),
            V((4, 48, 768), BF),
            V((4, 48, 768), BF),
            V((6, 3, 96, 768), BF),
            V((2, 4, 768, 768), BF),
            V((4, T, D), BF),
            V((4, T, D), BF),
            V((3, T, D), BF),
            V((T, D), BF),
            V((T, D), BF),
            V((T, D), BF),
            V((T, 128), F32),
            V((T, 128), F32),
            V((6, 2, T), F32),
            V((T, D), BF),
            V((T, D), BF),
            V((D, T), BF),
            V((T, D), BF),
            V((T, T), F32),
            V((T, D), F32),
            V((2, 16, 768), F32),
            V((6, 2, 16, 768), F32),
            V((3, 2, 16, 768), F32),
            V((128, 128), F32),
            V((2, 24, 768), F32),
            V((2, 24, 768), F32),
            V((4, 24, 768), F32),
            V((2, 24, 768), F32),
            dma((24, 10)),
            dma((6, 10)),
            pltpu.SemaphoreType.REGULAR((5, 4)),
            dma((12,)),
            dma((12,)),
            dma((10,)),
        ],
        compiler_params=pltpu.CompilerParams(
            collective_id=1, has_side_effects=True, vmem_limit_bytes=63 << 20
        ),
        name="backward",
    )(cot, seg, vec, squares, rows_old, columns_old, vec_now, vec_old, tokens, x_saved, whole, j_s, c_s, l_s, n1_s, r1_s, g_s, gp_s, n2_s, r2_s)


def update_kernel(
    fin, rows_new, columns_new, column_scale, vec_grad, vec_scale, vec_now, vec_old, final, grad_in, joint_w, output_w, expand_w, shrink_w,
    *refs,
):
    outs, scratch = refs[:31], refs[31:]
    activations, input_gradient = outs[0], outs[1]
    grads, small_grads = outs[2:6], outs[6:9]
    nexts, small_nexts = outs[9:13], outs[13:16]
    copies = outs[16:20]
    row_outs, column_outs = outs[20:28:2], outs[21:28:2]
    small_moments = outs[28:31]
    masters = (joint_w, output_w, expand_w, shrink_w)
    wbuf, gbuf, nbuf, cbuf, pbuf, in_sems, out_sems, pass_sems = scratch
    inward = [
        pltpu.make_async_copy(final, pbuf.at[0], pass_sems.at[0]),
        pltpu.make_async_copy(grad_in, pbuf.at[1], pass_sems.at[1]),
    ]
    through = [
        pltpu.make_async_copy(pbuf.at[0], activations, pass_sems.at[2]),
        pltpu.make_async_copy(pbuf.at[1], input_gradient, pass_sems.at[3]),
    ]
    pieces = []
    for layer in range(2):
        for m, count in enumerate((3, 1, 4, 4)):
            for b in range(count):
                kind = (0, 0, 1, 2)[m]
                t = 3 * (1 - layer) + (2, 1, 0)[kind]
                pieces.append((layer, m, b, t, 3 if m == 1 else b))

    def part(ref, layer, m, b):
        if m == 1:
            return ref.at[layer]
        if m == 3:
            return ref.at[layer, pl.ds(96 * b, 96), :]
        return ref.at[layer, :, pl.ds(768 * b, 768)]

    loads = [
        pltpu.make_async_copy(part(masters[m], layer, m, b), wbuf.at[n], in_sems.at[n])
        for n, (layer, m, b, t, block) in enumerate(pieces)
    ]
    for cp in loads + inward:
        cp.start()
    columns = jnp.concatenate([lax.rsqrt(rows_new[...]), jnp.zeros((112, 128), F32)], axis=0).T
    stores = []
    for n, (layer, m, b, t, block) in enumerate(pieces):
        if n == 12:
            for before, cp in zip(inward, through):
                before.wait()
                cp.start()
        if m < 3:
            left = columns[0:96, 6 * layer + m : 6 * layer + m + 1]
        else:
            left = jnp.concatenate([columns[:, 6 * layer + 3 + k : 6 * layer + 4 + k] for k in range(3)], axis=0)
            left = left[96 * b : 96 * b + 96]
        j = (0, 3, 4, 8)[m] + (b if m != 3 else 0)
        grad = fin[t, block].astype(F32) * ROOT_SCALE
        loads[n].wait()
        new = wbuf[n] - grad * left * column_scale[layer, j : j + 1, :]
        gbuf[n] = grad
        nbuf[n] = new
        cbuf[n] = new.astype(BF)
        for k, (src, dst) in enumerate(((gbuf, grads[m]), (nbuf, nexts[m]), (cbuf, copies[m]))):
            cp = pltpu.make_async_copy(src.at[n], part(dst, layer, m, b), out_sems.at[n, k])
            cp.start()
            stores.append(cp)
    for layer in range(2):
        grad, now = vec_grad[layer], vec_now[layer]
        moments = DECAY_RATE * vec_old[layer] + (1.0 - DECAY_RATE) * (grad * grad + FLOOR_SQUARE)
        new = now - vec_scale[layer] * (grad * lax.rsqrt(moments))
        for out, value in zip((small_grads, small_nexts, small_moments), (grad, new, moments)):
            out[0][layer] = value[0:2, 0:96]
            out[1][layer] = value[2:8, 0:96]
            for k in range(3):
                out[2][layer : layer + 1, 128 * k : 128 * k + 128] = value[8 + k : 9 + k, :]
        for m in range(3):
            row_outs[m][layer : layer + 1, :] = rows_new[6 * layer + m : 6 * layer + m + 1, 0:96]
        for k in range(3):
            row_outs[3][layer : layer + 1, 128 * k : 128 * k + 128] = rows_new[6 * layer + 3 + k : 6 * layer + 4 + k, :]
        for m, (first, count) in enumerate(((0, 3), (3, 1), (4, 4), (8, 1))):
            for k in range(count):
                column_outs[m][layer : layer + 1, 768 * k : 768 * k + 768] = columns_new[layer, first + k : first + k + 1, :]
    for cp in stores + through:
        cp.wait()


def update_call(*args):
    sd = jax.ShapeDtypeStruct
    any_spec = pl.BlockSpec(memory_space=pl.ANY)
    vm = pl.BlockSpec(memory_space=pltpu.VMEM)
    V = pltpu.VMEM
    mats = ((2, 96, 2304), (2, 96, 768), (2, 96, 3072), (2, 384, 768))
    small = ((2, 2, 96), (2, 6, 96), (2, 384))
    stats = ((2, 96), (2, 2304), (2, 96), (2, 768), (2, 96), (2, 3072), (2, 384), (2, 768))
    shapes = (
        [sd((T, D), BF)] * 2 + [sd(s, F32) for s in mats] + [sd(s, F32) for s in small] + [sd(s, F32) for s in mats]
        + [sd(s, F32) for s in small] + [sd(s, BF) for s in mats] + [sd(s, F32) for s in stats] + [sd(s, F32) for s in small]
    )
    specs = [any_spec] * 6 + [vm] * 3 + [any_spec] * 4 + [vm] * 3 + [any_spec] * 4 + [vm] * 11
    return pl.pallas_call(
        update_kernel,
        out_shape=shapes,
        in_specs=[vm] * 8 + [any_spec] * 6,
        out_specs=specs,
        scratch_shapes=[
            V((24, 96, 768), F32),
            V((24, 96, 768), F32),
            V((24, 96, 768), F32),
            V((24, 96, 768), BF),
            V((2, T, D), BF),
            pltpu.SemaphoreType.DMA((24,)),
            pltpu.SemaphoreType.DMA((24, 3)),
            pltpu.SemaphoreType.DMA((4,)),
        ],
        compiler_params=pltpu.CompilerParams(vmem_limit_bytes=56 << 20),
        name="update",
    )(*args)


def local_kernels(
    tokens,
    segments,
    cotangent,
    joint_weight,
    output_weight,
    expand_weight,
    shrink_weight,
    norm_gains,
    biases,
    hidden_bias,
    joint_rows,
    joint_columns,
    output_rows,
    output_columns,
    expand_rows,
    expand_columns,
    shrink_rows,
    shrink_columns,
    gain_moments,
    bias_moments,
    hidden_moments,
):
    row_count, slot_count, features = tokens.shape
    vecs = pack_vectors(norm_gains, biases, hidden_bias)
    (whole, vec, x_saved, j_s, c_s, l_s, n1_s, r1_s, g_s, gp_s, n2_s, r2_s, final, squares) = forward_call(
        tokens[0], segments, vecs, joint_weight, output_weight, expand_weight, shrink_weight
    )
    old = pack_vectors(gain_moments, bias_moments, hidden_moments, 1.0)
    rows_old = pack_rows(joint_rows, output_rows, expand_rows, shrink_rows)
    columns_old = jnp.concatenate([joint_columns, output_columns, expand_columns, shrink_columns], axis=1).reshape(2, 9, 768)
    blocks, grad_in, rows_new, columns_new, column_scale, vec_grad, vec_scale = backward_call(
        cotangent[0], segments, vec, squares, rows_old, columns_old, vecs, old,
        tokens[0], x_saved, whole, j_s, c_s, l_s, n1_s, r1_s, g_s, gp_s, n2_s, r2_s
    )
    outs = update_call(
        blocks, rows_new, columns_new, column_scale, vec_grad, vec_scale, vecs, old, final, grad_in,
        joint_weight, output_weight, expand_weight, shrink_weight
    )
    return (outs[0][None], outs[1][None]) + tuple(outs[2:])


def solution(mesh):
    placed = (
        P(("dp", "fsdp"), None, None),
        P(("dp", "fsdp"), None),
        P(("dp", "fsdp"), None, None),
        P(None, "fsdp", None),
        P(None, "fsdp", None),
        P(None, "fsdp", None),
        P(None, "fsdp", None),
        P(None, None, "fsdp"),
        P(None, None, "fsdp"),
        P(None, "fsdp"),
        P(None, "fsdp"),
        P(),
        P(None, "fsdp"),
        P(),
        P(None, "fsdp"),
        P(),
        P(None, "fsdp"),
        P(),
        P(None, None, "fsdp"),
        P(None, None, "fsdp"),
        P(None, "fsdp"),
    )
    known = dict(mesh.shape) == {"dp": 4, "fsdp": 8}
    return jax.shard_map(
        local_kernels if known else local_plain,
        mesh=mesh,
        in_specs=placed,
        out_specs=(
            P(("dp", "fsdp"), None, None),
            P(("dp", "fsdp"), None, None),
            P(None, "fsdp", None),
            P(None, "fsdp", None),
            P(None, "fsdp", None),
            P(None, "fsdp", None),
            P(None, None, "fsdp"),
            P(None, None, "fsdp"),
            P(None, "fsdp"),
            P(None, "fsdp", None),
            P(None, "fsdp", None),
            P(None, "fsdp", None),
            P(None, "fsdp", None),
            P(None, None, "fsdp"),
            P(None, None, "fsdp"),
            P(None, "fsdp"),
            P(None, "fsdp", None),
            P(None, "fsdp", None),
            P(None, "fsdp", None),
            P(None, "fsdp", None),
            P(None, "fsdp"),
            P(),
            P(None, "fsdp"),
            P(),
            P(None, "fsdp"),
            P(),
            P(None, "fsdp"),
            P(),
            P(None, None, "fsdp"),
            P(None, None, "fsdp"),
            P(None, "fsdp"),
        ),
        check_vma=False,
    )
```

```python
from functools import partial
import math

import jax
import jax.numpy as jnp
from jax import lax
from jax.sharding import PartitionSpec as P
from jax.experimental import pallas as pl
from jax.experimental.pallas import tpu as pltpu

HEADS = 12
HEAD_SIZE = 64


NORM_EPSILON = 1e-12
SCORE_SCALE = 0.125
MASK_VALUE = -1e30
FLOOR_SQUARE = 1e-30
FLOOR_SCALE = 0.001
DECAY_RATE = 0.5
CLIP_LIMIT = 0.25
STEP_RATE = 4.0


def product(left, right):
    return jnp.dot(left, right, preferred_element_type=jnp.float32)


def product_left(left, right):
    return lax.dot_general(
        left, right, (((0,), (0,)), ((), ())), preferred_element_type=jnp.float32
    )


def product_right(left, right):
    return lax.dot_general(
        left, right, (((1,), (1,)), ((), ())), preferred_element_type=jnp.float32
    )


def normalize(values):
    average = jnp.mean(values, axis=-1, keepdims=True)
    centered = values - average
    variance = jnp.mean(centered * centered, axis=-1, keepdims=True)
    inverse = lax.rsqrt(variance + NORM_EPSILON)
    return (centered * inverse, inverse)


def normalize_back(grad_scaled, scaled, inverse):
    first_mean = jnp.mean(grad_scaled, axis=-1, keepdims=True)
    second_mean = jnp.mean(grad_scaled * scaled, axis=-1, keepdims=True)
    return inverse * (grad_scaled - first_mean - scaled * second_mean)


def split_heads(joint_row):
    slot_count = joint_row.shape[0]
    shaped = joint_row.reshape(slot_count, 3, HEADS, HEAD_SIZE)
    return (shaped[:, 0], shaped[:, 1], shaped[:, 2])


def masked_scores(query_rows, key_rows, segment_row):
    scores = (
        jnp.einsum("qhe,khe->hqk", query_rows, key_rows, preferred_element_type=jnp.float32)
        * SCORE_SCALE
    )
    allowed = segment_row[:, None] == segment_row[None, :]
    return jnp.where(allowed[None], scores, MASK_VALUE)


def attend_forward(packed):
    joint_row, segment_row = packed
    query_rows, key_rows, value_rows = split_heads(joint_row)
    scores = masked_scores(query_rows, key_rows, segment_row)
    highest = jnp.max(scores, axis=-1, keepdims=True)
    raised = jnp.exp(scores - highest)
    denominator = jnp.sum(raised, axis=-1, keepdims=True)
    weights = (raised / denominator).astype(jnp.bfloat16)
    context = jnp.einsum("hqk,khe->qhe", weights, value_rows, preferred_element_type=jnp.float32)
    logsum = (highest + jnp.log(denominator))[:, :, 0]
    return (context.astype(jnp.bfloat16).reshape(joint_row.shape[0], HEADS * HEAD_SIZE), logsum)


def attend_backward(packed):
    joint_row, segment_row, logsum, grad_row = packed
    slot_count = joint_row.shape[0]
    query_rows, key_rows, value_rows = split_heads(joint_row)
    scores = masked_scores(query_rows, key_rows, segment_row)
    probabilities = jnp.exp(scores - logsum[:, :, None])
    upstream = grad_row.reshape(slot_count, HEADS, HEAD_SIZE)
    grad_probs = jnp.einsum(
        "qhe,khe->hqk", upstream, value_rows, preferred_element_type=jnp.float32
    )
    row_delta = jnp.sum(probabilities * grad_probs, axis=-1, keepdims=True)
    grad_scores = (probabilities * (grad_probs - row_delta)).astype(jnp.bfloat16)
    grad_query = (
        jnp.einsum("hqk,khe->qhe", grad_scores, key_rows, preferred_element_type=jnp.float32)
        * SCORE_SCALE
    )
    grad_key = (
        jnp.einsum("hqk,qhe->khe", grad_scores, query_rows, preferred_element_type=jnp.float32)
        * SCORE_SCALE
    )
    grad_value = jnp.einsum(
        "hqk,qhe->khe",
        probabilities.astype(jnp.bfloat16),
        upstream,
        preferred_element_type=jnp.float32,
    )
    stacked = jnp.stack([grad_query, grad_key, grad_value], axis=1)
    return stacked.reshape(slot_count, 3 * HEADS * HEAD_SIZE).astype(jnp.bfloat16)


def block_forward(hidden_in, segments, weights):
    joint_matrix, output_matrix, expand_matrix, shrink_matrix, gain_rows, bias_rows, inner_bias = (
        weights
    )
    gain_values = gain_rows.astype(jnp.float32)
    bias_values = bias_rows.astype(jnp.float32)
    row_count, slot_count = segments.shape
    zero_block = jnp.zeros_like(bias_values[0])
    joint_bias = jnp.concatenate([bias_values[0], zero_block, bias_values[1]])
    joint_out = (product(hidden_in.astype(jnp.bfloat16), joint_matrix) + joint_bias).astype(
        jnp.bfloat16
    )
    context, logsum = lax.map(
        attend_forward, (joint_out.reshape(row_count, slot_count, -1), segments)
    )
    context = context.reshape(row_count * slot_count, -1)
    attended = product(context, output_matrix) + bias_values[2]
    first_scaled, first_inverse = normalize(hidden_in + attended)
    first_norm = first_scaled * gain_values[0] + bias_values[3]
    pre_active = product(first_norm.astype(jnp.bfloat16), expand_matrix) + inner_bias.astype(
        jnp.float32
    )
    active = jax.nn.gelu(pre_active, approximate=False).astype(jnp.bfloat16)
    branch = product(active, shrink_matrix) + bias_values[4]
    second_scaled, second_inverse = normalize(first_norm + branch)
    result = second_scaled * gain_values[1] + bias_values[5]
    stored = (
        hidden_in,
        joint_out,
        context,
        logsum,
        first_scaled,
        first_inverse,
        pre_active,
        second_scaled,
        second_inverse,
    )
    return (result, stored)


def block_backward(grad_out, segments, weights, stored):
    joint_matrix, output_matrix, expand_matrix, shrink_matrix, gain_rows, bias_rows, inner_bias = (
        weights
    )
    (
        hidden_in,
        joint_out,
        context,
        logsum,
        first_scaled,
        first_inverse,
        pre_active,
        second_scaled,
        second_inverse,
    ) = stored
    gain_values = gain_rows.astype(jnp.float32)
    bias_values = bias_rows.astype(jnp.float32)
    row_count, slot_count = segments.shape
    features = hidden_in.shape[1]
    grad_second_bias = jnp.sum(grad_out, axis=0)
    grad_second_gain = jnp.sum(grad_out * second_scaled, axis=0)
    grad_sum = normalize_back(grad_out * gain_values[1], second_scaled, second_inverse)
    grad_branch = grad_sum.astype(jnp.bfloat16)
    active, gelu_back = jax.vjp(partial(jax.nn.gelu, approximate=False), pre_active)
    grad_shrink = product_left(active.astype(jnp.bfloat16), grad_branch)
    grad_active = product_right(grad_branch, shrink_matrix)
    grad_pre = gelu_back(grad_active)[0].astype(jnp.bfloat16)
    first_norm = first_scaled * gain_values[0] + bias_values[3]
    grad_expand = product_left(first_norm.astype(jnp.bfloat16), grad_pre)
    grad_first = grad_sum + product_right(grad_pre, expand_matrix)
    grad_first_bias = jnp.sum(grad_first, axis=0)
    grad_first_gain = jnp.sum(grad_first * first_scaled, axis=0)
    grad_middle = normalize_back(grad_first * gain_values[0], first_scaled, first_inverse)
    grad_attended = grad_middle.astype(jnp.bfloat16)
    grad_output = product_left(context, grad_attended)
    grad_context = product_right(grad_attended, output_matrix).astype(jnp.bfloat16)
    grad_joint_out = lax.map(
        attend_backward,
        (
            joint_out.reshape(row_count, slot_count, -1),
            segments,
            logsum,
            grad_context.reshape(row_count, slot_count, -1),
        ),
    )
    grad_joint_out = grad_joint_out.reshape(row_count * slot_count, -1)
    grad_joint = product_left(hidden_in.astype(jnp.bfloat16), grad_joint_out)
    grad_input = grad_middle + product_right(grad_joint_out, joint_matrix)
    joint_sums = jnp.sum(grad_joint_out, axis=0, dtype=jnp.float32)
    bias_grads = jnp.stack(
        [
            joint_sums[:features],
            joint_sums[2 * features :],
            jnp.sum(grad_attended, axis=0, dtype=jnp.float32),
            grad_first_bias,
            jnp.sum(grad_branch, axis=0, dtype=jnp.float32),
            grad_second_bias,
        ]
    )
    gain_grads = jnp.stack([grad_first_gain, grad_second_gain])
    inner_grad = jnp.sum(grad_pre, axis=0, dtype=jnp.float32)
    return (
        grad_input,
        (grad_joint, grad_output, grad_expand, grad_shrink, gain_grads, bias_grads, inner_grad),
    )


def factored_partials(gradient, weight, rows_old):
    squared = gradient * gradient + FLOOR_SQUARE
    rows_next = DECAY_RATE * rows_old + (1.0 - DECAY_RATE) * jnp.mean(squared, axis=2)
    return (
        rows_next,
        jnp.sum(squared, axis=1),
        jnp.sum(rows_next, axis=1),
        jnp.sum(weight * weight, axis=(1, 2)),
    )


def vector_partials(gradient, moments_old):
    moments_next = DECAY_RATE * moments_old + (1.0 - DECAY_RATE) * (
        gradient * gradient + FLOOR_SQUARE
    )
    return (moments_next, gradient * lax.rsqrt(moments_next))


def local_plain(
    tokens,
    segments,
    cotangent,
    joint_weight,
    output_weight,
    expand_weight,
    shrink_weight,
    norm_gains,
    biases,
    hidden_bias,
    joint_rows,
    joint_columns,
    output_rows,
    output_columns,
    expand_rows,
    expand_columns,
    shrink_rows,
    shrink_columns,
    gain_moments,
    bias_moments,
    hidden_moments,
):
    layers = joint_weight.shape[0]
    row_count, slot_count, features = tokens.shape
    hidden = tokens.astype(jnp.float32).reshape(row_count * slot_count, features)
    gathered_list = []
    stored_list = []
    for number in range(layers):
        weights = (
            lax.all_gather(joint_weight[number].astype(jnp.bfloat16), "fsdp", axis=0, tiled=True),
            lax.all_gather(output_weight[number].astype(jnp.bfloat16), "fsdp", axis=0, tiled=True),
            lax.all_gather(expand_weight[number].astype(jnp.bfloat16), "fsdp", axis=0, tiled=True),
            lax.all_gather(shrink_weight[number].astype(jnp.bfloat16), "fsdp", axis=0, tiled=True),
            lax.all_gather(norm_gains[number].astype(jnp.bfloat16), "fsdp", axis=1, tiled=True),
            lax.all_gather(biases[number].astype(jnp.bfloat16), "fsdp", axis=1, tiled=True),
            lax.all_gather(hidden_bias[number].astype(jnp.bfloat16), "fsdp", axis=0, tiled=True),
        )
        hidden, stored = block_forward(hidden, segments, weights)
        gathered_list.append(weights)
        stored_list.append(stored)
    activations = hidden.reshape(row_count, slot_count, features).astype(jnp.bfloat16)
    grad_hidden = cotangent.astype(jnp.float32).reshape(row_count * slot_count, features)
    collected = []
    for number in reversed(range(layers)):
        weights = (
            lax.all_gather(joint_weight[number].astype(jnp.bfloat16), "fsdp", axis=0, tiled=True),
            lax.all_gather(output_weight[number].astype(jnp.bfloat16), "fsdp", axis=0, tiled=True),
            lax.all_gather(expand_weight[number].astype(jnp.bfloat16), "fsdp", axis=0, tiled=True),
            lax.all_gather(shrink_weight[number].astype(jnp.bfloat16), "fsdp", axis=0, tiled=True),
            lax.all_gather(norm_gains[number].astype(jnp.bfloat16), "fsdp", axis=1, tiled=True),
            lax.all_gather(biases[number].astype(jnp.bfloat16), "fsdp", axis=1, tiled=True),
            lax.all_gather(hidden_bias[number].astype(jnp.bfloat16), "fsdp", axis=0, tiled=True),
        )
        grad_hidden, local_grads = block_backward(
            grad_hidden, segments, weights, stored_list[number]
        )
        grad_joint, grad_output, grad_expand, grad_shrink, gain_grads, bias_grads, inner_grad = (
            local_grads
        )
        shards = (
            lax.psum_scatter(grad_joint, "fsdp", scatter_dimension=0, tiled=True),
            lax.psum_scatter(grad_output, "fsdp", scatter_dimension=0, tiled=True),
            lax.psum_scatter(grad_expand, "fsdp", scatter_dimension=0, tiled=True),
            lax.psum_scatter(grad_shrink, "fsdp", scatter_dimension=0, tiled=True),
            lax.psum_scatter(gain_grads, "fsdp", scatter_dimension=1, tiled=True),
            lax.psum_scatter(bias_grads, "fsdp", scatter_dimension=1, tiled=True),
            lax.psum_scatter(inner_grad, "fsdp", scatter_dimension=0, tiled=True),
        )
        summed = (
            lax.psum(shards[0].astype(jnp.bfloat16), "dp").astype(jnp.float32),
            lax.psum(shards[1].astype(jnp.bfloat16), "dp").astype(jnp.float32),
            lax.psum(shards[2].astype(jnp.bfloat16), "dp").astype(jnp.float32),
            lax.psum(shards[3].astype(jnp.bfloat16), "dp").astype(jnp.float32),
            lax.psum(shards[4].astype(jnp.bfloat16), "dp").astype(jnp.float32),
            lax.psum(shards[5].astype(jnp.bfloat16), "dp").astype(jnp.float32),
            lax.psum(shards[6].astype(jnp.bfloat16), "dp").astype(jnp.float32),
        )
        collected.append(summed)
    collected = collected[::-1]
    input_gradient = grad_hidden.reshape(row_count, slot_count, features).astype(jnp.bfloat16)
    fsdp_count = lax.axis_size("fsdp")
    token_total = row_count * slot_count * lax.axis_size("dp") * fsdp_count
    root_scale = 1.0 / math.sqrt(token_total)
    stacked_grads = [
        jnp.stack([entry[index] for entry in collected]) * root_scale for index in range(7)
    ]
    matrices = (
        (stacked_grads[0], joint_weight, joint_rows, joint_columns),
        (stacked_grads[1], output_weight, output_rows, output_columns),
        (stacked_grads[2], expand_weight, expand_rows, expand_columns),
        (stacked_grads[3], shrink_weight, shrink_rows, shrink_columns),
    )
    partial_list = [factored_partials(item[0], item[1], item[2]) for item in matrices]
    vectors = (
        (stacked_grads[4], norm_gains, gain_moments),
        (stacked_grads[5], biases, bias_moments),
        (stacked_grads[6][:, None, :], hidden_bias[:, None, :], hidden_moments[:, None, :]),
    )
    vector_list = [vector_partials(item[0], item[2]) for item in vectors]
    vector_squares = jnp.concatenate(
        [jnp.sum(item[1] * item[1], axis=2) for item in vectors], axis=1
    )
    statistics = lax.psum(
        (
            partial_list[0][1],
            partial_list[1][1],
            partial_list[2][1],
            partial_list[3][1],
            jnp.stack([item[2] for item in partial_list], axis=1),
            jnp.stack([item[3] for item in partial_list], axis=1),
            vector_squares,
        ),
        "fsdp",
    )
    updates = []
    columns_list = []
    for index in range(4):
        gradient = matrices[index][0]
        total_rows = gradient.shape[1] * fsdp_count
        rows_next = partial_list[index][0]
        columns_next = DECAY_RATE * matrices[index][3] + (1.0 - DECAY_RATE) * (
            statistics[index] / total_rows
        )
        row_average = statistics[4][:, index] / total_rows
        estimate = rows_next[:, :, None] * columns_next[:, None, :] / row_average[:, None, None]
        updates.append(gradient * lax.rsqrt(estimate))
        columns_list.append(columns_next)
    matrix_squares = jnp.stack([jnp.sum(item * item, axis=(1, 2)) for item in updates], axis=1)
    vector_updates = jnp.concatenate(
        [jnp.sum(item[1] * item[1], axis=2) for item in vector_list], axis=1
    )
    norms = lax.psum((matrix_squares, vector_updates), "fsdp")
    matrix_next = []
    for index in range(4):
        gradient = matrices[index][0]
        entry_count = gradient.shape[1] * fsdp_count * gradient.shape[2]
        clip_ratio = jnp.sqrt(norms[0][:, index] / entry_count) / CLIP_LIMIT
        update = updates[index] / jnp.maximum(clip_ratio, 1.0)[:, None, None]
        stride = STEP_RATE * jnp.maximum(
            FLOOR_SCALE, jnp.sqrt(statistics[5][:, index] / entry_count)
        )
        matrix_next.append(matrices[index][1] - stride[:, None, None] * update)
    vector_next = []
    offset = 0
    for index in range(3):
        gradient = vectors[index][0]
        kinds = gradient.shape[1]
        entry_count = gradient.shape[2] * fsdp_count
        clip_ratio = jnp.sqrt(norms[1][:, offset : offset + kinds] / entry_count) / CLIP_LIMIT
        update = vector_list[index][1] / jnp.maximum(clip_ratio, 1.0)[:, :, None]
        stride = STEP_RATE * jnp.maximum(
            FLOOR_SCALE, jnp.sqrt(statistics[6][:, offset : offset + kinds] / entry_count)
        )
        vector_next.append(vectors[index][1] - stride[:, :, None] * update)
        offset = offset + kinds
    return (
        activations,
        input_gradient,
        stacked_grads[0],
        stacked_grads[1],
        stacked_grads[2],
        stacked_grads[3],
        stacked_grads[4],
        stacked_grads[5],
        stacked_grads[6],
        matrix_next[0],
        matrix_next[1],
        matrix_next[2],
        matrix_next[3],
        vector_next[0],
        vector_next[1],
        vector_next[2][:, 0, :],
        matrix_next[0].astype(jnp.bfloat16),
        matrix_next[1].astype(jnp.bfloat16),
        matrix_next[2].astype(jnp.bfloat16),
        matrix_next[3].astype(jnp.bfloat16),
        partial_list[0][0],
        columns_list[0],
        partial_list[1][0],
        columns_list[1],
        partial_list[2][0],
        columns_list[2],
        partial_list[3][0],
        columns_list[3],
        vector_list[0][0],
        vector_list[1][0],
        vector_list[2][0][:, 0, :],
    )


F32 = jnp.float32
BF = jnp.bfloat16
T = 512
D = 768


def nn(a, b):
    return lax.dot_general(a, b, (((1,), (0,)), ((), ())), preferred_element_type=F32)


def nt(a, b):
    return lax.dot_general(a, b, (((1,), (1,)), ((), ())), preferred_element_type=F32)


def rows_at(i, n):
    return pl.ds(pl.multiple_of(i * n, n), n)


def build_mask(seg_ref, bias_ref):
    row = seg_ref[...]
    wide = jnp.broadcast_to(row, (128, T)).T
    for j in range(T // 128):
        bias_ref[:, j * 128 : (j + 1) * 128] = jnp.where(
            wide == row[:, j * 128 : (j + 1) * 128], 0.0, MASK_VALUE
        ).astype(F32)


def joint_forward(xb, wa, vec, joint, tile=T):
    for b in range(3):
        @pl.loop(0, T // tile)
        def _(i, b=b):
            r = rows_at(i, tile)
            out = nn(xb[r, :], wa[b])
            if b == 0:
                out = out + vec[2:3, :]
            if b == 2:
                out = out + vec[3:4, :]
            joint[b, r, :] = out.astype(BF)


def head_masks():
    lane = lax.broadcasted_iota(jnp.int32, (1, 128), 1)
    return [
        jnp.where(lane < 64, 1.0, 0.0).astype(F32),
        jnp.where(lane >= 64, 1.0, 0.0).astype(F32),
    ]


def attend_forward_pair(p, joint, bias, ctx, logsum):
    lanes = pl.ds(pl.multiple_of(p * 128, 128), 128)
    masks = head_masks()
    q2 = joint[0, :, lanes]
    k2 = joint[1, :, lanes]
    vt = joint[2, :, lanes].T
    outs, sums = [], []
    for h in range(2):
        qm = q2 * (masks[h] * 0.125).astype(BF)
        st = nt(k2, qm) + bias[...]
        top = jnp.max(st, axis=0, keepdims=True)
        e = jnp.exp(st - top)
        total = jnp.sum(e, axis=0, keepdims=True)
        ct = nn(vt[64 * h : 64 * h + 64, :], e.astype(BF))
        outs.append(ct * (1.0 / total))
        sums.append(top + jnp.log(total))
    ctx[:, lanes] = jnp.concatenate(outs, axis=0).T.astype(BF)
    logsum[p] = jnp.concatenate(sums, axis=0)


def norm_parts(u):
    avg = jnp.mean(u, axis=-1, keepdims=True)
    c = u - avg
    var = jnp.mean(c * c, axis=-1, keepdims=True)
    inv = lax.rsqrt(var + NORM_EPSILON)
    return c * inv, inv


def out_forward(ctx, x, wo, vec, n1, r1, h, hb, tile=T):
    @pl.loop(0, T // tile)
    def _(i):
        r = rows_at(i, tile)
        u = nn(ctx[r, :], wo[...]) + vec[4:5, :] + x[r, :].astype(F32)
        n, inv = norm_parts(u)
        y = n * vec[0:1, :] + vec[5:6, :]
        n1[r, :] = n.astype(n1.dtype)
        r1[r, :] = jnp.broadcast_to(inv, (tile, 128))
        h[r, :] = y
        hb[r, :] = y.astype(BF)


def gelu_parts(z):
    a = jnp.abs(z)
    e = jnp.exp(z * z * -0.5)
    t = 1.0 / (1.0 + 0.23164189 * a)
    poly = t * (
        0.127414796 + t * (-0.142248368 + t * (0.7107068705 + t * (-0.7265760135 + t * 0.5307027145)))
    )
    tail = poly * e
    cdf = jnp.where(z >= 0.0, 1.0 - tail, tail)
    return z * cdf, cdf + z * (e * 0.3989422804014327)


def ffn_up(hb, we, vec, g, gp, b, tile=T):
    @pl.loop(0, T // tile)
    def _(i):
        r = rows_at(i, tile)
        z = nn(hb[r, :], we[b]) + vec[8 + b : 9 + b, :]
        act, der = gelu_parts(z)
        g[b, r, :] = act.astype(BF)
        gp[b, r, :] = der.astype(BF)


def ffn_down(g, ws, vec, h, n2, r2, x_out, xb_out, tile=T):
    @pl.loop(0, T // tile)
    def _(i):
        r = rows_at(i, tile)
        u = h[r, :] + vec[6:7, :]
        for b in range(4):
            u = u + nn(g[b, r, :], ws[b])
        n, inv = norm_parts(u)
        y = n * vec[1:2, :] + vec[7:8, :]
        n2[r, :] = n.astype(n2.dtype)
        r2[r, :] = jnp.broadcast_to(inv, (tile, 128))
        if x_out is not None:
            x_out[r, :] = y
        xb_out[r, :] = y.astype(BF)


def sum8(v):
    return jnp.sum(v.reshape(v.shape[0] // 8, 8, v.shape[1]), axis=0)


def norm_backward(dy, n, r, gain_row, du, dub, sums, rows, tile=256):
    def step(i, carry):
        s = rows_at(i, tile)
        g = dy[s, :].astype(F32)
        nv = n[s, :].astype(F32)
        inv = r[s, 0:1]
        e = g * gain_row
        m1 = jnp.mean(e, axis=-1, keepdims=True)
        m2 = jnp.mean(e * nv, axis=-1, keepdims=True)
        d = inv * (e - m1 - nv * m2)
        db = d.astype(BF)
        du[s, :] = d
        dub[s, :] = db
        return (
            carry[0] + sum8(g * nv),
            carry[1] + sum8(g),
            carry[2] + sum8(db.astype(F32)),
        )

    zero = jnp.zeros((8, D), F32)
    out = lax.fori_loop(0, T // tile, step, (zero, zero, zero))
    for k in range(3):
        sums[rows[k] : rows[k] + 1, :] = jnp.sum(out[k], axis=0, keepdims=True)


def transpose_into(src, dst, tile=128):
    @pl.loop(0, T // tile)
    def _(i):
        dst[:, rows_at(i, tile)] = src[rows_at(i, tile), :].T


def weight_grad(at, bmat, out, tile=256):
    @pl.loop(0, D // tile)
    def _(i):
        r = rows_at(i, tile)
        out[r, :] = nn(at[r, :], bmat[...]).astype(BF)


def ffn_back_block(dob, ws, gp, dz, sums, b, tile=T):
    def step(i, acc):
        r = rows_at(i, tile)
        v = (nt(dob[r, :], ws[b]) * gp[b, r, :].astype(F32)).astype(BF)
        dz[b, r, :] = v
        return acc + sum8(v.astype(F32))

    acc = lax.fori_loop(0, T // tile, step, jnp.zeros((8, D), F32))
    sums[8 + b : 9 + b, :] = jnp.sum(acc, axis=0, keepdims=True)


def ffn_back_input(dz, we, du, tile=T):
    @pl.loop(0, T // tile)
    def _(i):
        r = rows_at(i, tile)
        u = du[r, :]
        for b in range(4):
            u = u + nt(dz[b, r, :], we[b])
        du[r, :] = u


def context_back(dab, wo, dc, tile=T):
    @pl.loop(0, T // tile)
    def _(i):
        r = rows_at(i, tile)
        dc[r, :] = nt(dab[r, :], wo[...]).astype(BF)


def attend_backward_pair(p, joint, bias, logsum, ctx, dc, dj):
    lanes = pl.ds(pl.multiple_of(p * 128, 128), 128)
    masks = head_masks()
    q2 = joint[0, :, lanes]
    k2 = joint[1, :, lanes]
    v2 = joint[2, :, lanes]
    d2 = dc[:, lanes]
    kt = k2.T
    ls = logsum[p]
    both = d2.astype(F32) * ctx[:, lanes].astype(F32)
    high = both.astype(BF)
    low = (both - high.astype(F32)).astype(BF)
    pick = jnp.concatenate(masks + [jnp.zeros((6, 128), F32)], axis=0).astype(BF)
    delta = nt(pick, high) + nt(pick, low)
    dk = jnp.zeros((T, 128), F32)
    dv = jnp.zeros((T, 128), F32)
    dqt = []
    for h in range(2):
        qm = q2 * (masks[h] * 0.125).astype(BF)
        dm = d2 * masks[h].astype(BF)
        prob = jnp.exp(nt(k2, qm) + bias[...] - ls[h : h + 1, :])
        ds = (prob * (nt(v2, dm) - delta[h : h + 1, :])).astype(BF)
        dv = dv + nn(prob.astype(BF), dm)
        dk = dk + nn(ds, qm)
        dqt.append(nn(kt[64 * h : 64 * h + 64, :], ds))
    dj[0, :, lanes] = (jnp.concatenate(dqt, axis=0) * 0.125).T.astype(BF)
    dj[1, :, lanes] = dk.astype(BF)
    dj[2, :, lanes] = dv.astype(BF)


def input_back(dj, wa, du, dx, sums, tile=T):
    def step(i, carry):
        r = rows_at(i, tile)
        u = du[r, :]
        for b in range(3):
            u = u + nt(dj[b, r, :], wa[b])
        dx[r, :] = u.astype(dx.dtype)
        return (carry[0] + sum8(dj[0, r, :].astype(F32)), carry[1] + sum8(dj[2, r, :].astype(F32)))

    zero = jnp.zeros((8, D), F32)
    out = lax.fori_loop(0, T // tile, step, (zero, zero))
    sums[2:3, :] = jnp.sum(out[0], axis=0, keepdims=True)
    sums[3:4, :] = jnp.sum(out[1], axis=0, keepdims=True)


MESH = pl.DeviceIdType.MESH
PAIRS = 6
PIECE = 96
GROUPS = 6


def place():
    q = lax.axis_index("dp")
    f = lax.axis_index("fsdp")
    z = f // 2
    c = f % 2
    x_side = (q + 1 - 2 * (q % 2), f)
    y_side = ((q + 2) % 4, f)
    sibling = (q, f + 1 - 2 * c)
    planes = [(q, (f + 2 * k) % 8) for k in range(1, 4)]
    return q, z, c, x_side, y_side, sibling, planes


def greet(peers):
    barrier = pltpu.get_barrier_semaphore()
    for peer in peers:
        pl.semaphore_signal(barrier, inc=1, device_id=peer, device_id_type=MESH)
    pl.semaphore_wait(barrier, len(peers))


def hidden_piece(kind, b, zz, c, first, count):
    if kind < 2:
        start = 192 * zz + 96 * c + first
        return b, pl.ds(pl.multiple_of(start, 16), count)
    start = 384 * c + 96 * b + first
    return zz, pl.ds(pl.multiple_of(start, 16), count)


PARTS = [(g, first, 32) for g in range(6) for first in (0, 32, 64)]


class Gather:
    def __init__(self, whole, sbuf, sems):
        self.whole, self.sbuf, self.sems = whole, sbuf, sems
        q, z, c, self.x_side, self.y_side, self.sibling, self.planes = place()
        self.q, self.z, self.c = q, z, c
        self.qx = q + 1 - 2 * (q % 2)
        self.qy = (q + 2) % 4
        self.qd = (self.qx + 2) % 4
        self.others = [(z + k) % 4 for k in range(1, 4)]

    def spot(self, k, b, zz, cols=None):
        g, first, count = PARTS[k]
        lead, rows = hidden_piece(g % 3, b, zz, self.c, first, count)
        if cols is None:
            return self.whole.at[g, lead, rows, :]
        return self.whole.at[g, lead, rows, pl.ds(384 * cols, 384)]

    def send(self, k, src, dst, slot, peer):
        pltpu.make_async_remote_copy(
            src_ref=src, dst_ref=dst, send_sem=self.sems.at[k, slot], recv_sem=self.sems.at[k, slot + 1],
            device_id=peer, device_id_type=MESH,
        ).start()

    def total(self, k, slot, rows, cols=768):
        lead = self.whole.at[0, 0, pl.ds(0, rows), pl.ds(0, cols)] if rows <= 768 else self.whole.at[0, pl.ds(0, rows // 768)]
        pltpu.make_async_copy(lead, lead, self.sems.at[k, slot]).wait()

    def z_send(self, k):
        g, first, count = PARTS[k]
        src = self.sbuf.at[g, self.q, pl.ds(first, count), :]
        for peer in self.planes:
            self.send(k, src, self.spot(k, self.q, self.z), 0, peer)
        for b in range(4):
            mine = self.sbuf.at[g, b, pl.ds(first, count), :]
            self.send(k, mine, self.spot(k, b, self.z), 10, self.sibling)
            pltpu.make_async_copy(mine, self.spot(k, b, self.z), self.sems.at[k, 12]).start()

    def xy_send(self, k):
        count = PARTS[k][2]
        self.total(k, 1, 3 * count)
        for zz in self.others:
            spot = self.spot(k, self.q, zz)
            self.send(k, spot, spot, 2, self.x_side)
            self.send(k, spot, spot, 4, self.y_side)
        for zz in self.others:
            spot = self.spot(k, self.q, zz)
            self.send(k, spot, spot, 10, self.sibling)

    def diagonal_send(self, k):
        count = PARTS[k][2]
        self.total(k, 3, 3 * count)
        self.total(k, 5, 3 * count)
        for zz in self.others:
            spot = self.spot(k, self.qy, zz, 0)
            self.send(k, spot, spot, 6, self.x_side)
            spot = self.spot(k, self.qx, zz, 1)
            self.send(k, spot, spot, 8, self.y_side)
        for zz in self.others:
            for b in (self.qx, self.qy):
                spot = self.spot(k, b, zz)
                self.send(k, spot, spot, 10, self.sibling)

    def last_send(self, k):
        count = PARTS[k][2]
        self.total(k, 7, 3 * count, 384)
        self.total(k, 9, 3 * count, 384)
        for zz in self.others:
            spot = self.spot(k, self.qd, zz)
            self.send(k, spot, spot, 10, self.sibling)

    def finish(self, k):
        count = PARTS[k][2]
        self.total(k, 11, 16 * count)
        self.total(k, 12, 4 * count)

    def drain(self, k):
        count = PARTS[k][2]
        self.total(k, 0, 3 * count)
        self.total(k, 2, 3 * count)
        self.total(k, 4, 3 * count)
        self.total(k, 6, 3 * count, 384)
        self.total(k, 8, 3 * count, 384)
        self.total(k, 10, 16 * count)


UNIT_TIMES = (("joint", 2.1),) + tuple((f"att{p}", 1.3) for p in range(6)) + (("out", 1.0),) + tuple(
    (f"up{b}", 1.0) for b in range(4)
) + (("down", 2.8),)


SPREAD = 0.7


def pack_vectors(ref, gains, biases, hidden, fill):
    ref[...] = jnp.full(ref.shape, fill, F32)
    for layer in range(2):
        ref[layer, 0:2, 0:96] = gains[layer]
        for r in range(6):
            ref[layer, 2 + r : 3 + r, 0:96] = biases[r, layer : layer + 1, :]
        for k in range(3):
            ref[layer, 8 + k : 9 + k, :] = hidden[layer : layer + 1, 128 * k : 128 * k + 128]


def forward_plan():
    count = len(PARTS)
    steps = []
    for i in range(count + 3):
        for lag, kind in enumerate(("xy", "dg", "last", "fin")):
            if 0 <= i - lag < count:
                steps.append((kind, i - lag))
    units = [(layer, name, cost) for layer in range(2) for name, cost in UNIT_TIMES]
    last = {PARTS[k][0]: k for k in range(count)}
    need = {"joint": 0, "up0": 1, "down": 2}
    order, finished, at, budget = [], set(), 0, 0.0
    for step in steps:
        order.append(step)
        if step[0] == "fin":
            finished.add(step[1])
        budget += SPREAD
        while at < len(units):
            layer, name, cost = units[at]
            if name in need and last[3 * layer + need[name]] not in finished:
                budget = min(budget, 0.0)
                break
            if cost > budget + 0.5:
                break
            budget -= cost
            order.append(("run", layer, name))
            at += 1
    return order + [("run", layer, name) for layer, name, cost in units[at:]]


def forward_kernel(
    tokens, seg, gains, biases, hidden, joint_w, output_w, expand_w, shrink_w,
    whole, vec_out, x_saved, j_saved, c_saved, l_saved, n1_saved, r1_saved, g_saved, gp_saved, n2_saved, r2_saved, final, squares,
    stage, sbuf, wv, bias, x1, h, hb, xb, joint, ctx, logsum, n1, r1, g, gp, n2, r2, vg, vec, vec_now,
    sems, stage_sems, wv_sems, vec_sems, out_sems,
):
    masters = (joint_w, output_w, expand_w, shrink_w)
    gather = Gather(whole, sbuf, sems)
    q, z, c = gather.q, gather.z, gather.c

    def stage_copies(grp):
        layer, kind = divmod(grp, 3)
        slot = grp % 2
        out = []
        for b in range(4):
            if kind == 0:
                src = output_w.at[layer] if b == 3 else joint_w.at[layer, :, pl.ds(768 * b, 768)]
            elif kind == 1:
                src = expand_w.at[layer, :, pl.ds(768 * b, 768)]
            else:
                src = shrink_w.at[layer, pl.ds(96 * b, 96), :]
            out.append(pltpu.make_async_copy(src, stage.at[slot, b], stage_sems.at[slot, b]))
        return out

    def take(grp):
        layer, kind = divmod(grp, 3)
        slot = grp % 2
        for cp in stage_copies(grp):
            cp.wait()
        sums = []
        for b in range(4):
            value = stage[slot, b]
            sbuf[grp, b] = value.astype(BF)
            sums.append(jnp.sum(value * value, axis=0, keepdims=True))
        if kind == 0:
            squares[4 * layer : 4 * layer + 1, :] = sums[0] + sums[1] + sums[2]
            squares[4 * layer + 1 : 4 * layer + 2, :] = sums[3]
        else:
            row = 4 * layer + 1 + kind
            squares[row : row + 1, :] = sums[0] + sums[1] + sums[2] + sums[3]
        if grp + 2 < GROUPS:
            for cp in stage_copies(grp + 2):
                cp.start()

    for grp in range(2):
        for cp in stage_copies(grp):
            cp.start()
    take(0)
    greet([gather.x_side, gather.y_side, gather.sibling] + gather.planes)
    gather.z_send(0)

    pack_vectors(vec_now, gains, biases, hidden, 0.0)
    vg[z, c] = vec_now[...].reshape(32, 128)

    def vec_copy(zz, peer, slot):
        return pltpu.make_async_remote_copy(
            src_ref=vg.at[zz, c], dst_ref=vg.at[zz, c], send_sem=vec_sems.at[2 * slot], recv_sem=vec_sems.at[2 * slot + 1],
            device_id=peer, device_id_type=MESH,
        )

    def vec_total(slot, count):
        ref = vg.at[0, pl.ds(0, 1)] if count == 1 else (vg.at[0, pl.ds(0, 2)] if count == 2 else vg.at[pl.ds(0, 2)])
        pltpu.make_async_copy(ref, ref, vec_sems.at[slot]).wait()

    for k, peer in enumerate(gather.planes):
        vec_copy(z, peer, k).start()
    take(1)
    gather.z_send(1)
    take(2)
    take(3)
    for k in range(3):
        vec_copy((z + 3 - k) % 4, gather.planes[0], k).wait_recv()
    for zz in range(4):
        vec_copy(zz, gather.sibling, 3 + zz).start()
    take(4)
    take(5)
    build_mask(seg, bias)
    for zz in range(4):
        vec_copy(zz, gather.sibling, 3 + zz).wait_recv()
    lane = lax.broadcasted_iota(jnp.int32, (128, 768), 1)
    spot = lax.broadcasted_iota(jnp.int32, (128, 768), 0)
    for layer in range(2):
        acc = jnp.zeros((8, 768), F32)
        for m in range(8):
            pick = jnp.where((lane == spot + 96 * m) & (spot < 96), 1.0, 0.0).astype(BF)
            acc = acc + nn(vg[m // 2, m % 2, 16 * layer : 16 * layer + 8, :].astype(BF), pick)
            for k in range(3):
                row = vg[m // 2, m % 2, 16 * layer + 8 + k : 16 * layer + 9 + k, :].astype(BF).astype(F32)
                start = 384 * (m % 2) + 128 * k
                vec[layer, 8 + m // 2 : 9 + m // 2, start : start + 128] = row
        vec[layer, 0:8, :] = acc
        vec[layer, 12:16, :] = jnp.zeros((4, 768), F32)

    started = []

    def save(src, dst):
        n = len(started)
        cp = pltpu.make_async_copy(src, dst, out_sems.at[n])
        cp.start()
        started.append(cp)

    def load(grp):
        return pltpu.make_async_copy(whole.at[grp], wv.at[grp % 3], wv_sems.at[grp % 3])

    def event(kind, k):
        if kind == "xy":
            gather.xy_send(k)
            if k + 2 < len(PARTS):
                gather.z_send(k + 2)
        elif kind == "dg":
            gather.diagonal_send(k)
        elif kind == "last":
            gather.last_send(k)
        elif kind == "fin":
            gather.finish(k)
            grp, first, count = PARTS[k]
            if first + count == 96:
                load(grp).start()

    order = forward_plan()
    pos = 0
    while pos < len(order):
        item = order[pos]
        if item[0] != "run":
            event(*item)
            pos += 1
            continue
        _, layer, name = item
        vl = vec.at[layer]
        x_in = tokens if layer == 0 else x1
        xb_in = tokens if layer == 0 else xb
        if name == "joint":
            load(3 * layer).wait()
            joint_forward(xb_in, wv.at[0], vl, joint.at[layer])
            save(joint.at[layer], j_saved.at[layer])
        elif name.startswith("att"):
            hooks, first = {}, int(name[3:])
            p, look = first, pos
            while True:
                it = order[look]
                if it[0] == "run":
                    if not it[2].startswith("att"):
                        break
                    p = int(it[2][3:]) + 1
                else:
                    hooks.setdefault(p, []).append(it)
                look += 1
            tail = hooks.pop(6, [])

            @pl.loop(0, PAIRS)
            def _(p):
                for at, items in hooks.items():
                    @pl.when(p == at)
                    def _():
                        for it in items:
                            event(*it)
                attend_forward_pair(p, joint.at[layer], bias, ctx.at[layer], logsum.at[layer])

            for it in tail:
                event(*it)
            save(ctx.at[layer], c_saved.at[layer])
            save(logsum.at[layer], l_saved.at[layer])
            pos = look
            continue
        elif name == "out":
            out_forward(ctx.at[layer], x_in, wv.at[0, 3], vl, n1.at[layer], r1.at[layer], h, hb)
            save(n1.at[layer], n1_saved.at[layer])
            save(r1.at[layer], r1_saved.at[layer])
        elif name.startswith("up"):
            b = int(name[2:])
            if b == 0:
                load(3 * layer + 1).wait()
            ffn_up(hb, wv.at[1], vl, g.at[layer], gp.at[layer], b)
            if b == 3:
                save(g.at[layer], g_saved.at[layer])
                save(gp.at[layer], gp_saved.at[layer])
        else:
            load(3 * layer + 2).wait()
            ffn_down(g.at[layer], wv.at[2], vl, h, n2.at[layer], r2.at[layer], x1 if layer == 0 else None, xb if layer == 0 else hb)
            save(n2.at[layer], n2_saved.at[layer])
            save(r2.at[layer], r2_saved.at[layer])
            if layer == 0:
                save(xb, x_saved)
            else:
                save(hb, final)
        pos += 1
    save(vec, vec_out)
    for k in range(len(PARTS)):
        gather.drain(k)
    for k in range(3):
        vec_copy(z, gather.planes[k], k).wait_send()
    for zz in range(4):
        vec_copy(zz, gather.sibling, 3 + zz).wait_send()
    for cp in started:
        cp.wait()


def forward_call(tokens, seg, gains, biases, hidden, joint_w, output_w, expand_w, shrink_w):
    sd = jax.ShapeDtypeStruct
    any_spec = pl.BlockSpec(memory_space=pl.ANY)
    vm = pl.BlockSpec(memory_space=pltpu.VMEM)
    V = pltpu.VMEM
    saved = [
        sd((6, 4, 768, 768), BF),
        sd((2, 16, 768), F32),
        sd((T, D), BF),
        sd((2, 3, T, D), BF),
        sd((2, T, D), BF),
        sd((2, 6, 2, T), F32),
        sd((2, T, D), BF),
        sd((2, T, 128), F32),
        sd((2, 4, T, D), BF),
        sd((2, 4, T, D), BF),
        sd((2, T, D), BF),
        sd((2, T, 128), F32),
        sd((T, D), BF),
        sd((8, 768), F32),
    ]
    scratch = [
        V((2, 4, 96, 768), F32),
        V((6, 4, 96, 768), BF),
        V((3, 4, 768, 768), BF),
        V((T, T), F32),
        V((T, D), F32),
        V((T, D), F32),
        V((T, D), BF),
        V((T, D), BF),
        V((2, 3, T, D), BF),
        V((2, T, D), BF),
        V((2, 6, 2, T), F32),
        V((2, T, D), BF),
        V((2, T, 128), F32),
        V((2, 4, T, D), BF),
        V((2, 4, T, D), BF),
        V((2, T, D), BF),
        V((2, T, 128), F32),
        V((4, 2, 32, 128), F32),
        V((2, 16, 768), F32),
        V((2, 16, 128), F32),
        pltpu.SemaphoreType.DMA((len(PARTS), 13)),
        pltpu.SemaphoreType.DMA((2, 4)),
        pltpu.SemaphoreType.DMA((3,)),
        pltpu.SemaphoreType.DMA((14,)),
        pltpu.SemaphoreType.DMA((24,)),
    ]
    return pl.pallas_call(
        forward_kernel,
        out_shape=saved,
        in_specs=[vm] * 5 + [any_spec] * 4,
        out_specs=[any_spec] * 13 + [vm],
        scratch_shapes=scratch,
        compiler_params=pltpu.CompilerParams(
            collective_id=0, has_side_effects=True, vmem_limit_bytes=62 << 20
        ),
        name="forward",
    )(tokens, seg, gains, biases, hidden, joint_w, output_w, expand_w, shrink_w)


ROOT_SCALE = 1.0 / math.sqrt(32 * T)

BACK_UNITS = (
    (("ln2", 1.2),)
    + tuple((f"s{i}", 1.3) for i in range(4))
    + tuple((f"dz{i}", 1.0) for i in range(4))
    + (("ht", 0.9), ("e0", 1.5), ("e1", 1.5), ("dh", 2.8), ("ln1", 1.2), ("o", 2.4))
    + tuple((f"att{p}", 1.75) for p in range(6))
    + (("xt", 0.5), ("q0", 1.5), ("q1", 1.5), ("dx", 2.4))
)
GROUP_OF = {"s": 0, "e": 1, "o": 2, "q": 2}
PARTS_OF = {"s0": (0,), "s1": (1,), "s2": (2,), "s3": (3,), "e0": (0, 1), "e1": (2, 3), "q0": (0, 1), "q1": (2, 3)}


def backward_plan():
    now, xy_free, z_free, core_free = 0.0, 0.0, 0.0, 0.0
    pending, order, summed = [], [], set()

    def emit(entry):
        nonlocal now, xy_free, z_free
        ready, name, t, zz = entry
        now = max(now, ready) + 0.4
        order.append((name, t, zz))
        if name == "xy1":
            xy_free = max(xy_free, now) + 3.2
            pending.append((xy_free + 1.5, "xy2", t, zz))
        elif name == "xy2":
            xy_free = max(xy_free, now) + 1.6
            pending.append((xy_free + 1.5, "z", t, zz))
        elif name == "z":
            z_free = max(z_free, now) + 3.2
            if sum(1 for o in order if o[0] == "z" and o[1] == t) == 4:
                pending.append((z_free + 1.5, "sum", t, 0))
        elif name == "sum":
            summed.add(t)
            xy_free = max(xy_free, now) + 3.2
            pending.append((xy_free + 1.5, "ag", t, 0))
        elif name == "ag":
            xy_free = max(xy_free, now) + 1.6
            pending.append((xy_free + 1.5, "fin", t, 0))
        elif name == "fin":
            pending.append((now, "stat", t, 0))
        elif name == "stat":
            now += 1.0
        elif name == "vec" and zz < 4:
            pending.append((now + 2.5, "vec", t, zz + 1))

    emitted = set()

    def force(name, t, zz):
        if t < 0 or (name, t, zz) in emitted:
            return
        for entry in list(pending):
            if entry[1:] == (name, t, zz):
                pending.remove(entry)
                settle(entry)
                return
        force({"xy2": "xy1", "z": "xy2"}[name], t, zz)
        force(name, t, zz)

    def settle(entry):
        name, t, zz = entry[1:]
        emitted.add((name, t, zz))
        after = {"xy1": "xy2", "xy2": "z"}.get(name)
        if after:
            force(after, t - 1, zz)
        emit(entry)

    def step(limit):
        pending.sort()
        if pending and pending[0][0] <= limit:
            settle(pending.pop(0))
            return True
        return False

    for layer in (1, 0):
        for name, cost in BACK_UNITS:
            while step(now):
                pass
            if name[0] in GROUP_OF and name != "ln2":
                t = 3 * (1 - layer) + GROUP_OF[name[0]]
                while t >= 3 and t - 3 not in summed:
                    step(1e9)
            for zz in PARTS_OF.get(name, ()):
                force("xy1", t - 1, zz)
            order.append(("run", layer, name))
            now += cost
            for zz in PARTS_OF.get(name, ()):
                core_free = max(core_free, now) + 1.0
                pending.append((core_free + 1.5, "xy1", 3 * (1 - layer) + GROUP_OF[name[0]], zz))
    pending.append((now, "vec", 0, 0))
    while step(1e9):
        pass
    return order


class Reduce:
    def __init__(self, gb, rc, rx1, ry1, rx2, ry2, rz, fin, sems, group_sems, credits):
        self.gb, self.rc, self.rx1, self.ry1, self.rx2, self.ry2, self.rz, self.fin = gb, rc, rx1, ry1, rx2, ry2, rz, fin
        self.sems, self.group_sems, self.credits = sems, group_sems, credits
        q, z, c, self.x_side, self.y_side, self.sibling, self.planes = place()
        self.q, self.z, self.c = q, z, c
        self.ax, self.ay = q % 2, q // 2

    def send(self, src, dst, sem, peer):
        pltpu.make_async_remote_copy(
            src_ref=src, dst_ref=dst, send_sem=sem[0], recv_sem=sem[1], device_id=peer, device_id_type=MESH
        ).start()

    def pair(self, t, zz, slot):
        return self.sems.at[4 * t + zz, 2 * slot], self.sems.at[4 * t + zz, 2 * slot + 1]

    def group_pair(self, t, slot):
        return self.group_sems.at[t, 2 * slot], self.group_sems.at[t, 2 * slot + 1]

    def wait(self, ref, sem):
        pltpu.make_async_copy(ref, ref, sem).wait()

    def credit_wait(self, t, phase, zz):
        if t > 0:
            pl.semaphore_wait(self.credits.at[phase, zz], 1)

    def credit_give(self, t, phase, zz, peer):
        if t < 5:
            pl.semaphore_signal(self.credits.at[phase, zz], inc=1, device_id=peer, device_id_type=MESH)

    def core_send(self, t, zz):
        self.credit_wait(t, 0, zz)
        self.send(self.gb.at[t % 3, :, :, zz, 1 - self.c], self.rc.at[zz], self.pair(t, zz, 0), self.sibling)

    def add(self, ref, other):
        ref[...] = (ref[...].astype(F32) + other[...].astype(F32)).astype(BF)

    def xy1(self, t, zz):
        gb, c = self.gb.at[t % 3], self.c
        self.wait(self.rc.at[0], self.pair(t, zz, 0)[1])
        for by in range(2):
            for bx in range(2):
                self.add(gb.at[by, bx, zz, c], self.rc.at[zz, by, bx])
        self.credit_give(t, 0, zz, self.sibling)
        self.credit_wait(t, 1, zz)
        self.send(gb.at[:, 1 - self.ax, zz, c, pl.ds(0, 48)], self.rx1.at[zz], self.pair(t, zz, 1), self.x_side)
        self.credit_wait(t, 2, zz)
        self.send(gb.at[1 - self.ay, :, zz, c, pl.ds(48, 48)], self.ry1.at[zz], self.pair(t, zz, 2), self.y_side)

    def xy2(self, t, zz):
        gb, c = self.gb.at[t % 3], self.c
        self.wait(self.rx1.at[0], self.pair(t, zz, 1)[1])
        self.wait(self.ry1.at[0], self.pair(t, zz, 2)[1])
        for k in range(2):
            self.add(gb.at[k, self.ax, zz, c, pl.ds(0, 48)], self.rx1.at[zz, k])
            self.add(gb.at[self.ay, k, zz, c, pl.ds(48, 48)], self.ry1.at[zz, k])
        self.credit_give(t, 1, zz, self.x_side)
        self.credit_give(t, 2, zz, self.y_side)
        self.credit_wait(t, 3, zz)
        self.send(gb.at[self.ay, 1 - self.ax, zz, c, pl.ds(48, 48)], self.rx2.at[zz], self.pair(t, zz, 3), self.x_side)
        self.credit_wait(t, 4, zz)
        self.send(gb.at[1 - self.ay, self.ax, zz, c, pl.ds(0, 48)], self.ry2.at[zz], self.pair(t, zz, 4), self.y_side)

    def z_send(self, t, zz):
        gb, c = self.gb.at[t % 3], self.c
        self.wait(self.rx2.at[0], self.pair(t, zz, 3)[1])
        self.wait(self.ry2.at[0], self.pair(t, zz, 4)[1])
        self.add(gb.at[self.ay, self.ax, zz, c, pl.ds(48, 48)], self.rx2.at[zz])
        self.add(gb.at[self.ay, self.ax, zz, c, pl.ds(0, 48)], self.ry2.at[zz])
        self.credit_give(t, 3, zz, self.x_side)
        self.credit_give(t, 4, zz, self.y_side)

        @pl.when(self.z != zz)
        def _():
            self.send(
                gb.at[self.ay, self.ax, zz, c], self.rz.at[t, (self.z + 3 - zz) % 4], self.group_pair(t, 0),
                (self.q, 2 * zz + c),
            )

    def total(self, t):
        gb, c = self.gb.at[t % 3], self.c
        self.wait(self.rz.at[0], self.group_pair(t, 0)[1])
        own = gb[self.ay, self.ax, self.z, c].astype(F32)
        for k in range(3):
            own = own + self.rz[t, k].astype(F32)
        self.fin[t, self.q] = own.astype(BF)
        spot = self.fin.at[t, self.q]
        self.send(spot, spot, self.group_pair(t, 1), self.x_side)
        self.send(spot, spot, self.group_pair(t, 2), self.y_side)

    def share(self, t):
        self.wait(self.fin.at[0, 0], self.group_pair(t, 1)[1])
        self.wait(self.fin.at[0, 0], self.group_pair(t, 2)[1])
        qx = self.q + 1 - 2 * self.ax
        qy = (self.q + 2) % 4
        spot = self.fin.at[t, qy, pl.ds(0, 48)]
        self.send(spot, spot, self.group_pair(t, 3), self.x_side)
        spot = self.fin.at[t, qx, pl.ds(48, 48)]
        self.send(spot, spot, self.group_pair(t, 4), self.y_side)

    def finish(self, t):
        self.wait(self.fin.at[0, 0, pl.ds(0, 48)], self.group_pair(t, 3)[1])
        self.wait(self.fin.at[0, 0, pl.ds(0, 48)], self.group_pair(t, 4)[1])

    def drain(self, t):
        for zz in range(4):
            self.wait(self.rc.at[0], self.pair(t, zz, 0)[0])
            self.wait(self.rx1.at[0], self.pair(t, zz, 1)[0])
            self.wait(self.ry1.at[0], self.pair(t, zz, 2)[0])
            self.wait(self.rx2.at[0], self.pair(t, zz, 3)[0])
            self.wait(self.ry2.at[0], self.pair(t, zz, 4)[0])
        self.wait(self.rz.at[0], self.group_pair(t, 0)[0])

    def drain_share(self, t):
        self.wait(self.fin.at[0, 0], self.group_pair(t, 1)[0])
        self.wait(self.fin.at[0, 0], self.group_pair(t, 2)[0])
        self.wait(self.fin.at[0, 0, pl.ds(0, 48)], self.group_pair(t, 3)[0])
        self.wait(self.fin.at[0, 0, pl.ds(0, 48)], self.group_pair(t, 4)[0])


def backward_kernel(
    cot, seg, vec, squares, joint_rows, output_rows, expand_rows, shrink_rows,
    joint_columns, output_columns, expand_columns, shrink_columns, gains, biases, hidden, gain_old, bias_old, hidden_old,
    tokens, x_saved, whole, j_saved, c_saved, l_saved, n1_saved, r1_saved, g_saved, gp_saved, n2_saved, r2_saved,
    fin, grad_in, rows_new, columns_new, column_scale, vec_grad, vec_scale,
    gb, rc, rx1, ry1, rx2, ry2, rz, wv, g, dz, dj, ctx, n1, n2, r1, r2, logsum, xb, dob, at, hb, bias, du, sums, vr, va,
    row_cols, pay, pay_in, pay_z, pay_sum, columns_old, vec_now, vec_old,
    sems, group_sems, credits, load_sems, vec_sems, pay_sems,
):
    red = Reduce(gb, rc, rx1, ry1, rx2, ry2, rz, fin, sems, group_sems, credits)
    q, z, c = red.q, red.z, red.c
    sources = {
        "n2": (n2_saved, n2), "r2": (r2_saved, r2), "g": (g_saved, g), "dz": (gp_saved, dz), "n1": (n1_saved, n1),
        "r1": (r1_saved, r1), "ctx": (c_saved, ctx), "dj": (j_saved, dj), "logsum": (l_saved, logsum), "xb": (None, xb),
    }
    names = list(sources)

    def load(name, layer):
        src, dst = sources[name]
        if name == "xb":
            src = x_saved if layer == 1 else tokens
        else:
            src = src.at[layer]
        return pltpu.make_async_copy(src, dst, load_sems.at[names.index(name)])

    def weights(t):
        layer, kind = 1 - t // 3, (2, 1, 0)[t % 3]
        return pltpu.make_async_copy(whole.at[3 * layer + kind], wv.at[t % 2], load_sems.at[10 + t % 2])

    def need(layer, *which):
        for name in which:
            load(name, layer).wait()

    def release(layer, *which):
        if layer == 1:
            for name in which:
                load(name, 0).start()

    def next_weights(t):
        if t + 2 < 6:
            weights(t + 2).start()

    for name in ("n2", "r2", "g"):
        load(name, 1).start()
    weights(0).start()
    load("dz", 1).start()
    weights(1).start()
    for name in ("n1", "r1", "ctx", "dj", "logsum", "xb"):
        load(name, 1).start()
    build_mask(seg, bias)
    sums[...] = jnp.zeros_like(sums)
    greet([red.x_side, red.y_side, red.sibling] + red.planes)

    def blocks_pair(slot, b, pair, left):
        out = nn(at[pl.ds(384 * pair, 384), :], left).astype(BF)
        gb[slot, b // 2, b % 2, pl.ds(2 * pair, 2)] = out.reshape(2, 2, 96, 768)

    def unit(layer, name):
        base = 3 * (1 - layer)
        vl, sl = vec.at[layer], sums.at[layer]
        if name == "ln2":
            need(layer, "n2", "r2")
            norm_backward(cot if layer == 1 else du, n2, r2, vl[1:2, :], du, dob, sl, (1, 7, 6))
            release(layer, "n2", "r2")
        elif name[0] == "s":
            zz = int(name[1])
            if zz == 0:
                need(layer, "g")
                if base >= 3:
                    red.drain(base - 3)
            transpose_into(g.at[zz], at)
            for cc in range(2):
                out = nn(at[pl.ds(384 * cc, 384), :], dob[...]).astype(BF)
                gb[base % 3, :, :, zz, cc] = out.reshape(2, 2, 96, 768)
            red.core_send(base, zz)
            if zz == 3:
                release(layer, "g")
        elif name.startswith("dz"):
            b = int(name[2])
            if b == 0:
                need(layer, "dz")
                weights(base).wait()
            ffn_back_block(dob, wv.at[base % 2], dz, dz, sl, b)
            if b == 3:
                next_weights(base)
        elif name == "ht":
            need(layer, "n1", "r1")
            hb[...] = (n1[...].astype(F32) * vl[0:1, :] + vl[5:6, :]).astype(BF)
            transpose_into(hb, at)
        elif name[0] == "e":
            pair = int(name[1])
            if pair == 0 and base >= 3:
                red.drain(base - 2)
            for b in range(4):
                blocks_pair((base + 1) % 3, b, pair, dz[b])
            for zz in (2 * pair, 2 * pair + 1):
                red.core_send(base + 1, zz)
        elif name == "dh":
            weights(base + 1).wait()
            ffn_back_input(dz, wv.at[(base + 1) % 2], du)
            release(layer, "dz")
            next_weights(base + 1)
        elif name == "ln1":
            norm_backward(du, n1, r1, vl[0:1, :], du, dob, sl, (0, 5, 4))
            release(layer, "n1", "r1")
        elif name == "o":
            need(layer, "ctx")
            weights(base + 2).wait()
            if base >= 3:
                red.drain(base - 1)
            transpose_into(ctx, at)
            for pair in range(2):
                blocks_pair((base + 2) % 3, 3, pair, dob[...])
            context_back(dob, wv.at[(base + 2) % 2, 3], hb)
        elif name == "xt":
            need(layer, "xb")
            transpose_into(xb, at)
            release(layer, "xb", "logsum", "ctx")
        elif name[0] == "q":
            pair = int(name[1])
            for b in range(3):
                blocks_pair((base + 2) % 3, b, pair, dj[b])
            for zz in (2 * pair, 2 * pair + 1):
                red.core_send(base + 2, zz)
        elif name == "dx":
            input_back(dj, wv.at[(base + 2) % 2], du, du, sl)
            if layer == 0:
                grad_in[...] = du[...].astype(BF)
            release(layer, "dj")
            next_weights(base + 2)

    def event(name, t, zz):
        if name == "xy1":
            red.xy1(t, zz)
        elif name == "xy2":
            red.xy2(t, zz)
        elif name == "z":
            red.z_send(t, zz)
        elif name == "sum":
            red.total(t)
        elif name == "ag":
            red.share(t)
        elif name == "fin":
            red.finish(t)
        elif name == "stat":
            statistics(t)
        else:
            vec_event(zz)

    def vec_copy(src, dst, k, peer):
        return pltpu.make_async_remote_copy(
            src_ref=src, dst_ref=dst, send_sem=vec_sems.at[2 * k], recv_sem=vec_sems.at[2 * k + 1],
            device_id=peer, device_id_type=MESH,
        )

    hops = ((sums, red.sibling), (va.at[0], red.x_side), (va.at[1], red.y_side))

    def vec_event(k):
        if 1 <= k <= 3:
            src, peer = hops[k - 1]
            vec_copy(src, vr.at[k - 1], k - 1, peer).wait()
            va[k - 1] = src[...] + vr[k - 1]
        if k <= 2:
            src, peer = hops[k]
            vec_copy(src, vr.at[k], k, peer).start()
        elif k == 3:
            for j, peer in enumerate(red.planes):
                vec_copy(va.at[2], vr.at[3 + j], 3 + j, peer).start()
        else:
            for j, peer in enumerate(red.planes):
                vec_copy(va.at[2], vr.at[3 + j], 3 + j, peer).wait()
            vec_grads(plane_sum(va[2], [vr[3], vr[4], vr[5]]))

    def plane_sum(own, others):
        acc = jnp.zeros(own.shape, F32)
        for plane in range(4):
            part = jnp.where(z == plane, own, 0.0)
            for k in range(3):
                part = jnp.where((z + 3 - k) % 4 == plane, others[k], part)
            acc = acc + part
        return acc

    f = 2 * z + c

    def vec_grads(total):
        down = lax.broadcasted_iota(jnp.int32, (768, 128), 0)
        across = lax.broadcasted_iota(jnp.int32, (768, 128), 1)
        pick = jnp.where((down == across + 96 * f) & (across < 96), 1.0, 0.0).astype(F32)
        for layer in range(2):
            sums[layer] = total[layer] * ROOT_SCALE
            mine = lax.dot_general(
                sums[layer, 0:8, :], pick, (((1,), (0,)), ((), ())), precision=lax.Precision.HIGHEST, preferred_element_type=F32
            )
            vec_grad[layer] = jnp.zeros((16, 128), F32)
            vec_grad[layer, 0:8, :] = mine
            for k in range(3):
                part = jnp.zeros((1, 128), F32)
                for zz in range(4):
                    for cc in range(2):
                        here = sums[layer, 8 + zz : 9 + zz, 384 * cc + 128 * k : 384 * cc + 128 * k + 128]
                        part = jnp.where(f == 2 * zz + cc, here, part)
                vec_grad[layer, 8 + k : 9 + k, :] = part

    def all_sum(v):
        return jnp.sum(jnp.sum(v, axis=1, keepdims=True), axis=0, keepdims=True)

    lane = lax.broadcasted_iota(jnp.int32, (1, 768), 1)
    lane_c = lax.broadcasted_iota(jnp.int32, (128, 128), 1)

    def row_column(layer, chunk):
        return row_cols[:, 6 * layer + chunk : 6 * layer + chunk + 1]

    def set_row_column(layer, chunk, value):
        if value.shape[0] < 128:
            value = jnp.concatenate([value, jnp.zeros((128 - value.shape[0], 1), F32)], axis=0)
        row_cols[...] = jnp.where(lane_c == 6 * layer + chunk, value, row_cols[...])

    def squared(t, b):
        v = fin[t, b].astype(F32) * ROOT_SCALE
        return v * v

    def put_scalar(layer, index, value):
        pay[layer, 18:19, :] = jnp.where(lane == index, value, pay[layer, 18:19, :])

    def row_sums(sq):
        return jnp.sum(sq + FLOOR_SQUARE, axis=1, keepdims=True)

    def column_sums(sq):
        return jnp.sum(sq + FLOOR_SQUARE, axis=0, keepdims=True)

    def statistics(t):
        layer, kind = 1 - t // 3, (2, 1, 0)[t % 3]
        if kind == 2:
            sums_of = jnp.concatenate([row_sums(squared(t, b)) for b in range(4)], axis=0)
            old = jnp.concatenate([row_column(layer, 3 + k) for k in range(3)], axis=0)
            new = DECAY_RATE * old + (1.0 - DECAY_RATE) * (sums_of / 768.0)
            for k in range(3):
                set_row_column(layer, 3 + k, new[128 * k : 128 * k + 128])
            col, quo = jnp.zeros((1, 768), F32), jnp.zeros((1, 768), F32)
            for b in range(4):
                sq = squared(t, b)
                col = col + column_sums(sq)
                quo = quo + jnp.sum(sq / new[96 * b : 96 * b + 96], axis=0, keepdims=True)
            pay[layer, 8:9, :] = col
            pay[layer, 17:18, :] = quo
            put_scalar(layer, 3, jnp.sum(new, axis=0, keepdims=True))
            return
        sets = (((0, 1, 2), 0, 0, 0), ((3,), 1, 3, 1)) if kind == 0 else (((0, 1, 2, 3), 2, 4, 2),)
        for blocks, chunk, first, index in sets:
            sums_of = jnp.zeros((96, 1), F32)
            for b in blocks:
                sums_of = sums_of + row_sums(squared(t, b))
            old = row_column(layer, chunk)[0:96]
            new = DECAY_RATE * old + (1.0 - DECAY_RATE) * (sums_of / (768.0 * len(blocks)))
            set_row_column(layer, chunk, new)
            for k, b in enumerate(blocks):
                sq = squared(t, b)
                pay[layer, first + k : first + k + 1, :] = column_sums(sq)
                pay[layer, 9 + first + k : 10 + first + k, :] = jnp.sum(sq / new, axis=0, keepdims=True)
            put_scalar(layer, index, jnp.sum(new, axis=0, keepdims=True))

    def vec_moments(layer):
        grad = vec_grad[layer]
        return DECAY_RATE * vec_old[layer] + (1.0 - DECAY_RATE) * (grad * grad + FLOOR_SQUARE)

    def exchange_statistics():
        for layer in range(2):
            for m in range(4):
                put_scalar(layer, 4 + m, all_sum(squares[4 * layer + m : 4 * layer + m + 1, :]))
            grad, now = vec_grad[layer], vec_now[layer]
            step = grad * grad / vec_moments(layer)
            for r in range(9):
                rows = slice(r, r + 1) if r < 8 else slice(8, 11)
                put_scalar(layer, 8 + r, all_sum(now[rows] * now[rows]))
                put_scalar(layer, 17 + r, all_sum(step[rows]))

        def copy(src, dst, k, peer):
            return pltpu.make_async_remote_copy(
                src_ref=src, dst_ref=dst, send_sem=pay_sems.at[2 * k], recv_sem=pay_sems.at[2 * k + 1],
                device_id=peer, device_id_type=MESH,
            )

        cp = copy(pay, pay_in, 0, red.sibling)
        cp.start()
        cp.wait()
        pay_z[3] = pay[c] + pay_in[c]
        copies = [copy(pay_z.at[3], pay_z.at[k], 1 + k, peer) for k, peer in enumerate(red.planes)]
        for cp in copies:
            cp.start()
        for cp in copies:
            cp.wait()
        pay_sum[c] = plane_sum(pay_z[3], [pay_z[0], pay_z[1], pay_z[2]])
        cp = copy(pay_sum.at[c], pay_sum.at[c], 4, red.sibling)
        cp.start()
        cp.wait()

    def finish_statistics():
        rows_new[...] = row_cols[...].T[0:16]
        for layer in range(2):
            scalars = pay_sum[layer, 18:19, :]
            pick = lambda index: scalars[:, index : index + 1]
            for m, (first, count, rows) in enumerate(((0, 3, 768.0), (3, 1, 768.0), (4, 4, 768.0), (8, 1, 3072.0))):
                new = DECAY_RATE * columns_old[layer, first : first + count, :] + (1.0 - DECAY_RATE) * (
                    pay_sum[layer, first : first + count, :] / rows
                )
                columns_new[layer, first : first + count, :] = new
                mean_rows = pick(m) / rows
                entries = rows * 768.0 * count
                energy = mean_rows * all_sum(pay_sum[layer, 9 + first : 9 + first + count, :] / new)
                clip = jnp.sqrt(energy / entries) / CLIP_LIMIT
                stride = STEP_RATE * jnp.maximum(FLOOR_SCALE, jnp.sqrt(pick(4 + m) / entries))
                column_scale[layer, first : first + count, :] = lax.rsqrt(new) * (
                    jnp.sqrt(mean_rows) * stride / jnp.maximum(clip, 1.0)
                )
            vec_scale[layer] = jnp.zeros((16, 128), F32)
            for r in range(9):
                entries = 768.0 if r < 8 else 3072.0
                clip = jnp.sqrt(pick(17 + r) / entries) / CLIP_LIMIT
                stride = STEP_RATE * jnp.maximum(FLOOR_SCALE, jnp.sqrt(pick(8 + r) / entries))
                value = stride / jnp.maximum(clip, 1.0)
                if r < 8:
                    vec_scale[layer, r : r + 1, :] = jnp.broadcast_to(value, (1, 128))
                else:
                    vec_scale[layer, 8:11, :] = jnp.broadcast_to(value, (3, 128))

    row_cols[...] = jnp.ones((128, 128), F32)
    for layer in range(2):
        for m, ref in enumerate((joint_rows, output_rows, expand_rows)):
            row_cols[6 * layer + m : 6 * layer + m + 1, 0:96] = ref[layer : layer + 1, :]
        for k in range(3):
            row_cols[6 * layer + 3 + k : 6 * layer + 4 + k, :] = shrink_rows[layer : layer + 1, 128 * k : 128 * k + 128]
        at_row = 0
        for ref, count in ((joint_columns, 3), (output_columns, 1), (expand_columns, 4), (shrink_columns, 1)):
            for k in range(count):
                columns_old[layer, at_row : at_row + 1, :] = ref[layer : layer + 1, 768 * k : 768 * k + 768]
                at_row += 1
    row_cols[...] = row_cols[...].T
    pack_vectors(vec_now, gains, biases, hidden, 0.0)
    pack_vectors(vec_old, gain_old, bias_old, hidden_old, 1.0)
    pay[...] = jnp.zeros_like(pay)

    order = backward_plan()
    pos = 0
    done_units = False
    while pos < len(order):
        item = order[pos]
        if item[0] != "run":
            event(*item)
            pos += 1
            continue
        _, layer, name = item
        if not name.startswith("att"):
            unit(layer, name)
            pos += 1
            continue
        hooks, look, p = {}, pos, 0
        while True:
            it = order[look]
            if it[0] == "run":
                if not it[2].startswith("att"):
                    break
                p = int(it[2][3:]) + 1
            else:
                hooks.setdefault(p, []).append(it)
            look += 1
        tail = hooks.pop(6, [])
        need(layer, "dj", "logsum")

        @pl.loop(0, PAIRS)
        def _(p):
            for at_pair, items in hooks.items():
                @pl.when(p == at_pair)
                def _():
                    for it in items:
                        event(*it)
            attend_backward_pair(p, dj, bias, logsum, ctx, hb, dj)

        for it in tail:
            event(*it)
        pos = look

    exchange_statistics()
    finish_statistics()
    for t in range(3, 6):
        red.drain(t)
    for t in range(6):
        red.drain_share(t)


def backward_call(*args):
    sd = jax.ShapeDtypeStruct
    any_spec = pl.BlockSpec(memory_space=pl.ANY)
    vm = pl.BlockSpec(memory_space=pltpu.VMEM)
    V = pltpu.VMEM
    dma = pltpu.SemaphoreType.DMA
    return pl.pallas_call(
        backward_kernel,
        out_shape=[
            sd((6, 4, 96, 768), BF), sd((T, D), BF), sd((16, 128), F32), sd((2, 9, 768), F32), sd((2, 9, 768), F32),
            sd((2, 16, 128), F32), sd((2, 16, 128), F32),
        ],
        in_specs=[vm] * 18 + [any_spec] * 12,
        out_specs=[vm] * 7,
        scratch_shapes=[
            V((3, 2, 2, 4, 2, 96, 768), BF),
            V((4, 2, 2, 96, 768), BF),
            V((4, 2, 48, 768), BF),
            V((4, 2, 48, 768), BF),
            V((4, 48, 768), BF),
            V((4, 48, 768), BF),
            V((6, 3, 96, 768), BF),
            V((2, 4, 768, 768), BF),
            V((4, T, D), BF),
            V((4, T, D), BF),
            V((3, T, D), BF),
            V((T, D), BF),
            V((T, D), BF),
            V((T, D), BF),
            V((T, 128), F32),
            V((T, 128), F32),
            V((6, 2, T), F32),
            V((T, D), BF),
            V((T, D), BF),
            V((D, T), BF),
            V((T, D), BF),
            V((T, T), F32),
            V((T, D), F32),
            V((2, 16, 768), F32),
            V((6, 2, 16, 768), F32),
            V((3, 2, 16, 768), F32),
            V((128, 128), F32),
            V((2, 24, 768), F32),
            V((2, 24, 768), F32),
            V((4, 24, 768), F32),
            V((2, 24, 768), F32),
            V((2, 9, 768), F32),
            V((2, 16, 128), F32),
            V((2, 16, 128), F32),
            dma((24, 10)),
            dma((6, 10)),
            pltpu.SemaphoreType.REGULAR((5, 4)),
            dma((12,)),
            dma((12,)),
            dma((10,)),
        ],
        compiler_params=pltpu.CompilerParams(
            collective_id=1, has_side_effects=True, vmem_limit_bytes=63 << 20
        ),
        name="backward",
    )(*args)


def update_kernel(
    fin, rows_new, columns_new, column_scale, vec_grad, vec_scale, gains, biases, hidden, gain_old, bias_old, hidden_old, final, grad_in, joint_w, output_w, expand_w, shrink_w,
    *refs,
):
    outs, scratch = refs[:31], refs[31:]
    activations, input_gradient = outs[0], outs[1]
    grads, small_grads = outs[2:6], outs[6:9]
    nexts, small_nexts = outs[9:13], outs[13:16]
    copies = outs[16:20]
    row_outs, column_outs = outs[20:28:2], outs[21:28:2]
    small_moments = outs[28:31]
    masters = (joint_w, output_w, expand_w, shrink_w)
    wbuf, gbuf, nbuf, cbuf, pbuf, vec_now, vec_old, in_sems, out_sems, pass_sems = scratch
    inward = [
        pltpu.make_async_copy(final, pbuf.at[0], pass_sems.at[0]),
        pltpu.make_async_copy(grad_in, pbuf.at[1], pass_sems.at[1]),
    ]
    through = [
        pltpu.make_async_copy(pbuf.at[0], activations, pass_sems.at[2]),
        pltpu.make_async_copy(pbuf.at[1], input_gradient, pass_sems.at[3]),
    ]
    pieces = []
    for layer in range(2):
        for m, count in enumerate((3, 1, 4, 4)):
            for b in range(count):
                kind = (0, 0, 1, 2)[m]
                t = 3 * (1 - layer) + (2, 1, 0)[kind]
                pieces.append((layer, m, b, t, 3 if m == 1 else b))

    def part(ref, layer, m, b):
        if m == 1:
            return ref.at[layer]
        if m == 3:
            return ref.at[layer, pl.ds(96 * b, 96), :]
        return ref.at[layer, :, pl.ds(768 * b, 768)]

    loads = [
        pltpu.make_async_copy(part(masters[m], layer, m, b), wbuf.at[n], in_sems.at[n])
        for n, (layer, m, b, t, block) in enumerate(pieces)
    ]
    for cp in loads + inward:
        cp.start()
    pack_vectors(vec_now, gains, biases, hidden, 0.0)
    pack_vectors(vec_old, gain_old, bias_old, hidden_old, 1.0)
    columns = jnp.concatenate([lax.rsqrt(rows_new[...]), jnp.zeros((112, 128), F32)], axis=0).T
    stores = []
    for n, (layer, m, b, t, block) in enumerate(pieces):
        if n == 12:
            for before, cp in zip(inward, through):
                before.wait()
                cp.start()
        if m < 3:
            left = columns[0:96, 6 * layer + m : 6 * layer + m + 1]
        else:
            left = jnp.concatenate([columns[:, 6 * layer + 3 + k : 6 * layer + 4 + k] for k in range(3)], axis=0)
            left = left[96 * b : 96 * b + 96]
        j = (0, 3, 4, 8)[m] + (b if m != 3 else 0)
        grad = fin[t, block].astype(F32) * ROOT_SCALE
        loads[n].wait()
        new = wbuf[n] - grad * left * column_scale[layer, j : j + 1, :]
        gbuf[n] = grad
        nbuf[n] = new
        cbuf[n] = new.astype(BF)
        for k, (src, dst) in enumerate(((gbuf, grads[m]), (nbuf, nexts[m]), (cbuf, copies[m]))):
            cp = pltpu.make_async_copy(src.at[n], part(dst, layer, m, b), out_sems.at[n, k])
            cp.start()
            stores.append(cp)
    for layer in range(2):
        grad, now = vec_grad[layer], vec_now[layer]
        moments = DECAY_RATE * vec_old[layer] + (1.0 - DECAY_RATE) * (grad * grad + FLOOR_SQUARE)
        new = now - vec_scale[layer] * (grad * lax.rsqrt(moments))
        for out, value in zip((small_grads, small_nexts, small_moments), (grad, new, moments)):
            out[0][layer] = value[0:2, 0:96]
            for r in range(6):
                out[1][r, layer : layer + 1, :] = value[2 + r : 3 + r, 0:96]
            for k in range(3):
                out[2][layer : layer + 1, 128 * k : 128 * k + 128] = value[8 + k : 9 + k, :]
        for m in range(3):
            row_outs[m][layer : layer + 1, :] = rows_new[6 * layer + m : 6 * layer + m + 1, 0:96]
        for k in range(3):
            row_outs[3][layer : layer + 1, 128 * k : 128 * k + 128] = rows_new[6 * layer + 3 + k : 6 * layer + 4 + k, :]
        for m, (first, count) in enumerate(((0, 3), (3, 1), (4, 4), (8, 1))):
            for k in range(count):
                column_outs[m][layer : layer + 1, 768 * k : 768 * k + 768] = columns_new[layer, first + k : first + k + 1, :]
    for cp in stores + through:
        cp.wait()


def update_call(*args):
    sd = jax.ShapeDtypeStruct
    any_spec = pl.BlockSpec(memory_space=pl.ANY)
    vm = pl.BlockSpec(memory_space=pltpu.VMEM)
    V = pltpu.VMEM
    mats = ((2, 96, 2304), (2, 96, 768), (2, 96, 3072), (2, 384, 768))
    small = ((2, 2, 96), (6, 2, 96), (2, 384))
    stats = ((2, 96), (2, 2304), (2, 96), (2, 768), (2, 96), (2, 3072), (2, 384), (2, 768))
    shapes = (
        [sd((T, D), BF)] * 2 + [sd(s, F32) for s in mats] + [sd(s, F32) for s in small] + [sd(s, F32) for s in mats]
        + [sd(s, F32) for s in small] + [sd(s, BF) for s in mats] + [sd(s, F32) for s in stats] + [sd(s, F32) for s in small]
    )
    specs = [any_spec] * 6 + [vm] * 3 + [any_spec] * 4 + [vm] * 3 + [any_spec] * 4 + [vm] * 11
    return pl.pallas_call(
        update_kernel,
        out_shape=shapes,
        in_specs=[vm] * 12 + [any_spec] * 6,
        out_specs=specs,
        scratch_shapes=[
            V((24, 96, 768), F32),
            V((24, 96, 768), F32),
            V((24, 96, 768), F32),
            V((24, 96, 768), BF),
            V((2, T, D), BF),
            V((2, 16, 128), F32),
            V((2, 16, 128), F32),
            pltpu.SemaphoreType.DMA((24,)),
            pltpu.SemaphoreType.DMA((24, 3)),
            pltpu.SemaphoreType.DMA((4,)),
        ],
        compiler_params=pltpu.CompilerParams(vmem_limit_bytes=56 << 20),
        name="update",
    )(*args)


def local_kernels(
    tokens,
    segments,
    cotangent,
    joint_weight,
    output_weight,
    expand_weight,
    shrink_weight,
    norm_gains,
    biases,
    hidden_bias,
    joint_rows,
    joint_columns,
    output_rows,
    output_columns,
    expand_rows,
    expand_columns,
    shrink_rows,
    shrink_columns,
    gain_moments,
    bias_moments,
    hidden_moments,
):
    turned = biases.transpose(1, 0, 2)
    turned_old = bias_moments.transpose(1, 0, 2)
    (whole, vec, x_saved, j_s, c_s, l_s, n1_s, r1_s, g_s, gp_s, n2_s, r2_s, final, squares) = forward_call(
        tokens[0], segments, norm_gains, turned, hidden_bias, joint_weight, output_weight, expand_weight, shrink_weight
    )
    vectors = (norm_gains, turned, hidden_bias, gain_moments, turned_old, hidden_moments)
    blocks, grad_in, rows_new, columns_new, column_scale, vec_grad, vec_scale = backward_call(
        cotangent[0], segments, vec, squares, joint_rows, output_rows, expand_rows, shrink_rows,
        joint_columns, output_columns, expand_columns, shrink_columns, *vectors,
        tokens[0], x_saved, whole, j_s, c_s, l_s, n1_s, r1_s, g_s, gp_s, n2_s, r2_s
    )
    outs = list(update_call(
        blocks, rows_new, columns_new, column_scale, vec_grad, vec_scale, *vectors, final, grad_in,
        joint_weight, output_weight, expand_weight, shrink_weight
    ))
    for n in (7, 14, 29):
        outs[n] = outs[n].transpose(1, 0, 2)
    return (outs[0][None], outs[1][None]) + tuple(outs[2:])


def solution(mesh):
    placed = (
        P(("dp", "fsdp"), None, None),
        P(("dp", "fsdp"), None),
        P(("dp", "fsdp"), None, None),
        P(None, "fsdp", None),
        P(None, "fsdp", None),
        P(None, "fsdp", None),
        P(None, "fsdp", None),
        P(None, None, "fsdp"),
        P(None, None, "fsdp"),
        P(None, "fsdp"),
        P(None, "fsdp"),
        P(),
        P(None, "fsdp"),
        P(),
        P(None, "fsdp"),
        P(),
        P(None, "fsdp"),
        P(),
        P(None, None, "fsdp"),
        P(None, None, "fsdp"),
        P(None, "fsdp"),
    )
    known = dict(mesh.shape) == {"dp": 4, "fsdp": 8}
    return jax.shard_map(
        local_kernels if known else local_plain,
        mesh=mesh,
        in_specs=placed,
        out_specs=(
            P(("dp", "fsdp"), None, None),
            P(("dp", "fsdp"), None, None),
            P(None, "fsdp", None),
            P(None, "fsdp", None),
            P(None, "fsdp", None),
            P(None, "fsdp", None),
            P(None, None, "fsdp"),
            P(None, None, "fsdp"),
            P(None, "fsdp"),
            P(None, "fsdp", None),
            P(None, "fsdp", None),
            P(None, "fsdp", None),
            P(None, "fsdp", None),
            P(None, None, "fsdp"),
            P(None, None, "fsdp"),
            P(None, "fsdp"),
            P(None, "fsdp", None),
            P(None, "fsdp", None),
            P(None, "fsdp", None),
            P(None, "fsdp", None),
            P(None, "fsdp"),
            P(),
            P(None, "fsdp"),
            P(),
            P(None, "fsdp"),
            P(),
            P(None, "fsdp"),
            P(),
            P(None, None, "fsdp"),
            P(None, None, "fsdp"),
            P(None, "fsdp"),
        ),
        check_vma=False,
    )
```

```python
from functools import partial
import math

import jax
import jax.numpy as jnp
from jax import lax
from jax.sharding import PartitionSpec as P
from jax.experimental import pallas as pl
from jax.experimental.pallas import tpu as pltpu

HEADS = 12
HEAD_SIZE = 64


NORM_EPSILON = 1e-12
SCORE_SCALE = 0.125
MASK_VALUE = -1e30
FLOOR_SQUARE = 1e-30
FLOOR_SCALE = 0.001
DECAY_RATE = 0.5
CLIP_LIMIT = 0.25
STEP_RATE = 4.0


def product(left, right):
    return jnp.dot(left, right, preferred_element_type=jnp.float32)


def product_left(left, right):
    return lax.dot_general(
        left, right, (((0,), (0,)), ((), ())), preferred_element_type=jnp.float32
    )


def product_right(left, right):
    return lax.dot_general(
        left, right, (((1,), (1,)), ((), ())), preferred_element_type=jnp.float32
    )


def normalize(values):
    average = jnp.mean(values, axis=-1, keepdims=True)
    centered = values - average
    variance = jnp.mean(centered * centered, axis=-1, keepdims=True)
    inverse = lax.rsqrt(variance + NORM_EPSILON)
    return (centered * inverse, inverse)


def normalize_back(grad_scaled, scaled, inverse):
    first_mean = jnp.mean(grad_scaled, axis=-1, keepdims=True)
    second_mean = jnp.mean(grad_scaled * scaled, axis=-1, keepdims=True)
    return inverse * (grad_scaled - first_mean - scaled * second_mean)


def split_heads(joint_row):
    slot_count = joint_row.shape[0]
    shaped = joint_row.reshape(slot_count, 3, HEADS, HEAD_SIZE)
    return (shaped[:, 0], shaped[:, 1], shaped[:, 2])


def masked_scores(query_rows, key_rows, segment_row):
    scores = (
        jnp.einsum("qhe,khe->hqk", query_rows, key_rows, preferred_element_type=jnp.float32)
        * SCORE_SCALE
    )
    allowed = segment_row[:, None] == segment_row[None, :]
    return jnp.where(allowed[None], scores, MASK_VALUE)


def attend_forward(packed):
    joint_row, segment_row = packed
    query_rows, key_rows, value_rows = split_heads(joint_row)
    scores = masked_scores(query_rows, key_rows, segment_row)
    highest = jnp.max(scores, axis=-1, keepdims=True)
    raised = jnp.exp(scores - highest)
    denominator = jnp.sum(raised, axis=-1, keepdims=True)
    weights = (raised / denominator).astype(jnp.bfloat16)
    context = jnp.einsum("hqk,khe->qhe", weights, value_rows, preferred_element_type=jnp.float32)
    logsum = (highest + jnp.log(denominator))[:, :, 0]
    return (context.astype(jnp.bfloat16).reshape(joint_row.shape[0], HEADS * HEAD_SIZE), logsum)


def attend_backward(packed):
    joint_row, segment_row, logsum, grad_row = packed
    slot_count = joint_row.shape[0]
    query_rows, key_rows, value_rows = split_heads(joint_row)
    scores = masked_scores(query_rows, key_rows, segment_row)
    probabilities = jnp.exp(scores - logsum[:, :, None])
    upstream = grad_row.reshape(slot_count, HEADS, HEAD_SIZE)
    grad_probs = jnp.einsum(
        "qhe,khe->hqk", upstream, value_rows, preferred_element_type=jnp.float32
    )
    row_delta = jnp.sum(probabilities * grad_probs, axis=-1, keepdims=True)
    grad_scores = (probabilities * (grad_probs - row_delta)).astype(jnp.bfloat16)
    grad_query = (
        jnp.einsum("hqk,khe->qhe", grad_scores, key_rows, preferred_element_type=jnp.float32)
        * SCORE_SCALE
    )
    grad_key = (
        jnp.einsum("hqk,qhe->khe", grad_scores, query_rows, preferred_element_type=jnp.float32)
        * SCORE_SCALE
    )
    grad_value = jnp.einsum(
        "hqk,qhe->khe",
        probabilities.astype(jnp.bfloat16),
        upstream,
        preferred_element_type=jnp.float32,
    )
    stacked = jnp.stack([grad_query, grad_key, grad_value], axis=1)
    return stacked.reshape(slot_count, 3 * HEADS * HEAD_SIZE).astype(jnp.bfloat16)


def block_forward(hidden_in, segments, weights):
    joint_matrix, output_matrix, expand_matrix, shrink_matrix, gain_rows, bias_rows, inner_bias = (
        weights
    )
    gain_values = gain_rows.astype(jnp.float32)
    bias_values = bias_rows.astype(jnp.float32)
    row_count, slot_count = segments.shape
    zero_block = jnp.zeros_like(bias_values[0])
    joint_bias = jnp.concatenate([bias_values[0], zero_block, bias_values[1]])
    joint_out = (product(hidden_in.astype(jnp.bfloat16), joint_matrix) + joint_bias).astype(
        jnp.bfloat16
    )
    context, logsum = lax.map(
        attend_forward, (joint_out.reshape(row_count, slot_count, -1), segments)
    )
    context = context.reshape(row_count * slot_count, -1)
    attended = product(context, output_matrix) + bias_values[2]
    first_scaled, first_inverse = normalize(hidden_in + attended)
    first_norm = first_scaled * gain_values[0] + bias_values[3]
    pre_active = product(first_norm.astype(jnp.bfloat16), expand_matrix) + inner_bias.astype(
        jnp.float32
    )
    active = jax.nn.gelu(pre_active, approximate=False).astype(jnp.bfloat16)
    branch = product(active, shrink_matrix) + bias_values[4]
    second_scaled, second_inverse = normalize(first_norm + branch)
    result = second_scaled * gain_values[1] + bias_values[5]
    stored = (
        hidden_in,
        joint_out,
        context,
        logsum,
        first_scaled,
        first_inverse,
        pre_active,
        second_scaled,
        second_inverse,
    )
    return (result, stored)


def block_backward(grad_out, segments, weights, stored):
    joint_matrix, output_matrix, expand_matrix, shrink_matrix, gain_rows, bias_rows, inner_bias = (
        weights
    )
    (
        hidden_in,
        joint_out,
        context,
        logsum,
        first_scaled,
        first_inverse,
        pre_active,
        second_scaled,
        second_inverse,
    ) = stored
    gain_values = gain_rows.astype(jnp.float32)
    bias_values = bias_rows.astype(jnp.float32)
    row_count, slot_count = segments.shape
    features = hidden_in.shape[1]
    grad_second_bias = jnp.sum(grad_out, axis=0)
    grad_second_gain = jnp.sum(grad_out * second_scaled, axis=0)
    grad_sum = normalize_back(grad_out * gain_values[1], second_scaled, second_inverse)
    grad_branch = grad_sum.astype(jnp.bfloat16)
    active, gelu_back = jax.vjp(partial(jax.nn.gelu, approximate=False), pre_active)
    grad_shrink = product_left(active.astype(jnp.bfloat16), grad_branch)
    grad_active = product_right(grad_branch, shrink_matrix)
    grad_pre = gelu_back(grad_active)[0].astype(jnp.bfloat16)
    first_norm = first_scaled * gain_values[0] + bias_values[3]
    grad_expand = product_left(first_norm.astype(jnp.bfloat16), grad_pre)
    grad_first = grad_sum + product_right(grad_pre, expand_matrix)
    grad_first_bias = jnp.sum(grad_first, axis=0)
    grad_first_gain = jnp.sum(grad_first * first_scaled, axis=0)
    grad_middle = normalize_back(grad_first * gain_values[0], first_scaled, first_inverse)
    grad_attended = grad_middle.astype(jnp.bfloat16)
    grad_output = product_left(context, grad_attended)
    grad_context = product_right(grad_attended, output_matrix).astype(jnp.bfloat16)
    grad_joint_out = lax.map(
        attend_backward,
        (
            joint_out.reshape(row_count, slot_count, -1),
            segments,
            logsum,
            grad_context.reshape(row_count, slot_count, -1),
        ),
    )
    grad_joint_out = grad_joint_out.reshape(row_count * slot_count, -1)
    grad_joint = product_left(hidden_in.astype(jnp.bfloat16), grad_joint_out)
    grad_input = grad_middle + product_right(grad_joint_out, joint_matrix)
    joint_sums = jnp.sum(grad_joint_out, axis=0, dtype=jnp.float32)
    bias_grads = jnp.stack(
        [
            joint_sums[:features],
            joint_sums[2 * features :],
            jnp.sum(grad_attended, axis=0, dtype=jnp.float32),
            grad_first_bias,
            jnp.sum(grad_branch, axis=0, dtype=jnp.float32),
            grad_second_bias,
        ]
    )
    gain_grads = jnp.stack([grad_first_gain, grad_second_gain])
    inner_grad = jnp.sum(grad_pre, axis=0, dtype=jnp.float32)
    return (
        grad_input,
        (grad_joint, grad_output, grad_expand, grad_shrink, gain_grads, bias_grads, inner_grad),
    )


def factored_partials(gradient, weight, rows_old):
    squared = gradient * gradient + FLOOR_SQUARE
    rows_next = DECAY_RATE * rows_old + (1.0 - DECAY_RATE) * jnp.mean(squared, axis=2)
    return (
        rows_next,
        jnp.sum(squared, axis=1),
        jnp.sum(rows_next, axis=1),
        jnp.sum(weight * weight, axis=(1, 2)),
    )


def vector_partials(gradient, moments_old):
    moments_next = DECAY_RATE * moments_old + (1.0 - DECAY_RATE) * (
        gradient * gradient + FLOOR_SQUARE
    )
    return (moments_next, gradient * lax.rsqrt(moments_next))


def local_plain(
    tokens,
    segments,
    cotangent,
    joint_weight,
    output_weight,
    expand_weight,
    shrink_weight,
    norm_gains,
    biases,
    hidden_bias,
    joint_rows,
    joint_columns,
    output_rows,
    output_columns,
    expand_rows,
    expand_columns,
    shrink_rows,
    shrink_columns,
    gain_moments,
    bias_moments,
    hidden_moments,
):
    layers = joint_weight.shape[0]
    row_count, slot_count, features = tokens.shape
    hidden = tokens.astype(jnp.float32).reshape(row_count * slot_count, features)
    gathered_list = []
    stored_list = []
    for number in range(layers):
        weights = (
            lax.all_gather(joint_weight[number].astype(jnp.bfloat16), "fsdp", axis=0, tiled=True),
            lax.all_gather(output_weight[number].astype(jnp.bfloat16), "fsdp", axis=0, tiled=True),
            lax.all_gather(expand_weight[number].astype(jnp.bfloat16), "fsdp", axis=0, tiled=True),
            lax.all_gather(shrink_weight[number].astype(jnp.bfloat16), "fsdp", axis=0, tiled=True),
            lax.all_gather(norm_gains[number].astype(jnp.bfloat16), "fsdp", axis=1, tiled=True),
            lax.all_gather(biases[number].astype(jnp.bfloat16), "fsdp", axis=1, tiled=True),
            lax.all_gather(hidden_bias[number].astype(jnp.bfloat16), "fsdp", axis=0, tiled=True),
        )
        hidden, stored = block_forward(hidden, segments, weights)
        gathered_list.append(weights)
        stored_list.append(stored)
    activations = hidden.reshape(row_count, slot_count, features).astype(jnp.bfloat16)
    grad_hidden = cotangent.astype(jnp.float32).reshape(row_count * slot_count, features)
    collected = []
    for number in reversed(range(layers)):
        weights = (
            lax.all_gather(joint_weight[number].astype(jnp.bfloat16), "fsdp", axis=0, tiled=True),
            lax.all_gather(output_weight[number].astype(jnp.bfloat16), "fsdp", axis=0, tiled=True),
            lax.all_gather(expand_weight[number].astype(jnp.bfloat16), "fsdp", axis=0, tiled=True),
            lax.all_gather(shrink_weight[number].astype(jnp.bfloat16), "fsdp", axis=0, tiled=True),
            lax.all_gather(norm_gains[number].astype(jnp.bfloat16), "fsdp", axis=1, tiled=True),
            lax.all_gather(biases[number].astype(jnp.bfloat16), "fsdp", axis=1, tiled=True),
            lax.all_gather(hidden_bias[number].astype(jnp.bfloat16), "fsdp", axis=0, tiled=True),
        )
        grad_hidden, local_grads = block_backward(
            grad_hidden, segments, weights, stored_list[number]
        )
        grad_joint, grad_output, grad_expand, grad_shrink, gain_grads, bias_grads, inner_grad = (
            local_grads
        )
        shards = (
            lax.psum_scatter(grad_joint, "fsdp", scatter_dimension=0, tiled=True),
            lax.psum_scatter(grad_output, "fsdp", scatter_dimension=0, tiled=True),
            lax.psum_scatter(grad_expand, "fsdp", scatter_dimension=0, tiled=True),
            lax.psum_scatter(grad_shrink, "fsdp", scatter_dimension=0, tiled=True),
            lax.psum_scatter(gain_grads, "fsdp", scatter_dimension=1, tiled=True),
            lax.psum_scatter(bias_grads, "fsdp", scatter_dimension=1, tiled=True),
            lax.psum_scatter(inner_grad, "fsdp", scatter_dimension=0, tiled=True),
        )
        summed = (
            lax.psum(shards[0].astype(jnp.bfloat16), "dp").astype(jnp.float32),
            lax.psum(shards[1].astype(jnp.bfloat16), "dp").astype(jnp.float32),
            lax.psum(shards[2].astype(jnp.bfloat16), "dp").astype(jnp.float32),
            lax.psum(shards[3].astype(jnp.bfloat16), "dp").astype(jnp.float32),
            lax.psum(shards[4].astype(jnp.bfloat16), "dp").astype(jnp.float32),
            lax.psum(shards[5].astype(jnp.bfloat16), "dp").astype(jnp.float32),
            lax.psum(shards[6].astype(jnp.bfloat16), "dp").astype(jnp.float32),
        )
        collected.append(summed)
    collected = collected[::-1]
    input_gradient = grad_hidden.reshape(row_count, slot_count, features).astype(jnp.bfloat16)
    fsdp_count = lax.axis_size("fsdp")
    token_total = row_count * slot_count * lax.axis_size("dp") * fsdp_count
    root_scale = 1.0 / math.sqrt(token_total)
    stacked_grads = [
        jnp.stack([entry[index] for entry in collected]) * root_scale for index in range(7)
    ]
    matrices = (
        (stacked_grads[0], joint_weight, joint_rows, joint_columns),
        (stacked_grads[1], output_weight, output_rows, output_columns),
        (stacked_grads[2], expand_weight, expand_rows, expand_columns),
        (stacked_grads[3], shrink_weight, shrink_rows, shrink_columns),
    )
    partial_list = [factored_partials(item[0], item[1], item[2]) for item in matrices]
    vectors = (
        (stacked_grads[4], norm_gains, gain_moments),
        (stacked_grads[5], biases, bias_moments),
        (stacked_grads[6][:, None, :], hidden_bias[:, None, :], hidden_moments[:, None, :]),
    )
    vector_list = [vector_partials(item[0], item[2]) for item in vectors]
    vector_squares = jnp.concatenate(
        [jnp.sum(item[1] * item[1], axis=2) for item in vectors], axis=1
    )
    statistics = lax.psum(
        (
            partial_list[0][1],
            partial_list[1][1],
            partial_list[2][1],
            partial_list[3][1],
            jnp.stack([item[2] for item in partial_list], axis=1),
            jnp.stack([item[3] for item in partial_list], axis=1),
            vector_squares,
        ),
        "fsdp",
    )
    updates = []
    columns_list = []
    for index in range(4):
        gradient = matrices[index][0]
        total_rows = gradient.shape[1] * fsdp_count
        rows_next = partial_list[index][0]
        columns_next = DECAY_RATE * matrices[index][3] + (1.0 - DECAY_RATE) * (
            statistics[index] / total_rows
        )
        row_average = statistics[4][:, index] / total_rows
        estimate = rows_next[:, :, None] * columns_next[:, None, :] / row_average[:, None, None]
        updates.append(gradient * lax.rsqrt(estimate))
        columns_list.append(columns_next)
    matrix_squares = jnp.stack([jnp.sum(item * item, axis=(1, 2)) for item in updates], axis=1)
    vector_updates = jnp.concatenate(
        [jnp.sum(item[1] * item[1], axis=2) for item in vector_list], axis=1
    )
    norms = lax.psum((matrix_squares, vector_updates), "fsdp")
    matrix_next = []
    for index in range(4):
        gradient = matrices[index][0]
        entry_count = gradient.shape[1] * fsdp_count * gradient.shape[2]
        clip_ratio = jnp.sqrt(norms[0][:, index] / entry_count) / CLIP_LIMIT
        update = updates[index] / jnp.maximum(clip_ratio, 1.0)[:, None, None]
        stride = STEP_RATE * jnp.maximum(
            FLOOR_SCALE, jnp.sqrt(statistics[5][:, index] / entry_count)
        )
        matrix_next.append(matrices[index][1] - stride[:, None, None] * update)
    vector_next = []
    offset = 0
    for index in range(3):
        gradient = vectors[index][0]
        kinds = gradient.shape[1]
        entry_count = gradient.shape[2] * fsdp_count
        clip_ratio = jnp.sqrt(norms[1][:, offset : offset + kinds] / entry_count) / CLIP_LIMIT
        update = vector_list[index][1] / jnp.maximum(clip_ratio, 1.0)[:, :, None]
        stride = STEP_RATE * jnp.maximum(
            FLOOR_SCALE, jnp.sqrt(statistics[6][:, offset : offset + kinds] / entry_count)
        )
        vector_next.append(vectors[index][1] - stride[:, :, None] * update)
        offset = offset + kinds
    return (
        activations,
        input_gradient,
        stacked_grads[0],
        stacked_grads[1],
        stacked_grads[2],
        stacked_grads[3],
        stacked_grads[4],
        stacked_grads[5],
        stacked_grads[6],
        matrix_next[0],
        matrix_next[1],
        matrix_next[2],
        matrix_next[3],
        vector_next[0],
        vector_next[1],
        vector_next[2][:, 0, :],
        matrix_next[0].astype(jnp.bfloat16),
        matrix_next[1].astype(jnp.bfloat16),
        matrix_next[2].astype(jnp.bfloat16),
        matrix_next[3].astype(jnp.bfloat16),
        partial_list[0][0],
        columns_list[0],
        partial_list[1][0],
        columns_list[1],
        partial_list[2][0],
        columns_list[2],
        partial_list[3][0],
        columns_list[3],
        vector_list[0][0],
        vector_list[1][0],
        vector_list[2][0][:, 0, :],
    )


F32 = jnp.float32
BF = jnp.bfloat16
T = 512
D = 768


def nn(a, b):
    return lax.dot_general(a, b, (((1,), (0,)), ((), ())), preferred_element_type=F32)


def nt(a, b):
    return lax.dot_general(a, b, (((1,), (1,)), ((), ())), preferred_element_type=F32)


def rows_at(i, n):
    return pl.ds(pl.multiple_of(i * n, n), n)


def build_mask(seg_ref, bias_ref):
    row = seg_ref[...]
    wide = jnp.broadcast_to(row, (128, T)).T
    for j in range(T // 128):
        bias_ref[:, j * 128 : (j + 1) * 128] = jnp.where(
            wide == row[:, j * 128 : (j + 1) * 128], 0.0, MASK_VALUE
        ).astype(F32)


def joint_forward(xb, wa, vec, joint, tile=T):
    for b in range(3):
        @pl.loop(0, T // tile)
        def _(i, b=b):
            r = rows_at(i, tile)
            out = nn(xb[r, :], wa[b])
            if b == 0:
                out = out + vec[2:3, :]
            if b == 2:
                out = out + vec[3:4, :]
            joint[b, r, :] = out.astype(BF)


def head_masks():
    lane = lax.broadcasted_iota(jnp.int32, (1, 128), 1)
    return [
        jnp.where(lane < 64, 1.0, 0.0).astype(F32),
        jnp.where(lane >= 64, 1.0, 0.0).astype(F32),
    ]


def attend_forward_pair(p, joint, bias, ctx, logsum):
    lanes = pl.ds(pl.multiple_of(p * 128, 128), 128)
    masks = head_masks()
    q2 = joint[0, :, lanes]
    k2 = joint[1, :, lanes]
    vt = joint[2, :, lanes].T
    outs, sums = [], []
    for h in range(2):
        qm = q2 * (masks[h] * 0.125).astype(BF)
        st = nt(k2, qm) + bias[...]
        top = jnp.max(st, axis=0, keepdims=True)
        e = jnp.exp(st - top)
        total = jnp.sum(e, axis=0, keepdims=True)
        ct = nn(vt[64 * h : 64 * h + 64, :], e.astype(BF))
        outs.append(ct * (1.0 / total))
        sums.append(top + jnp.log(total))
    ctx[:, lanes] = jnp.concatenate(outs, axis=0).T.astype(BF)
    logsum[p] = jnp.concatenate(sums, axis=0)


def norm_parts(u):
    avg = jnp.mean(u, axis=-1, keepdims=True)
    c = u - avg
    var = jnp.mean(c * c, axis=-1, keepdims=True)
    inv = lax.rsqrt(var + NORM_EPSILON)
    return c * inv, inv


def out_forward(ctx, x, wo, vec, n1, r1, h, hb, tile=T):
    @pl.loop(0, T // tile)
    def _(i):
        r = rows_at(i, tile)
        u = nn(ctx[r, :], wo[...]) + vec[4:5, :] + x[r, :].astype(F32)
        n, inv = norm_parts(u)
        y = n * vec[0:1, :] + vec[5:6, :]
        n1[r, :] = n.astype(n1.dtype)
        r1[r, :] = jnp.broadcast_to(inv, (tile, 128))
        h[r, :] = y
        hb[r, :] = y.astype(BF)


def gelu_parts(z):
    a = jnp.abs(z)
    e = jnp.exp(z * z * -0.5)
    t = 1.0 / (1.0 + 0.23164189 * a)
    poly = t * (
        0.127414796 + t * (-0.142248368 + t * (0.7107068705 + t * (-0.7265760135 + t * 0.5307027145)))
    )
    tail = poly * e
    cdf = jnp.where(z >= 0.0, 1.0 - tail, tail)
    return z * cdf, cdf + z * (e * 0.3989422804014327)


def ffn_up(hb, we, vec, g, gp, b, tile=T):
    @pl.loop(0, T // tile)
    def _(i):
        r = rows_at(i, tile)
        z = nn(hb[r, :], we[b]) + vec[8 + b : 9 + b, :]
        act, der = gelu_parts(z)
        g[b, r, :] = act.astype(BF)
        gp[b, r, :] = der.astype(BF)


def ffn_down(g, ws, vec, h, n2, r2, x_out, xb_out, tile=T):
    @pl.loop(0, T // tile)
    def _(i):
        r = rows_at(i, tile)
        u = h[r, :] + vec[6:7, :]
        for b in range(4):
            u = u + nn(g[b, r, :], ws[b])
        n, inv = norm_parts(u)
        y = n * vec[1:2, :] + vec[7:8, :]
        n2[r, :] = n.astype(n2.dtype)
        r2[r, :] = jnp.broadcast_to(inv, (tile, 128))
        if x_out is not None:
            x_out[r, :] = y
        xb_out[r, :] = y.astype(BF)


def sum8(v):
    return jnp.sum(v.reshape(v.shape[0] // 8, 8, v.shape[1]), axis=0)


def norm_backward(dy, n, r, gain_row, du, dub, sums, rows, tile=256):
    def step(i, carry):
        s = rows_at(i, tile)
        g = dy[s, :].astype(F32)
        nv = n[s, :].astype(F32)
        inv = r[s, 0:1]
        e = g * gain_row
        m1 = jnp.mean(e, axis=-1, keepdims=True)
        m2 = jnp.mean(e * nv, axis=-1, keepdims=True)
        d = inv * (e - m1 - nv * m2)
        db = d.astype(BF)
        du[s, :] = d
        dub[s, :] = db
        return (
            carry[0] + sum8(g * nv),
            carry[1] + sum8(g),
            carry[2] + sum8(db.astype(F32)),
        )

    zero = jnp.zeros((8, D), F32)
    out = lax.fori_loop(0, T // tile, step, (zero, zero, zero))
    for k in range(3):
        sums[rows[k] : rows[k] + 1, :] = jnp.sum(out[k], axis=0, keepdims=True)


def transpose_into(src, dst, tile=128):
    @pl.loop(0, T // tile)
    def _(i):
        dst[:, rows_at(i, tile)] = src[rows_at(i, tile), :].T


def weight_grad(at, bmat, out, tile=256):
    @pl.loop(0, D // tile)
    def _(i):
        r = rows_at(i, tile)
        out[r, :] = nn(at[r, :], bmat[...]).astype(BF)


def ffn_back_block(dob, ws, gp, dz, sums, b, tile=T):
    def step(i, acc):
        r = rows_at(i, tile)
        v = (nt(dob[r, :], ws[b]) * gp[b, r, :].astype(F32)).astype(BF)
        dz[b, r, :] = v
        return acc + sum8(v.astype(F32))

    acc = lax.fori_loop(0, T // tile, step, jnp.zeros((8, D), F32))
    sums[8 + b : 9 + b, :] = jnp.sum(acc, axis=0, keepdims=True)


def ffn_back_input(dz, we, du, tile=T):
    @pl.loop(0, T // tile)
    def _(i):
        r = rows_at(i, tile)
        u = du[r, :]
        for b in range(4):
            u = u + nt(dz[b, r, :], we[b])
        du[r, :] = u


def context_back(dab, wo, dc, tile=T):
    @pl.loop(0, T // tile)
    def _(i):
        r = rows_at(i, tile)
        dc[r, :] = nt(dab[r, :], wo[...]).astype(BF)


def attend_backward_pair(p, joint, bias, logsum, ctx, dc, dj):
    lanes = pl.ds(pl.multiple_of(p * 128, 128), 128)
    masks = head_masks()
    q2 = joint[0, :, lanes]
    k2 = joint[1, :, lanes]
    v2 = joint[2, :, lanes]
    d2 = dc[:, lanes]
    kt = k2.T
    ls = logsum[p]
    both = d2.astype(F32) * ctx[:, lanes].astype(F32)
    high = both.astype(BF)
    low = (both - high.astype(F32)).astype(BF)
    pick = jnp.concatenate(masks + [jnp.zeros((6, 128), F32)], axis=0).astype(BF)
    delta = nt(pick, high) + nt(pick, low)
    dk = jnp.zeros((T, 128), F32)
    dv = jnp.zeros((T, 128), F32)
    dqt = []
    for h in range(2):
        qm = q2 * (masks[h] * 0.125).astype(BF)
        dm = d2 * masks[h].astype(BF)
        prob = jnp.exp(nt(k2, qm) + bias[...] - ls[h : h + 1, :])
        ds = (prob * (nt(v2, dm) - delta[h : h + 1, :])).astype(BF)
        dv = dv + nn(prob.astype(BF), dm)
        dk = dk + nn(ds, qm)
        dqt.append(nn(kt[64 * h : 64 * h + 64, :], ds))
    dj[0, :, lanes] = (jnp.concatenate(dqt, axis=0) * 0.125).T.astype(BF)
    dj[1, :, lanes] = dk.astype(BF)
    dj[2, :, lanes] = dv.astype(BF)


def input_back(dj, wa, du, dx, sums, tile=T):
    def step(i, carry):
        r = rows_at(i, tile)
        u = du[r, :]
        for b in range(3):
            u = u + nt(dj[b, r, :], wa[b])
        dx[r, :] = u.astype(dx.dtype)
        return (carry[0] + sum8(dj[0, r, :].astype(F32)), carry[1] + sum8(dj[2, r, :].astype(F32)))

    zero = jnp.zeros((8, D), F32)
    out = lax.fori_loop(0, T // tile, step, (zero, zero))
    sums[2:3, :] = jnp.sum(out[0], axis=0, keepdims=True)
    sums[3:4, :] = jnp.sum(out[1], axis=0, keepdims=True)


MESH = pl.DeviceIdType.MESH
PAIRS = 6
PIECE = 96
GROUPS = 6


def place():
    q = lax.axis_index("dp")
    f = lax.axis_index("fsdp")
    z = f // 2
    c = f % 2
    x_side = (q + 1 - 2 * (q % 2), f)
    y_side = ((q + 2) % 4, f)
    sibling = (q, f + 1 - 2 * c)
    planes = [(q, (f + 2 * k) % 8) for k in range(1, 4)]
    return q, z, c, x_side, y_side, sibling, planes


def greet(peers):
    barrier = pltpu.get_barrier_semaphore()
    for peer in peers:
        pl.semaphore_signal(barrier, inc=1, device_id=peer, device_id_type=MESH)
    pl.semaphore_wait(barrier, len(peers))


def hidden_piece(kind, b, zz, c, first, count):
    if kind < 2:
        start = 192 * zz + 96 * c + first
        return b, pl.ds(pl.multiple_of(start, 16), count)
    start = 384 * c + 96 * b + first
    return zz, pl.ds(pl.multiple_of(start, 16), count)


PARTS = [(g, first, 32) for g in range(6) for first in (0, 32, 64)]


class Gather:
    def __init__(self, whole, sbuf, sems):
        self.whole, self.sbuf, self.sems = whole, sbuf, sems
        q, z, c, self.x_side, self.y_side, self.sibling, self.planes = place()
        self.q, self.z, self.c = q, z, c
        self.qx = q + 1 - 2 * (q % 2)
        self.qy = (q + 2) % 4
        self.qd = (self.qx + 2) % 4
        self.others = [(z + k) % 4 for k in range(1, 4)]

    def spot(self, k, b, zz, cols=None):
        g, first, count = PARTS[k]
        lead, rows = hidden_piece(g % 3, b, zz, self.c, first, count)
        if cols is None:
            return self.whole.at[g, lead, rows, :]
        return self.whole.at[g, lead, rows, pl.ds(384 * cols, 384)]

    def send(self, k, src, dst, slot, peer):
        pltpu.make_async_remote_copy(
            src_ref=src, dst_ref=dst, send_sem=self.sems.at[k, slot], recv_sem=self.sems.at[k, slot + 1],
            device_id=peer, device_id_type=MESH,
        ).start()

    def total(self, k, slot, rows, cols=768):
        lead = self.whole.at[0, 0, pl.ds(0, rows), pl.ds(0, cols)] if rows <= 768 else self.whole.at[0, pl.ds(0, rows // 768)]
        pltpu.make_async_copy(lead, lead, self.sems.at[k, slot]).wait()

    def z_send(self, k):
        g, first, count = PARTS[k]
        src = self.sbuf.at[g, self.q, pl.ds(first, count), :]
        for peer in self.planes:
            self.send(k, src, self.spot(k, self.q, self.z), 0, peer)
        for b in range(4):
            mine = self.sbuf.at[g, b, pl.ds(first, count), :]
            self.send(k, mine, self.spot(k, b, self.z), 10, self.sibling)
            pltpu.make_async_copy(mine, self.spot(k, b, self.z), self.sems.at[k, 12]).start()

    def xy_send(self, k):
        count = PARTS[k][2]
        self.total(k, 1, 3 * count)
        for zz in self.others:
            spot = self.spot(k, self.q, zz)
            self.send(k, spot, spot, 2, self.x_side)
            self.send(k, spot, spot, 4, self.y_side)
        for zz in self.others:
            spot = self.spot(k, self.q, zz)
            self.send(k, spot, spot, 10, self.sibling)

    def diagonal_send(self, k):
        count = PARTS[k][2]
        self.total(k, 3, 3 * count)
        self.total(k, 5, 3 * count)
        for zz in self.others:
            spot = self.spot(k, self.qy, zz, 0)
            self.send(k, spot, spot, 6, self.x_side)
            spot = self.spot(k, self.qx, zz, 1)
            self.send(k, spot, spot, 8, self.y_side)
        for zz in self.others:
            for b in (self.qx, self.qy):
                spot = self.spot(k, b, zz)
                self.send(k, spot, spot, 10, self.sibling)

    def last_send(self, k):
        count = PARTS[k][2]
        self.total(k, 7, 3 * count, 384)
        self.total(k, 9, 3 * count, 384)
        for zz in self.others:
            spot = self.spot(k, self.qd, zz)
            self.send(k, spot, spot, 10, self.sibling)

    def finish(self, k):
        count = PARTS[k][2]
        self.total(k, 11, 16 * count)
        self.total(k, 12, 4 * count)

    def drain(self, k):
        count = PARTS[k][2]
        self.total(k, 0, 3 * count)
        self.total(k, 2, 3 * count)
        self.total(k, 4, 3 * count)
        self.total(k, 6, 3 * count, 384)
        self.total(k, 8, 3 * count, 384)
        self.total(k, 10, 16 * count)


UNIT_TIMES = (("joint", 2.1),) + tuple((f"att{p}", 1.3) for p in range(6)) + (("out", 1.0),) + tuple(
    (f"up{b}", 1.0) for b in range(4)
) + (("down", 2.8),)


SPREAD = 0.95


def pack_vectors(ref, gains, biases, hidden, fill):
    ref[...] = jnp.full(ref.shape, fill, F32)
    for layer in range(2):
        ref[layer, 0:2, 0:96] = gains[layer]
        for r in range(6):
            ref[layer, 2 + r : 3 + r, 0:96] = biases[r, layer : layer + 1, :]
        for k in range(3):
            ref[layer, 8 + k : 9 + k, :] = hidden[layer : layer + 1, 128 * k : 128 * k + 128]


def forward_plan():
    count = len(PARTS)
    steps = []
    for i in range(count + 3):
        for lag, kind in enumerate(("xy", "dg", "last", "fin")):
            if 0 <= i - lag < count and (kind != "fin" or sum(PARTS[i - lag][1:]) == 96):
                steps.append((kind, i - lag))
    units = [(layer, name, cost) for layer in range(2) for name, cost in UNIT_TIMES]
    last = {PARTS[k][0]: k for k in range(count)}
    need = {"joint": 0, "up0": 1, "down": 2}
    order, finished, at, budget = [], set(), 0, 0.0
    for step in steps:
        order.append(step)
        if step[0] == "fin":
            finished.add(step[1])
        budget += SPREAD
        while at < len(units):
            layer, name, cost = units[at]
            if name in need and last[3 * layer + need[name]] not in finished:
                budget = min(budget, 0.0)
                break
            if cost > budget + 0.5:
                break
            budget -= cost
            order.append(("run", layer, name))
            at += 1
    return order + [("run", layer, name) for layer, name, cost in units[at:]]


def forward_kernel(
    tokens, seg, gains, biases, hidden, joint_w, output_w, expand_w, shrink_w,
    whole, vec_out, x_saved, j_saved, c_saved, l_saved, n1_saved, r1_saved, g_saved, gp_saved, n2_saved, r2_saved, final, squares,
    stage, sbuf, wv, bias, x1, h, hb, xb, joint, ctx, logsum, n1, r1, g, gp, n2, r2, vg, vec, vec_now,
    sems, stage_sems, wv_sems, vec_sems, out_sems,
):
    masters = (joint_w, output_w, expand_w, shrink_w)
    gather = Gather(whole, sbuf, sems)
    q, z, c = gather.q, gather.z, gather.c

    def stage_copies(grp):
        layer, kind = divmod(grp, 3)
        slot = grp % 2
        out = []
        for b in range(4):
            if kind == 0:
                src = output_w.at[layer] if b == 3 else joint_w.at[layer, :, pl.ds(768 * b, 768)]
            elif kind == 1:
                src = expand_w.at[layer, :, pl.ds(768 * b, 768)]
            else:
                src = shrink_w.at[layer, pl.ds(96 * b, 96), :]
            out.append(pltpu.make_async_copy(src, stage.at[slot, b], stage_sems.at[slot, b]))
        return out

    def take(grp):
        layer, kind = divmod(grp, 3)
        slot = grp % 2
        for cp in stage_copies(grp):
            cp.wait()
        sums = []
        for b in range(4):
            value = stage[slot, b]
            sbuf[grp, b] = value.astype(BF)
            sums.append(jnp.sum(value * value, axis=0, keepdims=True))
        if kind == 0:
            squares[4 * layer : 4 * layer + 1, :] = sums[0] + sums[1] + sums[2]
            squares[4 * layer + 1 : 4 * layer + 2, :] = sums[3]
        else:
            row = 4 * layer + 1 + kind
            squares[row : row + 1, :] = sums[0] + sums[1] + sums[2] + sums[3]
        if grp + 2 < GROUPS:
            for cp in stage_copies(grp + 2):
                cp.start()

    for grp in range(2):
        for cp in stage_copies(grp):
            cp.start()
    take(0)
    greet([gather.x_side, gather.y_side, gather.sibling] + gather.planes)
    gather.z_send(0)

    pack_vectors(vec_now, gains, biases, hidden, 0.0)
    vg[z, c] = vec_now[...].reshape(32, 128)

    def vec_copy(zz, peer, slot):
        return pltpu.make_async_remote_copy(
            src_ref=vg.at[zz, c], dst_ref=vg.at[zz, c], send_sem=vec_sems.at[2 * slot], recv_sem=vec_sems.at[2 * slot + 1],
            device_id=peer, device_id_type=MESH,
        )

    def vec_total(slot, count):
        ref = vg.at[0, pl.ds(0, 1)] if count == 1 else (vg.at[0, pl.ds(0, 2)] if count == 2 else vg.at[pl.ds(0, 2)])
        pltpu.make_async_copy(ref, ref, vec_sems.at[slot]).wait()

    for k, peer in enumerate(gather.planes):
        vec_copy(z, peer, k).start()
    take(1)
    gather.z_send(1)
    take(2)
    take(3)
    for k in range(3):
        vec_copy((z + 3 - k) % 4, gather.planes[0], k).wait_recv()
    for zz in range(4):
        vec_copy(zz, gather.sibling, 3 + zz).start()
    take(4)
    take(5)
    build_mask(seg, bias)
    for zz in range(4):
        vec_copy(zz, gather.sibling, 3 + zz).wait_recv()
    lane = lax.broadcasted_iota(jnp.int32, (128, 768), 1)
    spot = lax.broadcasted_iota(jnp.int32, (128, 768), 0)
    for layer in range(2):
        acc = jnp.zeros((8, 768), F32)
        for m in range(8):
            pick = jnp.where((lane == spot + 96 * m) & (spot < 96), 1.0, 0.0).astype(BF)
            acc = acc + nn(vg[m // 2, m % 2, 16 * layer : 16 * layer + 8, :].astype(BF), pick)
            for k in range(3):
                row = vg[m // 2, m % 2, 16 * layer + 8 + k : 16 * layer + 9 + k, :].astype(BF).astype(F32)
                start = 384 * (m % 2) + 128 * k
                vec[layer, 8 + m // 2 : 9 + m // 2, start : start + 128] = row
        vec[layer, 0:8, :] = acc
        vec[layer, 12:16, :] = jnp.zeros((4, 768), F32)

    started = []

    def save(src, dst):
        n = len(started)
        cp = pltpu.make_async_copy(src, dst, out_sems.at[n])
        cp.start()
        started.append(cp)

    def load(grp):
        return pltpu.make_async_copy(whole.at[grp], wv.at[grp % 3], wv_sems.at[grp % 3])

    def event(kind, k):
        if kind == "xy":
            gather.xy_send(k)
            if k + 2 < len(PARTS):
                gather.z_send(k + 2)
        elif kind == "dg":
            gather.diagonal_send(k)
        elif kind == "last":
            gather.last_send(k)
        elif kind == "fin":
            grp = PARTS[k][0]
            for part in range(len(PARTS)):
                if PARTS[part][0] == grp:
                    gather.finish(part)
            load(grp).start()

    order = forward_plan()
    pos = 0
    while pos < len(order):
        item = order[pos]
        if item[0] != "run":
            event(*item)
            pos += 1
            continue
        _, layer, name = item
        vl = vec.at[layer]
        x_in = tokens if layer == 0 else x1
        xb_in = tokens if layer == 0 else xb
        if name == "joint":
            load(3 * layer).wait()
            joint_forward(xb_in, wv.at[0], vl, joint.at[layer])
            save(joint.at[layer], j_saved.at[layer])
        elif name.startswith("att"):
            hooks, first = {}, int(name[3:])
            p, look = first, pos
            while True:
                it = order[look]
                if it[0] == "run":
                    if not it[2].startswith("att"):
                        break
                    p = int(it[2][3:]) + 1
                else:
                    hooks.setdefault(p, []).append(it)
                look += 1
            tail = hooks.pop(6, [])

            @pl.loop(0, PAIRS)
            def _(p):
                for at, items in hooks.items():
                    @pl.when(p == at)
                    def _():
                        for it in items:
                            event(*it)
                attend_forward_pair(p, joint.at[layer], bias, ctx.at[layer], logsum.at[layer])

            for it in tail:
                event(*it)
            save(ctx.at[layer], c_saved.at[layer])
            save(logsum.at[layer], l_saved.at[layer])
            pos = look
            continue
        elif name == "out":
            out_forward(ctx.at[layer], x_in, wv.at[0, 3], vl, n1.at[layer], r1.at[layer], h, hb)
            save(n1.at[layer], n1_saved.at[layer])
            save(r1.at[layer], r1_saved.at[layer])
        elif name.startswith("up"):
            b = int(name[2:])
            if b == 0:
                load(3 * layer + 1).wait()
            ffn_up(hb, wv.at[1], vl, g.at[layer], gp.at[layer], b)
            if b == 3:
                save(g.at[layer], g_saved.at[layer])
                save(gp.at[layer], gp_saved.at[layer])
        else:
            load(3 * layer + 2).wait()
            ffn_down(g.at[layer], wv.at[2], vl, h, n2.at[layer], r2.at[layer], x1 if layer == 0 else None, xb if layer == 0 else hb)
            save(n2.at[layer], n2_saved.at[layer])
            save(r2.at[layer], r2_saved.at[layer])
            if layer == 0:
                save(xb, x_saved)
            else:
                save(hb, final)
        pos += 1
    save(vec, vec_out)
    for k in range(len(PARTS)):
        gather.drain(k)
    for k in range(3):
        vec_copy(z, gather.planes[k], k).wait_send()
    for zz in range(4):
        vec_copy(zz, gather.sibling, 3 + zz).wait_send()
    for cp in started:
        cp.wait()


def forward_call(tokens, seg, gains, biases, hidden, joint_w, output_w, expand_w, shrink_w):
    sd = jax.ShapeDtypeStruct
    any_spec = pl.BlockSpec(memory_space=pl.ANY)
    vm = pl.BlockSpec(memory_space=pltpu.VMEM)
    V = pltpu.VMEM
    saved = [
        sd((6, 4, 768, 768), BF),
        sd((2, 16, 768), F32),
        sd((T, D), BF),
        sd((2, 3, T, D), BF),
        sd((2, T, D), BF),
        sd((2, 6, 2, T), F32),
        sd((2, T, D), BF),
        sd((2, T, 128), F32),
        sd((2, 4, T, D), BF),
        sd((2, 4, T, D), BF),
        sd((2, T, D), BF),
        sd((2, T, 128), F32),
        sd((T, D), BF),
        sd((8, 768), F32),
    ]
    scratch = [
        V((2, 4, 96, 768), F32),
        V((6, 4, 96, 768), BF),
        V((3, 4, 768, 768), BF),
        V((T, T), F32),
        V((T, D), F32),
        V((T, D), F32),
        V((T, D), BF),
        V((T, D), BF),
        V((2, 3, T, D), BF),
        V((2, T, D), BF),
        V((2, 6, 2, T), F32),
        V((2, T, D), BF),
        V((2, T, 128), F32),
        V((2, 4, T, D), BF),
        V((2, 4, T, D), BF),
        V((2, T, D), BF),
        V((2, T, 128), F32),
        V((4, 2, 32, 128), F32),
        V((2, 16, 768), F32),
        V((2, 16, 128), F32),
        pltpu.SemaphoreType.DMA((len(PARTS), 13)),
        pltpu.SemaphoreType.DMA((2, 4)),
        pltpu.SemaphoreType.DMA((3,)),
        pltpu.SemaphoreType.DMA((14,)),
        pltpu.SemaphoreType.DMA((24,)),
    ]
    return pl.pallas_call(
        forward_kernel,
        out_shape=saved,
        in_specs=[vm] * 5 + [any_spec] * 4,
        out_specs=[any_spec] * 13 + [vm],
        scratch_shapes=scratch,
        compiler_params=pltpu.CompilerParams(
            collective_id=0, has_side_effects=True, vmem_limit_bytes=62 << 20
        ),
        name="forward",
    )(tokens, seg, gains, biases, hidden, joint_w, output_w, expand_w, shrink_w)


ROOT_SCALE = 1.0 / math.sqrt(32 * T)

BACK_UNITS = (
    (("ln2", 1.2),)
    + tuple((f"s{i}", 1.3) for i in range(4))
    + tuple((f"dz{i}", 1.0) for i in range(4))
    + (("ht", 0.9), ("e0", 1.5), ("e1", 1.5), ("dh", 2.8), ("ln1", 1.2), ("o", 2.4))
    + tuple((f"att{p}", 1.75) for p in range(6))
    + (("xt", 0.5), ("q0", 1.5), ("q1", 1.5), ("dx", 2.4))
)
GROUP_OF = {"s": 0, "e": 1, "o": 2, "q": 2}
PARTS_OF = {"s0": (0,), "s1": (1,), "s2": (2,), "s3": (3,), "e0": (0, 1), "e1": (2, 3), "q0": (0, 1), "q1": (2, 3)}


LINK, LATENCY, STEP, COMPUTE = 3.2, 1.5, 0.4, 1.0


def backward_plan():
    now, xy_free, z_free, core_free = 0.0, 0.0, 0.0, 0.0
    pending, order, summed = [], [], set()

    def emit(entry):
        nonlocal now, xy_free, z_free
        ready, name, t, zz = entry
        now = max(now, ready) + STEP
        order.append((name, t, zz))
        if name == "xy1":
            xy_free = max(xy_free, now) + LINK
            pending.append((xy_free + LATENCY, "xy2", t, zz))
        elif name == "xy2":
            xy_free = max(xy_free, now) + LINK / 2
            pending.append((xy_free + LATENCY, "z", t, zz))
        elif name == "z":
            z_free = max(z_free, now) + LINK
            if sum(1 for o in order if o[0] == "z" and o[1] == t) == 4:
                pending.append((z_free + LATENCY, "sum", t, 0))
        elif name == "sum":
            summed.add(t)
            xy_free = max(xy_free, now) + LINK
            pending.append((xy_free + LATENCY, "ag", t, 0))
        elif name == "ag":
            xy_free = max(xy_free, now) + LINK / 2
            pending.append((xy_free + LATENCY, "fin", t, 0))
        elif name == "fin":
            pending.append((now, "stat", t, 0))
        elif name == "stat":
            now += 1.0
        elif name == "vec" and zz < 4:
            pending.append((now + 2.5, "vec", t, zz + 1))

    emitted = set()

    def force(name, t, zz):
        if t < 0 or (name, t, zz) in emitted:
            return
        for entry in list(pending):
            if entry[1:] == (name, t, zz):
                pending.remove(entry)
                settle(entry)
                return
        force({"xy2": "xy1", "z": "xy2"}[name], t, zz)
        force(name, t, zz)

    def settle(entry):
        name, t, zz = entry[1:]
        emitted.add((name, t, zz))
        after = {"xy1": "xy2", "xy2": "z"}.get(name)
        if after:
            force(after, t - 1, zz)
        emit(entry)

    def step(limit):
        pending.sort()
        if pending and pending[0][0] <= limit:
            settle(pending.pop(0))
            return True
        return False

    for layer in (1, 0):
        for name, cost in BACK_UNITS:
            while step(now):
                pass
            if name[0] in GROUP_OF and name != "ln2":
                t = 3 * (1 - layer) + GROUP_OF[name[0]]
                while t >= 3 and t - 3 not in summed:
                    step(1e9)
            for zz in PARTS_OF.get(name, ()):
                force("xy1", t - 1, zz)
            order.append(("run", layer, name))
            now += cost * COMPUTE
            for zz in PARTS_OF.get(name, ()):
                core_free = max(core_free, now) + 1.0
                pending.append((core_free + LATENCY, "xy1", 3 * (1 - layer) + GROUP_OF[name[0]], zz))
    pending.append((now, "vec", 0, 0))
    while step(1e9):
        pass
    return order


class Reduce:
    def __init__(self, gb, rc, rx1, ry1, rx2, ry2, rz, fin, sems, group_sems, credits):
        self.gb, self.rc, self.rx1, self.ry1, self.rx2, self.ry2, self.rz, self.fin = gb, rc, rx1, ry1, rx2, ry2, rz, fin
        self.sems, self.group_sems, self.credits = sems, group_sems, credits
        q, z, c, self.x_side, self.y_side, self.sibling, self.planes = place()
        self.q, self.z, self.c = q, z, c
        self.ax, self.ay = q % 2, q // 2

    def send(self, src, dst, sem, peer):
        pltpu.make_async_remote_copy(
            src_ref=src, dst_ref=dst, send_sem=sem[0], recv_sem=sem[1], device_id=peer, device_id_type=MESH
        ).start()

    def pair(self, t, zz, slot):
        return self.sems.at[4 * t + zz, 2 * slot], self.sems.at[4 * t + zz, 2 * slot + 1]

    def group_pair(self, t, slot):
        return self.group_sems.at[t, 2 * slot], self.group_sems.at[t, 2 * slot + 1]

    def wait(self, ref, sem):
        pltpu.make_async_copy(ref, ref, sem).wait()

    def credit_wait(self, t, phase, zz):
        if t > 0:
            pl.semaphore_wait(self.credits.at[phase, zz], 1)

    def credit_give(self, t, phase, zz, peer):
        if t < 5:
            pl.semaphore_signal(self.credits.at[phase, zz], inc=1, device_id=peer, device_id_type=MESH)

    def core_send(self, t, zz):
        self.credit_wait(t, 0, zz)
        self.send(self.gb.at[t % 3, :, :, zz, 1 - self.c], self.rc.at[zz], self.pair(t, zz, 0), self.sibling)

    def add(self, ref, other):
        ref[...] = (ref[...].astype(F32) + other[...].astype(F32)).astype(BF)

    def xy1(self, t, zz):
        gb, c = self.gb.at[t % 3], self.c
        self.wait(self.rc.at[0], self.pair(t, zz, 0)[1])
        for by in range(2):
            for bx in range(2):
                self.add(gb.at[by, bx, zz, c], self.rc.at[zz, by, bx])
        self.credit_give(t, 0, zz, self.sibling)
        self.credit_wait(t, 1, zz)
        self.send(gb.at[:, 1 - self.ax, zz, c, pl.ds(0, 48)], self.rx1.at[zz], self.pair(t, zz, 1), self.x_side)
        self.credit_wait(t, 2, zz)
        self.send(gb.at[1 - self.ay, :, zz, c, pl.ds(48, 48)], self.ry1.at[zz], self.pair(t, zz, 2), self.y_side)

    def xy2(self, t, zz):
        gb, c = self.gb.at[t % 3], self.c
        self.wait(self.rx1.at[0], self.pair(t, zz, 1)[1])
        self.wait(self.ry1.at[0], self.pair(t, zz, 2)[1])
        for k in range(2):
            self.add(gb.at[k, self.ax, zz, c, pl.ds(0, 48)], self.rx1.at[zz, k])
            self.add(gb.at[self.ay, k, zz, c, pl.ds(48, 48)], self.ry1.at[zz, k])
        self.credit_give(t, 1, zz, self.x_side)
        self.credit_give(t, 2, zz, self.y_side)
        self.credit_wait(t, 3, zz)
        self.send(gb.at[self.ay, 1 - self.ax, zz, c, pl.ds(48, 48)], self.rx2.at[zz], self.pair(t, zz, 3), self.x_side)
        self.credit_wait(t, 4, zz)
        self.send(gb.at[1 - self.ay, self.ax, zz, c, pl.ds(0, 48)], self.ry2.at[zz], self.pair(t, zz, 4), self.y_side)

    def z_send(self, t, zz):
        gb, c = self.gb.at[t % 3], self.c
        self.wait(self.rx2.at[0], self.pair(t, zz, 3)[1])
        self.wait(self.ry2.at[0], self.pair(t, zz, 4)[1])
        self.add(gb.at[self.ay, self.ax, zz, c, pl.ds(48, 48)], self.rx2.at[zz])
        self.add(gb.at[self.ay, self.ax, zz, c, pl.ds(0, 48)], self.ry2.at[zz])
        self.credit_give(t, 3, zz, self.x_side)
        self.credit_give(t, 4, zz, self.y_side)

        @pl.when(self.z != zz)
        def _():
            self.send(
                gb.at[self.ay, self.ax, zz, c], self.rz.at[t, (self.z + 3 - zz) % 4], self.group_pair(t, 0),
                (self.q, 2 * zz + c),
            )

    def total(self, t):
        gb, c = self.gb.at[t % 3], self.c
        self.wait(self.rz.at[0], self.group_pair(t, 0)[1])
        own = gb[self.ay, self.ax, self.z, c].astype(F32)
        for k in range(3):
            own = own + self.rz[t, k].astype(F32)
        self.fin[t, self.q] = own.astype(BF)
        spot = self.fin.at[t, self.q]
        self.send(spot, spot, self.group_pair(t, 1), self.x_side)
        self.send(spot, spot, self.group_pair(t, 2), self.y_side)

    def share(self, t):
        self.wait(self.fin.at[0, 0], self.group_pair(t, 1)[1])
        self.wait(self.fin.at[0, 0], self.group_pair(t, 2)[1])
        qx = self.q + 1 - 2 * self.ax
        qy = (self.q + 2) % 4
        spot = self.fin.at[t, qy, pl.ds(0, 48)]
        self.send(spot, spot, self.group_pair(t, 3), self.x_side)
        spot = self.fin.at[t, qx, pl.ds(48, 48)]
        self.send(spot, spot, self.group_pair(t, 4), self.y_side)

    def finish(self, t):
        self.wait(self.fin.at[0, 0, pl.ds(0, 48)], self.group_pair(t, 3)[1])
        self.wait(self.fin.at[0, 0, pl.ds(0, 48)], self.group_pair(t, 4)[1])

    def drain(self, t):
        for zz in range(4):
            self.wait(self.rc.at[0], self.pair(t, zz, 0)[0])
            self.wait(self.rx1.at[0], self.pair(t, zz, 1)[0])
            self.wait(self.ry1.at[0], self.pair(t, zz, 2)[0])
            self.wait(self.rx2.at[0], self.pair(t, zz, 3)[0])
            self.wait(self.ry2.at[0], self.pair(t, zz, 4)[0])
        self.wait(self.rz.at[0], self.group_pair(t, 0)[0])

    def drain_share(self, t):
        self.wait(self.fin.at[0, 0], self.group_pair(t, 1)[0])
        self.wait(self.fin.at[0, 0], self.group_pair(t, 2)[0])
        self.wait(self.fin.at[0, 0, pl.ds(0, 48)], self.group_pair(t, 3)[0])
        self.wait(self.fin.at[0, 0, pl.ds(0, 48)], self.group_pair(t, 4)[0])


def backward_kernel(
    cot, seg, vec, squares, joint_rows, output_rows, expand_rows, shrink_rows,
    joint_columns, output_columns, expand_columns, shrink_columns, gains, biases, hidden, gain_old, bias_old, hidden_old,
    tokens, x_saved, whole, j_saved, c_saved, l_saved, n1_saved, r1_saved, g_saved, gp_saved, n2_saved, r2_saved,
    fin, grad_in, rows_new, columns_new, column_scale, vec_grad, vec_scale,
    gb, rc, rx1, ry1, rx2, ry2, rz, wv, g, dz, dj, ctx, n1, n2, r1, r2, logsum, xb, dob, at, hb, bias, du, sums, vr, va,
    row_cols, pay, pay_in, pay_z, pay_sum, columns_old, vec_now, vec_old,
    sems, group_sems, credits, load_sems, vec_sems, pay_sems,
):
    red = Reduce(gb, rc, rx1, ry1, rx2, ry2, rz, fin, sems, group_sems, credits)
    q, z, c = red.q, red.z, red.c
    sources = {
        "n2": (n2_saved, n2), "r2": (r2_saved, r2), "g": (g_saved, g), "dz": (gp_saved, dz), "n1": (n1_saved, n1),
        "r1": (r1_saved, r1), "ctx": (c_saved, ctx), "dj": (j_saved, dj), "logsum": (l_saved, logsum), "xb": (None, xb),
    }
    names = list(sources)

    def load(name, layer):
        src, dst = sources[name]
        if name == "xb":
            src = x_saved if layer == 1 else tokens
        else:
            src = src.at[layer]
        return pltpu.make_async_copy(src, dst, load_sems.at[names.index(name)])

    def weights(t):
        layer, kind = 1 - t // 3, (2, 1, 0)[t % 3]
        return pltpu.make_async_copy(whole.at[3 * layer + kind], wv.at[t % 2], load_sems.at[10 + t % 2])

    def need(layer, *which):
        for name in which:
            load(name, layer).wait()

    def release(layer, *which):
        if layer == 1:
            for name in which:
                load(name, 0).start()

    def next_weights(t):
        if t + 2 < 6:
            weights(t + 2).start()

    for name in ("n2", "r2", "g"):
        load(name, 1).start()
    weights(0).start()
    load("dz", 1).start()
    weights(1).start()
    for name in ("n1", "r1", "ctx", "dj", "logsum", "xb"):
        load(name, 1).start()
    build_mask(seg, bias)
    sums[...] = jnp.zeros_like(sums)
    greet([red.x_side, red.y_side, red.sibling] + red.planes)

    def blocks_pair(slot, b, pair, left):
        out = nn(at[pl.ds(384 * pair, 384), :], left).astype(BF)
        gb[slot, b // 2, b % 2, pl.ds(2 * pair, 2)] = out.reshape(2, 2, 96, 768)

    def unit(layer, name):
        base = 3 * (1 - layer)
        vl, sl = vec.at[layer], sums.at[layer]
        if name == "ln2":
            need(layer, "n2", "r2")
            norm_backward(cot if layer == 1 else du, n2, r2, vl[1:2, :], du, dob, sl, (1, 7, 6))
            release(layer, "n2", "r2")
        elif name[0] == "s":
            zz = int(name[1])
            if zz == 0:
                need(layer, "g")
                if base >= 3:
                    red.drain(base - 3)
            transpose_into(g.at[zz], at)
            for cc in range(2):
                out = nn(at[pl.ds(384 * cc, 384), :], dob[...]).astype(BF)
                gb[base % 3, :, :, zz, cc] = out.reshape(2, 2, 96, 768)
            red.core_send(base, zz)
            if zz == 3:
                release(layer, "g")
        elif name.startswith("dz"):
            b = int(name[2])
            if b == 0:
                need(layer, "dz")
                weights(base).wait()
            ffn_back_block(dob, wv.at[base % 2], dz, dz, sl, b)
            if b == 3:
                next_weights(base)
        elif name == "ht":
            need(layer, "n1", "r1")
            hb[...] = (n1[...].astype(F32) * vl[0:1, :] + vl[5:6, :]).astype(BF)
            transpose_into(hb, at)
        elif name[0] == "e":
            pair = int(name[1])
            if pair == 0 and base >= 3:
                red.drain(base - 2)
            for b in range(4):
                blocks_pair((base + 1) % 3, b, pair, dz[b])
            for zz in (2 * pair, 2 * pair + 1):
                red.core_send(base + 1, zz)
        elif name == "dh":
            weights(base + 1).wait()
            ffn_back_input(dz, wv.at[(base + 1) % 2], du)
            release(layer, "dz")
            next_weights(base + 1)
        elif name == "ln1":
            norm_backward(du, n1, r1, vl[0:1, :], du, dob, sl, (0, 5, 4))
            release(layer, "n1", "r1")
        elif name == "o":
            need(layer, "ctx")
            weights(base + 2).wait()
            if base >= 3:
                red.drain(base - 1)
            transpose_into(ctx, at)
            for pair in range(2):
                blocks_pair((base + 2) % 3, 3, pair, dob[...])
            context_back(dob, wv.at[(base + 2) % 2, 3], hb)
        elif name == "xt":
            need(layer, "xb")
            transpose_into(xb, at)
            release(layer, "xb", "logsum", "ctx")
        elif name[0] == "q":
            pair = int(name[1])
            for b in range(3):
                blocks_pair((base + 2) % 3, b, pair, dj[b])
            for zz in (2 * pair, 2 * pair + 1):
                red.core_send(base + 2, zz)
        elif name == "dx":
            input_back(dj, wv.at[(base + 2) % 2], du, du, sl)
            if layer == 0:
                grad_in[...] = du[...].astype(BF)
            release(layer, "dj")
            next_weights(base + 2)

    def event(name, t, zz):
        if name == "xy1":
            red.xy1(t, zz)
        elif name == "xy2":
            red.xy2(t, zz)
        elif name == "z":
            red.z_send(t, zz)
        elif name == "sum":
            red.total(t)
        elif name == "ag":
            red.share(t)
        elif name == "fin":
            red.finish(t)
        elif name == "stat":
            statistics(t)
        else:
            vec_event(zz)

    def vec_copy(src, dst, k, peer):
        return pltpu.make_async_remote_copy(
            src_ref=src, dst_ref=dst, send_sem=vec_sems.at[2 * k], recv_sem=vec_sems.at[2 * k + 1],
            device_id=peer, device_id_type=MESH,
        )

    hops = ((sums, red.sibling), (va.at[0], red.x_side), (va.at[1], red.y_side))

    def vec_event(k):
        if 1 <= k <= 3:
            src, peer = hops[k - 1]
            vec_copy(src, vr.at[k - 1], k - 1, peer).wait()
            va[k - 1] = src[...] + vr[k - 1]
        if k <= 2:
            src, peer = hops[k]
            vec_copy(src, vr.at[k], k, peer).start()
        elif k == 3:
            for j, peer in enumerate(red.planes):
                vec_copy(va.at[2], vr.at[3 + j], 3 + j, peer).start()
        else:
            for j, peer in enumerate(red.planes):
                vec_copy(va.at[2], vr.at[3 + j], 3 + j, peer).wait()
            vec_grads(plane_sum(va[2], [vr[3], vr[4], vr[5]]))

    def plane_sum(own, others):
        acc = jnp.zeros(own.shape, F32)
        for plane in range(4):
            part = jnp.where(z == plane, own, 0.0)
            for k in range(3):
                part = jnp.where((z + 3 - k) % 4 == plane, others[k], part)
            acc = acc + part
        return acc

    f = 2 * z + c

    def vec_grads(total):
        down = lax.broadcasted_iota(jnp.int32, (768, 128), 0)
        across = lax.broadcasted_iota(jnp.int32, (768, 128), 1)
        pick = jnp.where((down == across + 96 * f) & (across < 96), 1.0, 0.0).astype(F32)
        for layer in range(2):
            sums[layer] = total[layer] * ROOT_SCALE
            mine = lax.dot_general(
                sums[layer, 0:8, :], pick, (((1,), (0,)), ((), ())), precision=lax.Precision.HIGHEST, preferred_element_type=F32
            )
            vec_grad[layer] = jnp.zeros((16, 128), F32)
            vec_grad[layer, 0:8, :] = mine
            for k in range(3):
                part = jnp.zeros((1, 128), F32)
                for zz in range(4):
                    for cc in range(2):
                        here = sums[layer, 8 + zz : 9 + zz, 384 * cc + 128 * k : 384 * cc + 128 * k + 128]
                        part = jnp.where(f == 2 * zz + cc, here, part)
                vec_grad[layer, 8 + k : 9 + k, :] = part

    def all_sum(v):
        return jnp.sum(jnp.sum(v, axis=1, keepdims=True), axis=0, keepdims=True)

    lane = lax.broadcasted_iota(jnp.int32, (1, 768), 1)
    lane_c = lax.broadcasted_iota(jnp.int32, (128, 128), 1)

    def row_column(layer, chunk):
        return row_cols[:, 6 * layer + chunk : 6 * layer + chunk + 1]

    def set_row_column(layer, chunk, value):
        if value.shape[0] < 128:
            value = jnp.concatenate([value, jnp.zeros((128 - value.shape[0], 1), F32)], axis=0)
        row_cols[...] = jnp.where(lane_c == 6 * layer + chunk, value, row_cols[...])

    def squared(t, b):
        v = fin[t, b].astype(F32) * ROOT_SCALE
        return v * v

    def put_scalar(layer, index, value):
        pay[layer, 18:19, :] = jnp.where(lane == index, value, pay[layer, 18:19, :])

    def row_sums(sq):
        return jnp.sum(sq + FLOOR_SQUARE, axis=1, keepdims=True)

    def column_sums(sq):
        return jnp.sum(sq + FLOOR_SQUARE, axis=0, keepdims=True)

    def statistics(t):
        layer, kind = 1 - t // 3, (2, 1, 0)[t % 3]
        if kind == 2:
            sums_of = jnp.concatenate([row_sums(squared(t, b)) for b in range(4)], axis=0)
            old = jnp.concatenate([row_column(layer, 3 + k) for k in range(3)], axis=0)
            new = DECAY_RATE * old + (1.0 - DECAY_RATE) * (sums_of / 768.0)
            for k in range(3):
                set_row_column(layer, 3 + k, new[128 * k : 128 * k + 128])
            col, quo = jnp.zeros((1, 768), F32), jnp.zeros((1, 768), F32)
            for b in range(4):
                sq = squared(t, b)
                col = col + column_sums(sq)
                quo = quo + jnp.sum(sq / new[96 * b : 96 * b + 96], axis=0, keepdims=True)
            pay[layer, 8:9, :] = col
            pay[layer, 17:18, :] = quo
            put_scalar(layer, 3, jnp.sum(new, axis=0, keepdims=True))
            return
        sets = (((0, 1, 2), 0, 0, 0), ((3,), 1, 3, 1)) if kind == 0 else (((0, 1, 2, 3), 2, 4, 2),)
        for blocks, chunk, first, index in sets:
            sums_of = jnp.zeros((96, 1), F32)
            for b in blocks:
                sums_of = sums_of + row_sums(squared(t, b))
            old = row_column(layer, chunk)[0:96]
            new = DECAY_RATE * old + (1.0 - DECAY_RATE) * (sums_of / (768.0 * len(blocks)))
            set_row_column(layer, chunk, new)
            for k, b in enumerate(blocks):
                sq = squared(t, b)
                pay[layer, first + k : first + k + 1, :] = column_sums(sq)
                pay[layer, 9 + first + k : 10 + first + k, :] = jnp.sum(sq / new, axis=0, keepdims=True)
            put_scalar(layer, index, jnp.sum(new, axis=0, keepdims=True))

    def vec_moments(layer):
        grad = vec_grad[layer]
        return DECAY_RATE * vec_old[layer] + (1.0 - DECAY_RATE) * (grad * grad + FLOOR_SQUARE)

    def exchange_statistics():
        for layer in range(2):
            for m in range(4):
                put_scalar(layer, 4 + m, all_sum(squares[4 * layer + m : 4 * layer + m + 1, :]))
            grad, now = vec_grad[layer], vec_now[layer]
            step = grad * grad / vec_moments(layer)
            for r in range(9):
                rows = slice(r, r + 1) if r < 8 else slice(8, 11)
                put_scalar(layer, 8 + r, all_sum(now[rows] * now[rows]))
                put_scalar(layer, 17 + r, all_sum(step[rows]))

        def copy(src, dst, k, peer):
            return pltpu.make_async_remote_copy(
                src_ref=src, dst_ref=dst, send_sem=pay_sems.at[2 * k], recv_sem=pay_sems.at[2 * k + 1],
                device_id=peer, device_id_type=MESH,
            )

        cp = copy(pay, pay_in, 0, red.sibling)
        cp.start()
        cp.wait()
        pay_z[3] = pay[c] + pay_in[c]
        copies = [copy(pay_z.at[3], pay_z.at[k], 1 + k, peer) for k, peer in enumerate(red.planes)]
        for cp in copies:
            cp.start()
        for cp in copies:
            cp.wait()
        pay_sum[c] = plane_sum(pay_z[3], [pay_z[0], pay_z[1], pay_z[2]])
        cp = copy(pay_sum.at[c], pay_sum.at[c], 4, red.sibling)
        cp.start()
        cp.wait()

    def finish_statistics():
        rows_new[...] = row_cols[...].T[0:16]
        for layer in range(2):
            scalars = pay_sum[layer, 18:19, :]
            pick = lambda index: scalars[:, index : index + 1]
            for m, (first, count, rows) in enumerate(((0, 3, 768.0), (3, 1, 768.0), (4, 4, 768.0), (8, 1, 3072.0))):
                new = DECAY_RATE * columns_old[layer, first : first + count, :] + (1.0 - DECAY_RATE) * (
                    pay_sum[layer, first : first + count, :] / rows
                )
                columns_new[layer, first : first + count, :] = new
                mean_rows = pick(m) / rows
                entries = rows * 768.0 * count
                energy = mean_rows * all_sum(pay_sum[layer, 9 + first : 9 + first + count, :] / new)
                clip = jnp.sqrt(energy / entries) / CLIP_LIMIT
                stride = STEP_RATE * jnp.maximum(FLOOR_SCALE, jnp.sqrt(pick(4 + m) / entries))
                column_scale[layer, first : first + count, :] = lax.rsqrt(new) * (
                    jnp.sqrt(mean_rows) * stride / jnp.maximum(clip, 1.0)
                )
            vec_scale[layer] = jnp.zeros((16, 128), F32)
            for r in range(9):
                entries = 768.0 if r < 8 else 3072.0
                clip = jnp.sqrt(pick(17 + r) / entries) / CLIP_LIMIT
                stride = STEP_RATE * jnp.maximum(FLOOR_SCALE, jnp.sqrt(pick(8 + r) / entries))
                value = stride / jnp.maximum(clip, 1.0)
                if r < 8:
                    vec_scale[layer, r : r + 1, :] = jnp.broadcast_to(value, (1, 128))
                else:
                    vec_scale[layer, 8:11, :] = jnp.broadcast_to(value, (3, 128))

    row_cols[...] = jnp.ones((128, 128), F32)
    for layer in range(2):
        for m, ref in enumerate((joint_rows, output_rows, expand_rows)):
            row_cols[6 * layer + m : 6 * layer + m + 1, 0:96] = ref[layer : layer + 1, :]
        for k in range(3):
            row_cols[6 * layer + 3 + k : 6 * layer + 4 + k, :] = shrink_rows[layer : layer + 1, 128 * k : 128 * k + 128]
        at_row = 0
        for ref, count in ((joint_columns, 3), (output_columns, 1), (expand_columns, 4), (shrink_columns, 1)):
            for k in range(count):
                columns_old[layer, at_row : at_row + 1, :] = ref[layer : layer + 1, 768 * k : 768 * k + 768]
                at_row += 1
    row_cols[...] = row_cols[...].T
    pack_vectors(vec_now, gains, biases, hidden, 0.0)
    pack_vectors(vec_old, gain_old, bias_old, hidden_old, 1.0)
    pay[...] = jnp.zeros_like(pay)

    order = backward_plan()
    pos = 0
    done_units = False
    while pos < len(order):
        item = order[pos]
        if item[0] != "run":
            event(*item)
            pos += 1
            continue
        _, layer, name = item
        if not name.startswith("att"):
            unit(layer, name)
            pos += 1
            continue
        hooks, look, p = {}, pos, 0
        while True:
            it = order[look]
            if it[0] == "run":
                if not it[2].startswith("att"):
                    break
                p = int(it[2][3:]) + 1
            else:
                hooks.setdefault(p, []).append(it)
            look += 1
        tail = hooks.pop(6, [])
        need(layer, "dj", "logsum")

        @pl.loop(0, PAIRS)
        def _(p):
            for at_pair, items in hooks.items():
                @pl.when(p == at_pair)
                def _():
                    for it in items:
                        event(*it)
            attend_backward_pair(p, dj, bias, logsum, ctx, hb, dj)

        for it in tail:
            event(*it)
        pos = look

    exchange_statistics()
    finish_statistics()
    for t in range(3, 6):
        red.drain(t)
    for t in range(6):
        red.drain_share(t)


def backward_call(*args):
    sd = jax.ShapeDtypeStruct
    any_spec = pl.BlockSpec(memory_space=pl.ANY)
    vm = pl.BlockSpec(memory_space=pltpu.VMEM)
    V = pltpu.VMEM
    dma = pltpu.SemaphoreType.DMA
    return pl.pallas_call(
        backward_kernel,
        out_shape=[
            sd((6, 4, 96, 768), BF), sd((T, D), BF), sd((16, 128), F32), sd((2, 9, 768), F32), sd((2, 9, 768), F32),
            sd((2, 16, 128), F32), sd((2, 16, 128), F32),
        ],
        in_specs=[vm] * 18 + [any_spec] * 12,
        out_specs=[vm] * 7,
        scratch_shapes=[
            V((3, 2, 2, 4, 2, 96, 768), BF),
            V((4, 2, 2, 96, 768), BF),
            V((4, 2, 48, 768), BF),
            V((4, 2, 48, 768), BF),
            V((4, 48, 768), BF),
            V((4, 48, 768), BF),
            V((6, 3, 96, 768), BF),
            V((2, 4, 768, 768), BF),
            V((4, T, D), BF),
            V((4, T, D), BF),
            V((3, T, D), BF),
            V((T, D), BF),
            V((T, D), BF),
            V((T, D), BF),
            V((T, 128), F32),
            V((T, 128), F32),
            V((6, 2, T), F32),
            V((T, D), BF),
            V((T, D), BF),
            V((D, T), BF),
            V((T, D), BF),
            V((T, T), F32),
            V((T, D), F32),
            V((2, 16, 768), F32),
            V((6, 2, 16, 768), F32),
            V((3, 2, 16, 768), F32),
            V((128, 128), F32),
            V((2, 24, 768), F32),
            V((2, 24, 768), F32),
            V((4, 24, 768), F32),
            V((2, 24, 768), F32),
            V((2, 9, 768), F32),
            V((2, 16, 128), F32),
            V((2, 16, 128), F32),
            dma((24, 10)),
            dma((6, 10)),
            pltpu.SemaphoreType.REGULAR((5, 4)),
            dma((12,)),
            dma((12,)),
            dma((10,)),
        ],
        compiler_params=pltpu.CompilerParams(
            collective_id=1, has_side_effects=True, vmem_limit_bytes=63 << 20
        ),
        name="backward",
    )(*args)


def update_kernel(
    fin, rows_new, columns_new, column_scale, vec_grad, vec_scale, gains, biases, hidden, gain_old, bias_old, hidden_old, final, grad_in, joint_w, output_w, expand_w, shrink_w,
    *refs,
):
    outs, scratch = refs[:31], refs[31:]
    activations, input_gradient = outs[0], outs[1]
    grads, small_grads = outs[2:6], outs[6:9]
    nexts, small_nexts = outs[9:13], outs[13:16]
    copies = outs[16:20]
    row_outs, column_outs = outs[20:28:2], outs[21:28:2]
    small_moments = outs[28:31]
    masters = (joint_w, output_w, expand_w, shrink_w)
    wbuf, gbuf, nbuf, cbuf, pbuf, fbuf, vec_now, vec_old, in_sems, out_sems, pass_sems = scratch
    inward = [
        pltpu.make_async_copy(final, pbuf.at[0], pass_sems.at[0]),
        pltpu.make_async_copy(grad_in, pbuf.at[1], pass_sems.at[1]),
    ]
    through = [
        pltpu.make_async_copy(pbuf.at[0], activations, pass_sems.at[2]),
        pltpu.make_async_copy(pbuf.at[1], input_gradient, pass_sems.at[3]),
    ]
    pieces = []
    for layer in range(2):
        for m, count in enumerate((3, 1, 4, 4)):
            for b in range(count):
                kind = (0, 0, 1, 2)[m]
                t = 3 * (1 - layer) + (2, 1, 0)[kind]
                pieces.append((layer, m, b, t, 3 if m == 1 else b))

    def part(ref, layer, m, b):
        if m == 1:
            return ref.at[layer]
        if m == 3:
            return ref.at[layer, pl.ds(96 * b, 96), :]
        return ref.at[layer, :, pl.ds(768 * b, 768)]

    loads = [
        pltpu.make_async_copy(part(masters[m], layer, m, b), wbuf.at[n], in_sems.at[n])
        for n, (layer, m, b, t, block) in enumerate(pieces)
    ]
    blocks = [
        pltpu.make_async_copy(fin.at[t, block], fbuf.at[n], in_sems.at[24 + n])
        for n, (layer, m, b, t, block) in enumerate(pieces)
    ]
    for one, two in zip(blocks, loads):
        one.start()
        two.start()
    for cp in inward:
        cp.start()
    pack_vectors(vec_now, gains, biases, hidden, 0.0)
    pack_vectors(vec_old, gain_old, bias_old, hidden_old, 1.0)
    columns = jnp.concatenate([lax.rsqrt(rows_new[...]), jnp.zeros((112, 128), F32)], axis=0).T
    stores = []
    for n, (layer, m, b, t, block) in enumerate(pieces):
        if n == 12:
            for before, cp in zip(inward, through):
                before.wait()
                cp.start()
        if m < 3:
            left = columns[0:96, 6 * layer + m : 6 * layer + m + 1]
        else:
            left = jnp.concatenate([columns[:, 6 * layer + 3 + k : 6 * layer + 4 + k] for k in range(3)], axis=0)
            left = left[96 * b : 96 * b + 96]
        j = (0, 3, 4, 8)[m] + (b if m != 3 else 0)
        blocks[n].wait()
        loads[n].wait()
        grad = fbuf[n].astype(F32) * ROOT_SCALE
        new = wbuf[n] - grad * left * column_scale[layer, j : j + 1, :]
        gbuf[n] = grad
        nbuf[n] = new
        cbuf[n] = new.astype(BF)
        for k, (src, dst) in enumerate(((gbuf, grads[m]), (nbuf, nexts[m]), (cbuf, copies[m]))):
            cp = pltpu.make_async_copy(src.at[n], part(dst, layer, m, b), out_sems.at[n, k])
            cp.start()
            stores.append(cp)
    for layer in range(2):
        grad, now = vec_grad[layer], vec_now[layer]
        moments = DECAY_RATE * vec_old[layer] + (1.0 - DECAY_RATE) * (grad * grad + FLOOR_SQUARE)
        new = now - vec_scale[layer] * (grad * lax.rsqrt(moments))
        for out, value in zip((small_grads, small_nexts, small_moments), (grad, new, moments)):
            out[0][layer] = value[0:2, 0:96]
            for r in range(6):
                out[1][r, layer : layer + 1, :] = value[2 + r : 3 + r, 0:96]
            for k in range(3):
                out[2][layer : layer + 1, 128 * k : 128 * k + 128] = value[8 + k : 9 + k, :]
        for m in range(3):
            row_outs[m][layer : layer + 1, :] = rows_new[6 * layer + m : 6 * layer + m + 1, 0:96]
        for k in range(3):
            row_outs[3][layer : layer + 1, 128 * k : 128 * k + 128] = rows_new[6 * layer + 3 + k : 6 * layer + 4 + k, :]
        for m, (first, count) in enumerate(((0, 3), (3, 1), (4, 4), (8, 1))):
            for k in range(count):
                column_outs[m][layer : layer + 1, 768 * k : 768 * k + 768] = columns_new[layer, first + k : first + k + 1, :]
    for cp in stores + through:
        cp.wait()


def update_call(*args):
    sd = jax.ShapeDtypeStruct
    any_spec = pl.BlockSpec(memory_space=pl.ANY)
    vm = pl.BlockSpec(memory_space=pltpu.VMEM)
    V = pltpu.VMEM
    mats = ((2, 96, 2304), (2, 96, 768), (2, 96, 3072), (2, 384, 768))
    small = ((2, 2, 96), (6, 2, 96), (2, 384))
    stats = ((2, 96), (2, 2304), (2, 96), (2, 768), (2, 96), (2, 3072), (2, 384), (2, 768))
    shapes = (
        [sd((T, D), BF)] * 2 + [sd(s, F32) for s in mats] + [sd(s, F32) for s in small] + [sd(s, F32) for s in mats]
        + [sd(s, F32) for s in small] + [sd(s, BF) for s in mats] + [sd(s, F32) for s in stats] + [sd(s, F32) for s in small]
    )
    specs = [any_spec] * 6 + [vm] * 3 + [any_spec] * 4 + [vm] * 3 + [any_spec] * 4 + [vm] * 11
    return pl.pallas_call(
        update_kernel,
        out_shape=shapes,
        in_specs=[any_spec] + [vm] * 11 + [any_spec] * 6,
        out_specs=specs,
        scratch_shapes=[
            V((24, 96, 768), F32),
            V((24, 96, 768), F32),
            V((24, 96, 768), F32),
            V((24, 96, 768), BF),
            V((2, T, D), BF),
            V((24, 96, 768), BF),
            V((2, 16, 128), F32),
            V((2, 16, 128), F32),
            pltpu.SemaphoreType.DMA((48,)),
            pltpu.SemaphoreType.DMA((24, 3)),
            pltpu.SemaphoreType.DMA((4,)),
        ],
        compiler_params=pltpu.CompilerParams(vmem_limit_bytes=56 << 20),
        name="update",
    )(*args)


def local_kernels(
    tokens,
    segments,
    cotangent,
    joint_weight,
    output_weight,
    expand_weight,
    shrink_weight,
    norm_gains,
    biases,
    hidden_bias,
    joint_rows,
    joint_columns,
    output_rows,
    output_columns,
    expand_rows,
    expand_columns,
    shrink_rows,
    shrink_columns,
    gain_moments,
    bias_moments,
    hidden_moments,
):
    turned = biases.transpose(1, 0, 2)
    turned_old = bias_moments.transpose(1, 0, 2)
    (whole, vec, x_saved, j_s, c_s, l_s, n1_s, r1_s, g_s, gp_s, n2_s, r2_s, final, squares) = forward_call(
        tokens[0], segments, norm_gains, turned, hidden_bias, joint_weight, output_weight, expand_weight, shrink_weight
    )
    vectors = (norm_gains, turned, hidden_bias, gain_moments, turned_old, hidden_moments)
    blocks, grad_in, rows_new, columns_new, column_scale, vec_grad, vec_scale = backward_call(
        cotangent[0], segments, vec, squares, joint_rows, output_rows, expand_rows, shrink_rows,
        joint_columns, output_columns, expand_columns, shrink_columns, *vectors,
        tokens[0], x_saved, whole, j_s, c_s, l_s, n1_s, r1_s, g_s, gp_s, n2_s, r2_s
    )
    outs = list(update_call(
        blocks, rows_new, columns_new, column_scale, vec_grad, vec_scale, *vectors, final, grad_in,
        joint_weight, output_weight, expand_weight, shrink_weight
    ))
    for n in (7, 14, 29):
        outs[n] = outs[n].transpose(1, 0, 2)
    return (outs[0][None], outs[1][None]) + tuple(outs[2:])


def solution(mesh):
    placed = (
        P(("dp", "fsdp"), None, None),
        P(("dp", "fsdp"), None),
        P(("dp", "fsdp"), None, None),
        P(None, "fsdp", None),
        P(None, "fsdp", None),
        P(None, "fsdp", None),
        P(None, "fsdp", None),
        P(None, None, "fsdp"),
        P(None, None, "fsdp"),
        P(None, "fsdp"),
        P(None, "fsdp"),
        P(),
        P(None, "fsdp"),
        P(),
        P(None, "fsdp"),
        P(),
        P(None, "fsdp"),
        P(),
        P(None, None, "fsdp"),
        P(None, None, "fsdp"),
        P(None, "fsdp"),
    )
    known = dict(mesh.shape) == {"dp": 4, "fsdp": 8}
    return jax.shard_map(
        local_kernels if known else local_plain,
        mesh=mesh,
        in_specs=placed,
        out_specs=(
            P(("dp", "fsdp"), None, None),
            P(("dp", "fsdp"), None, None),
            P(None, "fsdp", None),
            P(None, "fsdp", None),
            P(None, "fsdp", None),
            P(None, "fsdp", None),
            P(None, None, "fsdp"),
            P(None, None, "fsdp"),
            P(None, "fsdp"),
            P(None, "fsdp", None),
            P(None, "fsdp", None),
            P(None, "fsdp", None),
            P(None, "fsdp", None),
            P(None, None, "fsdp"),
            P(None, None, "fsdp"),
            P(None, "fsdp"),
            P(None, "fsdp", None),
            P(None, "fsdp", None),
            P(None, "fsdp", None),
            P(None, "fsdp", None),
            P(None, "fsdp"),
            P(),
            P(None, "fsdp"),
            P(),
            P(None, "fsdp"),
            P(),
            P(None, "fsdp"),
            P(),
            P(None, None, "fsdp"),
            P(None, None, "fsdp"),
            P(None, "fsdp"),
        ),
        check_vma=False,
    )
```
